128 devices in a mesh: ctx: 32 (over y, x_hi, z), seq: 4 (over x_lo, core).
Axes of the slice: x: 4 (x_hi: 2, x_lo: 2; x = x_hi * 2 + x_lo), y: 4, z: 4, core: 2. Of those that a mesh axis runs over, the one named last changes fastest.
Arguments:
- tokens: bfloat16 [131072, 1024], P(('ctx', 'seq')), may hold values from -24 to 24
- w_query: bfloat16 [1024, 128], P(('ctx', 'seq')), may hold values from -0.1875 to 0.1875
- w_key: bfloat16 [1024, 128], P(('ctx', 'seq')), may hold values from -0.1875 to 0.1875
- w_value: bfloat16 [1024, 1024], P(('ctx', 'seq')), may hold values from -2 to 2
- w_out: bfloat16 [1024, 1024], P(('ctx', 'seq')), may hold values from -2 to 2
- cotangent: bfloat16 [131072, 1024], P(('ctx', 'seq')), may hold values from -6 to 6
Outputs:
- mixed: bfloat16 [131072, 1024], P(('ctx', 'seq'))
- grad_tokens: bfloat16 [131072, 1024], P(('ctx', 'seq'))
- grad_query: float32 [1024, 128], P(('ctx', 'seq'))
- grad_key: float32 [1024, 128], P(('ctx', 'seq'))
- grad_value: float32 [1024, 1024], P(('ctx', 'seq'))
- grad_out: float32 [1024, 1024], P(('ctx', 'seq'))
The draws below stay inside these ranges and needn't reach their ends.
All inputs are finite; a program needn't handle non-finite values.
Results may differ from the reference program's by a relative error of at most 0.013.
Values may be sent and summed in bfloat16 or wider, within the bound.
No kernel may reach another device: no remote copies, remote signals or barrier semaphores. Data moves between devices by JAX's collectives and lax.ppermute only.
A program may use at most 128 MiB of HBM per device.

```python
import jax
import jax.numpy as jnp
from jax import lax

D = 1024
H = 8
DK = 16
DV = 128
F = 273
TOKENS = 131072


def raised(values, own_key, source, target, parts, factor):
    owner, partner = [(jnp.arange(values.shape[dim]) // (values.shape[dim] // parts)).reshape([-1 if axis == dim else 1 for axis in range(values.ndim)]) for dim in (source, target)]
    chosen = jax.random.permutation(own_key, parts)[partner]
    strong = (owner == chosen) | (owner == (partner + parts // 2) % parts)
    return jnp.where(strong, factor * values, values)


def level_of(stream_key, extent, pieces, least, top_value):
    def one(axis_at, shards_of):
        steps = jax.random.uniform(jax.random.fold_in(jax.random.fold_in(stream_key, 6), axis_at), (shards_of,), jnp.float32, least / len(pieces), top_value / len(pieces))
        return jnp.repeat(jnp.exp(steps), extent[axis_at] // shards_of).reshape((-1,) + (1,) * (len(extent) - axis_at - 1))

    level = one(*pieces[0])
    for cut in pieces[1:]:
        level = level * one(*cut)
    return level


def scatter_about(own_key, extent, width, limit, shards=(), held_as=jnp.bfloat16):
    result = width * jax.random.normal(own_key, extent, jnp.float32)
    if shards:
        result = result * level_of(own_key, extent, shards, -0.22, 0.18)
    return jnp.clip(result, -limit, limit).astype(held_as)


def heavy_noise(stream_key, shape, spread, reach, shards, heavy, held_as=jnp.bfloat16):
    values = spread * jax.random.normal(stream_key, shape, jnp.float32)
    if shards:
        values = values * level_of(stream_key, shape, shards, -0.22, 0.18)
    return jnp.clip(raised(values, jax.random.fold_in(stream_key, 3), *heavy), -reach, reach).astype(held_as)


def setup_inputs(seed: int = 0) -> dict:
    keys = jax.random.split(jax.random.key(seed), 7)
    return {
        "tokens": heavy_noise(keys[0], (TOKENS, D), 1.0, 24.0, ((0, 128),), (0, 1, 128, 5.5)),
        "w_query": scatter_about(keys[1], (D, H * DK), D ** -0.5, 0.1875, ((0, 128),)),
        "w_key": scatter_about(keys[2], (D, H * DK), D ** -0.5, 0.1875, ((0, 128),)),
        "w_value": scatter_about(keys[3], (D, H * DV), (4.0 / D ** 0.5), 2.0, ((0, 128),)),
        "w_out": scatter_about(keys[4], (H * DV, D), (4.0 / (H * DV) ** 0.5), 2.0, ((0, 128),)),
        "cotangent": scatter_about(keys[5], (TOKENS, D), 1.0, 6.0, ((0, 128),)),
    }


def features(projected, head_count):
    tok_rows = projected.shape[0]
    head_dim = projected.shape[1] // head_count
    per_head = jnp.transpose(projected.reshape(tok_rows, head_count, head_dim), (1, 2, 0))
    linear = per_head * head_dim ** (-0.25)
    square = (per_head[:, :, None, :] * per_head[:, None, :, :]).reshape(head_count, head_dim * head_dim, tok_rows)
    square = square * (2.0 * head_dim) ** (-0.5)
    ones_row = jnp.ones((head_count, 1, tok_rows), jnp.float32)
    return jnp.concatenate([ones_row, linear, square], axis=1)

def project_block(tok_block, w_joined, qk_cols):
    mixed_qkv = jnp.dot(tok_block, w_joined, preferred_element_type=jnp.float32).astype(jnp.bfloat16)
    query_bf = mixed_qkv[:, :qk_cols]
    key_bf = mixed_qkv[:, qk_cols:2 * qk_cols]
    value_bf = mixed_qkv[:, 2 * qk_cols:]
    query_feat = features(query_bf.astype(jnp.float32), H).astype(jnp.bfloat16)
    key_feat = features(key_bf.astype(jnp.float32), H).astype(jnp.bfloat16)
    return (query_bf, key_bf, value_bf, query_feat, key_feat)

def attend(query_feat, state_sum, norm_sum):
    high = lax.Precision.HIGH
    query_wide = query_feat.astype(jnp.float32)
    numerator = jnp.einsum('hft,hfe->the', query_wide, state_sum, precision=high)
    denominator = jnp.einsum('hft,hf->th', query_wide, norm_sum, precision=high)
    return (query_wide, numerator / denominator[:, :, None], denominator)

def reference(tokens, w_query, w_key, w_value, w_out, cotangent):
    highest = lax.Precision.HIGHEST
    high = lax.Precision.HIGH
    qk_cols = w_query.shape[1]
    value_cols = w_value.shape[1]
    w_joined = jnp.concatenate([w_query, w_key, w_value], axis=1)
    block_len = min(TOKENS, 4096)
    block_count = TOKENS // block_len
    tok_blocks = tokens.reshape(block_count, block_len, D)
    cot_blocks = cotangent.reshape(block_count, block_len, D)

    def state_step(running, tok_block):
        query_bf, key_bf, value_bf, query_feat, key_feat = project_block(tok_block, w_joined, qk_cols)
        value_heads = value_bf.reshape(block_len, H, DV).astype(jnp.float32)
        key_wide = key_feat.astype(jnp.float32)
        state_add = jnp.einsum('hft,the->hfe', key_wide, value_heads, precision=highest)
        norm_add = lax.optimization_barrier(jnp.sum(key_wide, axis=2))
        return ((running[0] + state_add, running[1] + norm_add), None)
    state_init = (jnp.zeros((H, F, DV), jnp.float32), jnp.zeros((H, F), jnp.float32))
    (state_sum, norm_sum), ignored = lax.scan(state_step, state_init, tok_blocks)

    def grad_step(running, blocks):
        tok_block, cot_block = blocks
        query_bf, key_bf, value_bf, query_feat, key_feat = project_block(tok_block, w_joined, qk_cols)
        query_wide, attended, denominator = attend(query_feat, state_sum, norm_sum)
        attended_bf = attended.reshape(block_len, value_cols).astype(jnp.bfloat16)
        mixed_block = jnp.dot(attended_bf, w_out, preferred_element_type=jnp.float32).astype(jnp.bfloat16)
        upstream = jnp.dot(cot_block, w_out.T, preferred_element_type=jnp.float32).reshape(block_len, H, DV)
        grad_num = upstream / denominator[:, :, None]
        grad_den = -lax.optimization_barrier(jnp.sum(grad_num * attended, axis=2))
        state_add = jnp.einsum('hft,the->hfe', query_wide, grad_num, precision=high)
        norm_add = jnp.einsum('hft,th->hf', query_wide, grad_den, precision=high)
        return ((running[0] + state_add, running[1] + norm_add), mixed_block)
    (state_grad, norm_grad), mixed_blocks = lax.scan(grad_step, state_init, (tok_blocks, cot_blocks))

    def weight_step(running, blocks):
        tok_block, cot_block = blocks
        query_bf, key_bf, value_bf, query_feat, key_feat = project_block(tok_block, w_joined, qk_cols)
        query_wide, attended, denominator = attend(query_feat, state_sum, norm_sum)
        attended_bf = attended.reshape(block_len, value_cols).astype(jnp.bfloat16)
        upstream = jnp.dot(cot_block, w_out.T, preferred_element_type=jnp.float32).reshape(block_len, H, DV)
        grad_num = upstream / denominator[:, :, None]
        grad_den = -lax.optimization_barrier(jnp.sum(grad_num * attended, axis=2))
        query_fgrad = jnp.einsum('the,hfe->hft', grad_num, state_sum, precision=highest)
        query_fgrad = query_fgrad + jnp.einsum('th,hf->hft', grad_den, norm_sum, precision=highest)
        value_heads = value_bf.reshape(block_len, H, DV).astype(jnp.float32)
        key_fgrad = jnp.einsum('the,hfe->hft', value_heads, state_grad, precision=high) + norm_grad[:, :, None]
        key_wide = key_feat.astype(jnp.float32)
        value_grad = jnp.einsum('hft,hfe->the', key_wide, state_grad, precision=high)
        value_grad = value_grad.reshape(block_len, value_cols).astype(jnp.bfloat16)
        ignored_q, query_back = jax.vjp(lambda projected: features(projected, H), query_bf.astype(jnp.float32))
        ignored_k, key_back = jax.vjp(lambda projected: features(projected, H), key_bf.astype(jnp.float32))
        query_grad = query_back(query_fgrad)[0].astype(jnp.bfloat16)
        key_grad = key_back(key_fgrad)[0].astype(jnp.bfloat16)
        joined_grad = jnp.concatenate([query_grad, key_grad, value_grad], axis=1)
        tok_grad = jnp.dot(joined_grad, w_joined.T, preferred_element_type=jnp.float32).astype(jnp.bfloat16)
        joined_add = jnp.dot(tok_block.T, joined_grad, preferred_element_type=jnp.float32)
        out_add = jnp.dot(attended_bf.T, cot_block, preferred_element_type=jnp.float32)
        return ((running[0] + joined_add, running[1] + out_add), tok_grad)
    weight_init = (jnp.zeros((D, w_joined.shape[1]), jnp.float32), jnp.zeros((value_cols, D), jnp.float32))
    (joined_sum, out_sum), tok_grads = lax.scan(weight_step, weight_init, (tok_blocks, cot_blocks))
    scale_factor = TOKENS ** (-0.5)
    joined_sum = joined_sum * scale_factor
    mixed = mixed_blocks.reshape(TOKENS, D)
    grad_tokens = tok_grads.reshape(TOKENS, D)
    grad_query = joined_sum[:, :qk_cols]
    grad_key = joined_sum[:, qk_cols:2 * qk_cols]
    grad_value = joined_sum[:, 2 * qk_cols:]
    grad_out = out_sum * scale_factor
    return (mixed, grad_tokens, grad_query, grad_key, grad_value, grad_out)
```

```python
import jax
import jax.numpy as jnp
from jax import lax
from jax.sharding import PartitionSpec as P

H = 8
DK = 16
DV = 128
BANDS = DK // 2 + 1
FPAD = (BANDS + 2) * DK
AXES = ("ctx", "seq")
BF = jnp.bfloat16
F32 = jnp.float32
SQUARE = (2.0 * DK) ** (-0.5)
LINEAR = DK ** (-0.25)


def dot(a, b, contract):
    return lax.dot_general(a, b, ((contract[:1], contract[1:]), ((), ())), preferred_element_type=F32)


def band_weight():
    row = jnp.arange(FPAD)
    twice = (row >= DK) & (row < (BANDS - 1) * DK)
    return jnp.where(twice, 2.0, 1.0).astype(F32)


def shifted(u, d):
    return jnp.concatenate([u[d:], u[:d]], axis=0) if d else u


def features(u):
    tok = u.shape[1]
    bands = [u * shifted(u, d) * SQUARE for d in range(BANDS)]
    first = lax.broadcasted_iota(jnp.int32, (DK, tok), 0) == 0
    return jnp.concatenate(bands + [u * LINEAR, jnp.where(first, 1.0, 0.0)], axis=0).astype(BF)


def features_back(u, fgrad):
    def band(d):
        return fgrad[d * DK : (d + 1) * DK]

    total = band(0) * u + band(BANDS - 1) * shifted(u, BANDS - 1)
    for d in range(1, BANDS - 1):
        total = total + band(d) * shifted(u, d) + shifted(band(d) * u, DK - d)
    return total * (2.0 * SQUARE) + band(BANDS) * LINEAR


def head_rows(array, head, size):
    return array[head * size : (head + 1) * size]


def keys_phase(tokens, w_qkv, heads):
    qk = heads * DK
    qk_t = dot(w_qkv[:, : 2 * qk], tokens, (0, 1)).astype(BF)
    value = dot(tokens, w_qkv[:, 2 * qk :], (1, 0)).astype(BF)
    states, norms, feats = [], [], []
    for head in range(heads):
        feat = features(head_rows(qk_t[qk:], head, DK).astype(F32))
        states.append(dot(feat, value[:, head * DV : (head + 1) * DV], (1, 0)))
        norms.append(jnp.sum(feat.astype(F32), axis=1))
        feats.append(feat)
    return qk_t, value, jnp.concatenate(feats), jnp.concatenate(states).astype(BF), jnp.concatenate(norms)


def query_phase(qk_t, up_t, norm, heads):
    weight = band_weight()
    sgrads, feats, scales = [], [], []
    for head in range(heads):
        feat = features(head_rows(qk_t, head, DK).astype(F32))
        weighted = weight * head_rows(norm, head, FPAD)
        scale = 1.0 / jnp.sum(feat.astype(F32) * weighted[:, None], axis=0, keepdims=True)
        grad_num = (head_rows(up_t, head, DV) * scale).astype(BF)
        sgrads.append(dot(feat, grad_num, (1, 1)))
        feats.append(feat)
        scales.append(scale)
    return jnp.concatenate(feats), jnp.concatenate(scales), jnp.concatenate(sgrads).astype(BF)


def attend_phase(qk_t, feats, scales, up_t, state, norm, heads):
    weight = band_weight()
    attended, qgrads, ngrads = [], [], []
    for head in range(heads):
        feat = head_rows(feats, head, FPAD)
        scale = scales[head : head + 1]
        head_state = head_rows(state, head, FPAD)
        weighted = (head_state.astype(F32) * weight[:, None]).astype(BF)
        att = dot(weighted, feat, (0, 0)) * scale
        grad_num = head_rows(up_t, head, DV) * scale
        grad_den = -jnp.sum(grad_num * att, axis=0, keepdims=True)
        ngrads.append(jnp.sum(feat.astype(F32) * grad_den, axis=1))
        fgrad = dot(head_state, grad_num.astype(BF), (1, 0))
        fgrad = fgrad + head_rows(norm, head, FPAD)[:, None] * grad_den
        u = head_rows(qk_t, head, DK).astype(F32)
        qgrads.append(features_back(u, fgrad).astype(BF))
        attended.append(att.astype(BF))
    return jnp.concatenate(attended), jnp.concatenate(qgrads), jnp.concatenate(ngrads)


def back_phase(qk_t, value, feats, sgrad, ngrad, heads):
    weight = band_weight()
    kgrads, vgrads = [], []
    for head in range(heads):
        head_sgrad = head_rows(sgrad, head, FPAD)
        fgrad = dot(head_sgrad, value[:, head * DV : (head + 1) * DV], (1, 1))
        fgrad = fgrad + head_rows(ngrad, head, FPAD)[:, None]
        u = head_rows(qk_t[heads * DK :], head, DK).astype(F32)
        kgrads.append(features_back(u, fgrad).astype(BF))
        weighted = (head_sgrad.astype(F32) * weight[:, None]).astype(BF)
        vgrads.append(dot(weighted, head_rows(feats, head, FPAD), (0, 0)).astype(BF))
    return jnp.concatenate(kgrads), jnp.concatenate(vgrads)


def per_device(chips, tokens, w_query, w_key, w_value, w_out, cotangent):
    n = 2 * chips
    heads = H // 2
    core = lax.axis_index("seq") % 2
    same_core = [[2 * p + c for p in range(chips)] for c in range(2)]
    swap = [(i, i ^ 1) for i in range(n)]
    scale_factor = (tokens.shape[0] * n) ** (-0.5)

    def exchange(x):
        return lax.ppermute(x, AXES, swap)

    def spread(x):
        return lax.all_to_all(x, AXES, 0, 0, axis_index_groups=same_core, tiled=True)

    def sum_small(x):
        row = jnp.pad(x, (0, -x.shape[0] % 1024)).reshape(1, -1, 128)
        every = spread(jnp.broadcast_to(row, (chips,) + row.shape[1:]))
        return jnp.sum(every, axis=0).reshape(-1)[: x.shape[0]]

    def sum_state(x):
        rows, cols = x.shape
        part = rows // chips
        own = jnp.sum(spread(x.reshape(chips, part, cols)).astype(F32), axis=0).astype(BF)
        return spread(jnp.broadcast_to(own[None], (chips, part, cols))).reshape(rows, cols)

    halves = [
        jnp.concatenate(
            [
                w_query[:, c * heads * DK : (c + 1) * heads * DK],
                w_key[:, c * heads * DK : (c + 1) * heads * DK],
                w_value[:, c * heads * DV : (c + 1) * heads * DV],
            ],
            axis=1,
        )
        for c in range(2)
    ]
    to_send = jnp.broadcast_to(jnp.stack(halves)[None], (chips, 2) + halves[0].shape)
    w_qkv = lax.all_to_all(to_send.reshape((n,) + halves[0].shape), AXES, 0, 0, tiled=True)
    w_qkv = w_qkv.reshape(-1, halves[0].shape[1])
    out_rows = lax.ppermute(w_out, AXES, [(c * chips + p, 2 * p + c) for p in range(chips) for c in range(2)])
    w_out_half = spread(jnp.broadcast_to(out_rows[None], (chips,) + out_rows.shape)).reshape(-1, out_rows.shape[1])

    tok = jnp.concatenate([tokens, exchange(tokens)])
    cot = jnp.concatenate([cotangent, exchange(cotangent)])
    own = tokens.shape[0]

    qk_t, value, key_feat, state_part, norm_part = keys_phase(tok, w_qkv, heads)
    norm = sum_small(norm_part)
    state = sum_state(state_part)
    up_t = dot(w_out_half, cot, (1, 1))
    query_feat, scales, sgrad_part = query_phase(qk_t, up_t, norm, heads)
    sgrad = sum_state(sgrad_part)
    moments = dot(tok, key_feat, (0, 1))

    attended_t, qgrad_t, ngrad_part = attend_phase(qk_t, query_feat, scales, up_t, state, norm, heads)
    ngrad = sum_small(ngrad_part)
    mixed_part = dot(attended_t, w_out_half, (0, 0)).astype(BF)
    mixed_other = exchange(mixed_part[own:])
    mixed = (mixed_part[:own].astype(F32) + mixed_other.astype(F32)).astype(BF)

    early = jnp.concatenate([moments, dot(tok, qgrad_t, (0, 1))], axis=1).astype(BF)
    early = jnp.sum(spread(early.reshape(chips, -1, early.shape[1])).astype(F32), axis=0)
    out_part = dot(attended_t, cot, (1, 0)).astype(BF)
    out_sum = jnp.sum(spread(out_part.reshape(chips, -1, out_part.shape[1])).astype(F32), axis=0)
    grad_out = lax.ppermute(out_sum, AXES, [(2 * p + c, c * chips + p) for p in range(chips) for c in range(2)])

    kgrad_t, vgrad_t = back_phase(qk_t, value, key_feat, sgrad, ngrad, heads)
    kgrad_part = dot(tok, kgrad_t, (0, 1)).astype(BF)
    kgrad_all = lax.all_to_all(kgrad_part.reshape(n, -1, kgrad_part.shape[1]), AXES, 0, 0, tiled=True)
    kgrad_sum = jnp.sum(kgrad_all.reshape((chips, 2) + kgrad_all.shape[1:]).astype(F32), axis=0)
    joined_t = jnp.concatenate([qgrad_t, kgrad_t, vgrad_t])
    gtok_part = dot(joined_t, w_qkv, (0, 1)).astype(BF)
    gtok_other = exchange(gtok_part[own:])
    grad_tokens = (gtok_part[:own].astype(F32) + gtok_other.astype(F32)).astype(BF)

    weight = band_weight()
    gvalue = jnp.concatenate(
        [
            jnp.dot(
                early[:, h * FPAD : (h + 1) * FPAD] * weight,
                head_rows(sgrad, h, FPAD).astype(F32),
                precision=lax.Precision.HIGH,
            )
            for h in range(heads)
        ],
        axis=1,
    )
    mine = jnp.concatenate([early[:, heads * FPAD :], gvalue], axis=1)
    rows = mine.shape[0] // 2
    got = exchange(lax.dynamic_slice_in_dim(mine, (1 - core) * rows, rows, 0))
    kept = lax.dynamic_slice_in_dim(mine, core * rows, rows, 0)
    low, high = jnp.where(core == 0, kept, got), jnp.where(core == 0, got, kept)
    qk = heads * DK
    grad_query = jnp.concatenate([low[:, :qk], high[:, :qk]], axis=1) * scale_factor
    grad_value = jnp.concatenate([low[:, qk:], high[:, qk:]], axis=1) * scale_factor
    grad_key = jnp.concatenate([kgrad_sum[0], kgrad_sum[1]], axis=1) * scale_factor
    return (mixed, grad_tokens, grad_query, grad_key, grad_value, grad_out * scale_factor)


def solution(mesh):
    chips = mesh.size // 2
    placed = P(AXES, None)
    return jax.shard_map(
        lambda *args: per_device(chips, *args),
        mesh=mesh,
        in_specs=(placed,) * 6,
        out_specs=(placed,) * 6,
        check_vma=False,
    )
```

```python
import jax
import jax.numpy as jnp
from jax import lax
from jax.experimental import pallas as pl
from jax.experimental.pallas import tpu as pltpu
from jax.sharding import PartitionSpec as P

H = 8
DK = 16
DV = 128
BANDS = DK // 2 + 1
FPAD = (BANDS + 2) * DK
SPAD = 256
AXES = ("ctx", "seq")
BF = jnp.bfloat16
F32 = jnp.float32
SQUARE = (2.0 * DK) ** (-0.5)
LINEAR = DK ** (-0.25)


def dot(a, b, contract):
    return lax.dot_general(a, b, ((contract[:1], contract[1:]), ((), ())), preferred_element_type=F32)


def band_weight(shape, dim):
    row = lax.broadcasted_iota(jnp.int32, shape, dim)
    twice = (row >= DK) & (row < (BANDS - 1) * DK)
    return jnp.where(twice, 2.0, 1.0).astype(F32)


def shifted(u, d):
    return pltpu.roll(u, DK - d, 0) if d else u


def features(u):
    bands = [u * shifted(u, d) * SQUARE for d in range(BANDS)]
    first = lax.broadcasted_iota(jnp.int32, u.shape, 0) == 0
    return jnp.concatenate(bands + [u * LINEAR, jnp.where(first, 1.0, 0.0)], axis=0).astype(BF)


def features_back(u, fgrad):
    def band(d):
        return fgrad[d * DK : (d + 1) * DK]

    total = band(0) * u + band(BANDS - 1) * shifted(u, BANDS - 1)
    for d in range(1, BANDS - 1):
        total = total + band(d) * shifted(u, d) + shifted(band(d) * u, DK - d)
    return total * (2.0 * SQUARE) + band(BANDS) * LINEAR


def in_parts(row):
    high = row.astype(BF).astype(F32)
    rest = row - high
    mid = rest.astype(BF).astype(F32)
    at = lax.broadcasted_iota(jnp.int32, (16, row.shape[1]), 0)
    low = jnp.where(at == 2, rest - mid, 0.0)
    return jnp.where(at == 0, high, jnp.where(at == 1, mid, low)).astype(BF)


def rows_of(array, head, size):
    return array[head * size : (head + 1) * size]


def column(rows, head):
    return rows.T[:FPAD, head : head + 1]


def call(body, tok_count, ins, in_kinds, outs, out_kinds, scratch, flops):
    block = min(512, tok_count)

    def spec(shape, kind):
        if kind is None:
            return pl.BlockSpec(shape, lambda i: (0,) * len(shape))
        if kind == 0:
            return pl.BlockSpec((block, shape[1]), lambda i: (i, 0))
        return pl.BlockSpec((shape[0], block), lambda i: (0, i))

    nbytes = sum(x.size * x.dtype.itemsize for x in list(ins) + list(outs))
    return pl.pallas_call(
        body,
        grid=(tok_count // block,),
        in_specs=[spec(x.shape, k) for x, k in zip(ins, in_kinds)],
        out_specs=[spec(x.shape, k) for x, k in zip(outs, out_kinds)],
        out_shape=outs,
        scratch_shapes=scratch,
        compiler_params=pltpu.CompilerParams(
            dimension_semantics=("arbitrary",), vmem_limit_bytes=48 * 2**20
        ),
        cost_estimate=pl.CostEstimate(flops=flops, bytes_accessed=nbytes, transcendentals=0),
    )(*ins)


def shape(dims, dtype):
    return jax.ShapeDtypeStruct(dims, dtype)


def clear_at_first(*refs):
    @pl.when(pl.program_id(0) == 0)
    def _():
        for ref in refs:
            ref[...] = jnp.zeros(ref.shape, ref.dtype)


def at_last(fn):
    pl.when(pl.program_id(0) == pl.num_programs(0) - 1)(fn)


def keys_phase(tokens, w_qkv, heads):
    qk = heads * DK

    def body(tok_ref, w_ref, qk_ref, value_ref, feat_ref, state_ref, norm_ref, state_acc, norm_acc):
        clear_at_first(state_acc, norm_acc)
        joined = dot(tok_ref[...], w_ref[...], (1, 0))
        qk_t = joined[:, : 2 * qk].T.astype(BF)
        value = joined[:, 2 * qk :].astype(BF)
        qk_ref[...] = qk_t
        value_ref[...] = value
        keys = qk_t.astype(F32)[qk:]
        ones = jnp.ones((16, value.shape[0]), BF)
        for head in range(heads):
            feat = features(rows_of(keys, head, DK))
            feat_ref[head * FPAD : (head + 1) * FPAD, :] = feat
            state_acc[head, :FPAD, :] += dot(feat, value[:, head * DV : (head + 1) * DV], (1, 0))
            norm_acc[head, :, :FPAD] += dot(ones, feat, (1, 1))

        @at_last
        def _():
            norm_ref[...] = jnp.zeros(norm_ref.shape, F32)
            for head in range(heads):
                state_ref[head * SPAD : (head + 1) * SPAD, :] = state_acc[head].astype(BF)
                norm_ref[head : head + 1, :] = norm_acc[head, :1, :]

    count = tokens.shape[0]
    return call(
        body,
        count,
        (tokens, w_qkv),
        (0, None),
        (
            shape((2 * qk, count), BF),
            shape((count, heads * DV), BF),
            shape((heads * FPAD, count), BF),
            shape((heads * SPAD, DV), BF),
            shape((8, SPAD), F32),
        ),
        (1, 0, 1, None, None),
        [pltpu.VMEM((heads, SPAD, DV), F32), pltpu.VMEM((heads, 16, SPAD), F32)],
        2 * count * (tokens.shape[1] * w_qkv.shape[1] + heads * FPAD * DV * 2),
    )


def upstream_phase(qk_t, cot, w_out_half, heads):
    count = cot.shape[0]

    def body(qk_ref, cot_ref, w_ref, up_ref, feat_ref):
        up_ref[...] = dot(w_ref[...], cot_ref[...], (1, 1))
        query = qk_ref[...].astype(F32)
        for head in range(heads):
            feat_ref[head * FPAD : (head + 1) * FPAD, :] = features(rows_of(query, head, DK))

    return call(
        body,
        count,
        (qk_t, cot, w_out_half),
        (1, 0, None),
        (shape((heads * DV, count), F32), shape((heads * FPAD, count), BF)),
        (1, 1),
        [],
        2 * count * cot.shape[1] * heads * DV,
    )


def query_phase(feats, up_t, norm, heads):
    count = up_t.shape[1]

    def body(feat_ref, up_ref, norm_ref, scale_ref, sgrad_ref, acc):
        clear_at_first(acc)
        weighted = norm_ref[...] * band_weight((8, SPAD), 1)
        at = lax.broadcasted_iota(jnp.int32, scale_ref.shape, 0)
        scales = jnp.zeros(scale_ref.shape, F32)
        for head in range(heads):
            feat = feat_ref[head * FPAD : (head + 1) * FPAD, :]
            parts = in_parts(weighted[head : head + 1, :])[:, :FPAD]
            scale = 1.0 / jnp.sum(dot(parts, feat, (1, 0)), axis=0, keepdims=True)
            grad_num = (up_ref[head * DV : (head + 1) * DV, :] * scale).astype(BF)
            acc[head, :FPAD, :] += dot(feat, grad_num, (1, 1))
            scales = jnp.where(at == head, scale, scales)
        scale_ref[...] = scales

        @at_last
        def _():
            for head in range(heads):
                sgrad_ref[head * SPAD : (head + 1) * SPAD, :] = acc[head].astype(BF)

    return call(
        body,
        count,
        (feats, up_t, norm),
        (1, 1, None),
        (shape((8, count), F32), shape((heads * SPAD, DV), BF)),
        (1, None),
        [pltpu.VMEM((heads, SPAD, DV), F32)],
        2 * count * heads * FPAD * DV * 2,
    )


def attend_phase(qk_t, feats, scales, up_t, state, norm, heads):
    count = up_t.shape[1]

    def body(qk_ref, feat_ref, scale_ref, up_ref, state_ref, norm_ref, att_ref, qgrad_ref, ngrad_ref, turned, acc):
        clear_at_first(acc)

        @pl.when(pl.program_id(0) == 0)
        def _():
            for head in range(heads):
                whole = state_ref[head * SPAD : (head + 1) * SPAD, :].astype(F32)
                turned[head] = (whole * band_weight((SPAD, DV), 0)).T.astype(BF)

        query = qk_ref[...].astype(F32)
        norms = norm_ref[...]
        for head in range(heads):
            feat = feat_ref[head * FPAD : (head + 1) * FPAD, :]
            scale = scale_ref[head : head + 1, :]
            att = dot(turned[head, :, :FPAD], feat, (1, 0)) * scale
            grad_num = up_ref[head * DV : (head + 1) * DV, :] * scale
            grad_den = -jnp.sum(grad_num * att, axis=0, keepdims=True)
            acc[head, :, :FPAD] += dot(in_parts(grad_den), feat, (1, 1))
            fgrad = dot(state_ref[head * SPAD : head * SPAD + FPAD, :], grad_num.astype(BF), (1, 0))
            fgrad = fgrad + column(norms, head) * grad_den
            qgrad_ref[head * DK : (head + 1) * DK, :] = features_back(rows_of(query, head, DK), fgrad).astype(BF)
            att_ref[head * DV : (head + 1) * DV, :] = att.astype(BF)

        @at_last
        def _():
            ngrad_ref[...] = jnp.zeros(ngrad_ref.shape, F32)
            for head in range(heads):
                ngrad_ref[head : head + 1, :] = jnp.sum(acc[head], axis=0, keepdims=True)

    return call(
        body,
        count,
        (qk_t, feats, scales, up_t, state, norm),
        (1, 1, 1, 1, None, None),
        (shape((heads * DV, count), BF), shape((heads * DK, count), BF), shape((8, SPAD), F32)),
        (1, 1, None),
        [pltpu.VMEM((heads, DV, SPAD), BF), pltpu.VMEM((heads, 16, SPAD), F32)],
        2 * count * heads * FPAD * DV * 4,
    )


def back_phase(qk_t, value, feats, sgrad, heads):
    count = value.shape[0]
    qk = heads * DK

    def body(qk_ref, value_ref, feat_ref, sgrad_ref, kgrad_ref, vgrad_ref, turned):
        @pl.when(pl.program_id(0) == 0)
        def _():
            for head in range(heads):
                whole = sgrad_ref[head * SPAD : (head + 1) * SPAD, :].astype(F32)
                turned[head] = (whole * band_weight((SPAD, DV), 0)).T.astype(BF)

        keys = qk_ref[...].astype(F32)[qk:]
        for head in range(heads):
            fgrad = dot(
                sgrad_ref[head * SPAD : head * SPAD + FPAD, :],
                value_ref[:, head * DV : (head + 1) * DV],
                (1, 1),
            )
            kgrad_ref[head * DK : (head + 1) * DK, :] = features_back(rows_of(keys, head, DK), fgrad)
            feat = feat_ref[head * FPAD : (head + 1) * FPAD, :]
            vgrad_ref[head * DV : (head + 1) * DV, :] = dot(turned[head, :, :FPAD], feat, (1, 0)).astype(BF)

    return call(
        body,
        count,
        (qk_t, value, feats, sgrad),
        (1, 0, 1, None),
        (shape((qk, count), F32), shape((heads * DV, count), BF)),
        (1, 1),
        [pltpu.VMEM((heads, DV, SPAD), BF)],
        2 * count * heads * FPAD * DV * 3,
    )


def key_phase(qk_t, partial, ngrad, tokens, heads):
    count, width = tokens.shape
    qk = heads * DK

    def body(qk_ref, partial_ref, ngrad_ref, tok_ref, kgrad_ref, wgrad_ref, acc):
        clear_at_first(acc)
        keys = qk_ref[...].astype(F32)[qk:]
        rows = ngrad_ref[...]
        whole = []
        for head in range(heads):
            key = rows_of(keys, head, DK)
            fgrad = jnp.broadcast_to(column(rows, head), (FPAD, key.shape[1]))
            whole.append(rows_of(partial_ref[...], head, DK) + features_back(key, fgrad))
        kgrad = jnp.concatenate(whole, axis=0).astype(BF)
        kgrad_ref[...] = kgrad
        acc[...] += dot(kgrad, tok_ref[...], (1, 0))

        @at_last
        def _():
            wgrad_ref[...] = acc[...].T.astype(BF)

    return call(
        body,
        count,
        (qk_t, partial, ngrad, tokens),
        (1, 1, None, 0),
        (shape((qk, count), BF), shape((width, qk), BF)),
        (1, None),
        [pltpu.VMEM((qk, width), F32)],
        2 * count * width * qk,
    )


def per_device(chips, tokens, w_query, w_key, w_value, w_out, cotangent):
    n = 2 * chips
    heads = H // 2
    core = lax.axis_index("seq") % 2
    same_core = [[2 * p + c for p in range(chips)] for c in range(2)]
    swap = [(i, i ^ 1) for i in range(n)]
    scale_factor = (tokens.shape[0] * n) ** (-0.5)

    def exchange(x):
        return lax.ppermute(x, AXES, swap)

    def spread(x):
        return lax.all_to_all(x, AXES, 0, 0, axis_index_groups=same_core, tiled=True)

    def sum_small(x):
        return jnp.sum(spread(jnp.broadcast_to(x[None], (chips,) + x.shape)), axis=0)

    def sum_state(x):
        rows, cols = x.shape
        part = rows // chips
        own = jnp.sum(spread(x.reshape(chips, part, cols)).astype(F32), axis=0).astype(BF)
        return spread(jnp.broadcast_to(own[None], (chips, part, cols))).reshape(rows, cols)

    halves = [
        jnp.concatenate(
            [
                w_query[:, c * heads * DK : (c + 1) * heads * DK],
                w_key[:, c * heads * DK : (c + 1) * heads * DK],
                w_value[:, c * heads * DV : (c + 1) * heads * DV],
            ],
            axis=1,
        )
        for c in range(2)
    ]
    to_send = jnp.broadcast_to(jnp.stack(halves)[None], (chips, 2) + halves[0].shape)
    w_qkv = lax.all_to_all(to_send.reshape((n,) + halves[0].shape), AXES, 0, 0, tiled=True)
    w_qkv = w_qkv.reshape(-1, halves[0].shape[1])
    out_rows = lax.ppermute(w_out, AXES, [(c * chips + p, 2 * p + c) for p in range(chips) for c in range(2)])
    w_out_half = spread(jnp.broadcast_to(out_rows[None], (chips,) + out_rows.shape)).reshape(-1, out_rows.shape[1])

    tok = jnp.concatenate([tokens, exchange(tokens)])
    cot = jnp.concatenate([cotangent, exchange(cotangent)])
    own = tokens.shape[0]

    qk_t, value, key_feat, state_part, norm_part = keys_phase(tok, w_qkv, heads)
    norm = sum_small(norm_part)
    state = sum_state(state_part)
    up_t, query_feat = upstream_phase(qk_t, cot, w_out_half, heads)
    scales, sgrad_part = query_phase(query_feat, up_t, norm, heads)
    sgrad = sum_state(sgrad_part)
    moments = dot(tok, key_feat, (0, 1))

    attended_t, qgrad_t, ngrad_part = attend_phase(qk_t, query_feat, scales, up_t, state, norm, heads)
    ngrad = sum_small(ngrad_part)
    mixed_part = dot(attended_t, w_out_half, (0, 0)).astype(BF)
    mixed_other = exchange(mixed_part[own:])
    mixed = (mixed_part[:own].astype(F32) + mixed_other.astype(F32)).astype(BF)

    early = jnp.concatenate([moments, dot(tok, qgrad_t, (0, 1))], axis=1).astype(BF)
    early = jnp.sum(spread(early.reshape(chips, -1, early.shape[1])).astype(F32), axis=0)
    out_part = dot(attended_t, cot, (1, 0)).astype(BF)
    out_sum = jnp.sum(spread(out_part.reshape(chips, -1, out_part.shape[1])).astype(F32), axis=0)
    grad_out = lax.ppermute(out_sum, AXES, [(2 * p + c, c * chips + p) for p in range(chips) for c in range(2)])

    kgrad_rest, vgrad_t = back_phase(qk_t, value, key_feat, sgrad, heads)
    kgrad_t, kgrad_part = key_phase(qk_t, kgrad_rest, ngrad, tok, heads)
    kgrad_all = lax.all_to_all(kgrad_part.reshape(n, -1, kgrad_part.shape[1]), AXES, 0, 0, tiled=True)
    kgrad_sum = jnp.sum(kgrad_all.reshape((chips, 2) + kgrad_all.shape[1:]).astype(F32), axis=0)
    joined_t = jnp.concatenate([qgrad_t, kgrad_t, vgrad_t])
    gtok_part = dot(joined_t, w_qkv, (0, 1)).astype(BF)
    gtok_other = exchange(gtok_part[own:])
    grad_tokens = (gtok_part[:own].astype(F32) + gtok_other.astype(F32)).astype(BF)

    weight = band_weight((1, FPAD), 1)
    gvalue = jnp.concatenate(
        [
            jnp.dot(
                early[:, h * FPAD : (h + 1) * FPAD] * weight,
                sgrad[h * SPAD : h * SPAD + FPAD].astype(F32),
                precision=lax.Precision.HIGH,
            )
            for h in range(heads)
        ],
        axis=1,
    )
    mine = jnp.concatenate([early[:, heads * FPAD :], gvalue], axis=1)
    rows = mine.shape[0] // 2
    got = exchange(lax.dynamic_slice_in_dim(mine, (1 - core) * rows, rows, 0))
    kept = lax.dynamic_slice_in_dim(mine, core * rows, rows, 0)
    low, high = jnp.where(core == 0, kept, got), jnp.where(core == 0, got, kept)
    qk = heads * DK
    grad_query = jnp.concatenate([low[:, :qk], high[:, :qk]], axis=1) * scale_factor
    grad_value = jnp.concatenate([low[:, qk:], high[:, qk:]], axis=1) * scale_factor
    grad_key = jnp.concatenate([kgrad_sum[0], kgrad_sum[1]], axis=1) * scale_factor
    return (mixed, grad_tokens, grad_query, grad_key, grad_value, grad_out * scale_factor)


def solution(mesh):
    chips = mesh.size // 2
    placed = P(AXES, None)
    return jax.shard_map(
        lambda *args: per_device(chips, *args),
        mesh=mesh,
        in_specs=(placed,) * 6,
        out_specs=(placed,) * 6,
        check_vma=False,
    )
```

```python
import jax
import jax.numpy as jnp
from jax import lax
from jax.experimental import pallas as pl
from jax.experimental.pallas import tpu as pltpu
from jax.sharding import PartitionSpec as P

H = 8
DK = 16
DV = 128
BANDS = DK // 2 + 1
FPAD = (BANDS + 2) * DK
SPAD = 256
AXES = ("ctx", "seq")
BF = jnp.bfloat16
F32 = jnp.float32
SQUARE = (2.0 * DK) ** (-0.5)
LINEAR = DK ** (-0.25)


def dot(a, b, contract):
    return lax.dot_general(a, b, ((contract[:1], contract[1:]), ((), ())), preferred_element_type=F32)


def band_weight(shape, dim):
    row = lax.broadcasted_iota(jnp.int32, shape, dim)
    twice = (row >= DK) & (row < (BANDS - 1) * DK)
    return jnp.where(twice, 2.0, 1.0).astype(F32)


def shifted(u, d):
    return pltpu.roll(u, DK - d, 0) if d else u


def features(u):
    bands = [u * shifted(u, d) * SQUARE for d in range(BANDS)]
    first = lax.broadcasted_iota(jnp.int32, u.shape, 0) == 0
    return jnp.concatenate(bands + [u * LINEAR, jnp.where(first, 1.0, 0.0)], axis=0).astype(BF)


def features_back(u, fgrad):
    def band(d):
        return fgrad[d * DK : (d + 1) * DK]

    total = band(0) * u + band(BANDS - 1) * shifted(u, BANDS - 1)
    for d in range(1, BANDS - 1):
        total = total + band(d) * shifted(u, d) + shifted(band(d) * u, DK - d)
    return total * (2.0 * SQUARE) + band(BANDS) * LINEAR


def in_parts(row):
    high = row.astype(BF).astype(F32)
    rest = row - high
    mid = rest.astype(BF).astype(F32)
    at = lax.broadcasted_iota(jnp.int32, (16, row.shape[1]), 0)
    low = jnp.where(at == 2, rest - mid, 0.0)
    return jnp.where(at == 0, high, jnp.where(at == 1, mid, low)).astype(BF)


def rows_of(array, head, size):
    return array[head * size : (head + 1) * size]


def head_row(rows, head):
    first, second = rows[4 * head : 4 * head + 2, :], rows[4 * head + 2 : 4 * head + 4, :]
    both = first + second
    return jnp.concatenate([both[:1], both[1:]], axis=1)


def split_rows(per_head):
    found = []
    for row in per_head:
        high = row.astype(BF).astype(F32)
        for part in (high, row - high):
            found += [part[:, :128], part[:, 128:]]
    found += [jnp.zeros((1, 128), F32)] * (16 - len(found))
    return jnp.concatenate(found, axis=0).astype(BF)


def column(row):
    return jnp.broadcast_to(row, (8, row.shape[1])).T[:FPAD, :1]


def weighted_turned(state_ref, head):
    whole = state_ref[head * SPAD : (head + 1) * SPAD, :].astype(F32)
    return (whole * band_weight((SPAD, DV), 0)).T.astype(BF)


def call(body, count, ins, kinds, outs, out_kinds, scratch, flops, skip=0):
    block = min(512, count, *[x[0].shape[0] for x, k in zip(ins, kinds) if k == "pair"])
    steps, first = count // block, skip // block
    in_specs, args = [], []
    for x, kind in zip(ins, kinds):
        if kind is None:
            in_specs.append(pl.BlockSpec(x.shape, lambda i: (0, 0)))
        elif kind == 0:
            in_specs.append(pl.BlockSpec((block, x.shape[1]), lambda i: (i + first, 0)))
        elif kind == 1:
            in_specs.append(pl.BlockSpec((x.shape[0], block), lambda i: (0, i + first)))
        elif kind == "here":
            in_specs.append(pl.BlockSpec((block, x.shape[1]), lambda i: (i, 0)))
        else:
            half = steps // 2
            in_specs.append(pl.BlockSpec((block, x[0].shape[1]), lambda i: (jnp.minimum(i, half - 1), 0)))
            in_specs.append(pl.BlockSpec((block, x[0].shape[1]), lambda i: (jnp.maximum(i - half, 0), 0)))
        args += list(x) if kind == "pair" else [x]
    out_specs = []
    for x, kind in zip(outs, out_kinds):
        if kind is None:
            out_specs.append(pl.BlockSpec(x.shape, lambda i: (0, 0)))
        elif kind == 0:
            out_specs.append(pl.BlockSpec((block, x.shape[1]), lambda i: (i, 0)))
        else:
            out_specs.append(pl.BlockSpec((x.shape[0], block), lambda i: (0, i)))
    nbytes = sum(x.size * x.dtype.itemsize for x in args + list(outs))
    return pl.pallas_call(
        body,
        grid=(steps,),
        in_specs=in_specs,
        out_specs=out_specs,
        out_shape=outs,
        scratch_shapes=scratch,
        compiler_params=pltpu.CompilerParams(dimension_semantics=("arbitrary",), vmem_limit_bytes=48 * 2**20),
        cost_estimate=pl.CostEstimate(flops=flops, bytes_accessed=nbytes, transcendentals=0),
    )(*args)


def either(first_ref, second_ref):
    return jnp.where(pl.program_id(0) < pl.num_programs(0) // 2, first_ref[...], second_ref[...])


def shape(dims, dtype):
    return jax.ShapeDtypeStruct(dims, dtype)


def clear_at_first(*refs):
    @pl.when(pl.program_id(0) == 0)
    def _():
        for ref in refs:
            ref[...] = jnp.zeros(ref.shape, ref.dtype)


def at_first(fn):
    pl.when(pl.program_id(0) == 0)(fn)


def at_last(fn):
    pl.when(pl.program_id(0) == pl.num_programs(0) - 1)(fn)


def keys_phase(tokens, w_qkv, heads):
    qk = heads * DK

    def body(own_ref, other_ref, w_ref, qk_ref, value_ref, feat_ref, state_ref, norm_ref, state_acc, norm_acc):
        clear_at_first(state_acc, norm_acc)
        joined = dot(either(own_ref, other_ref), w_ref[...], (1, 0))
        qk_t = joined[:, : 2 * qk].T.astype(BF)
        value = joined[:, 2 * qk :].astype(BF)
        qk_ref[...] = qk_t
        value_ref[...] = value
        keys = qk_t.astype(F32)[qk:]
        ones = jnp.ones((16, value.shape[0]), BF)
        for head in range(heads):
            feat = features(rows_of(keys, head, DK))
            feat_ref[head * FPAD : (head + 1) * FPAD, :] = feat
            state_acc[head, :FPAD, :] += dot(feat, value[:, head * DV : (head + 1) * DV], (1, 0))
            norm_acc[head, :, :FPAD] += dot(ones, feat, (1, 1))

        @at_last
        def _():
            for head in range(heads):
                state_ref[head * SPAD : (head + 1) * SPAD, :] = state_acc[head].astype(BF)
            norm_ref[...] = split_rows([norm_acc[head][:1] for head in range(heads)])

    count = 2 * tokens[0].shape[0]
    return call(
        body,
        count,
        (tokens, w_qkv),
        ("pair", None),
        (
            shape((2 * qk, count), BF),
            shape((count, heads * DV), BF),
            shape((heads * FPAD, count), BF),
            shape((heads * SPAD, DV), BF),
            shape((16, 128), BF),
        ),
        (1, 0, 1, None, None),
        [pltpu.VMEM((heads, SPAD, DV), F32), pltpu.VMEM((heads, 16, SPAD), F32)],
        2 * count * (w_qkv.size + heads * FPAD * DV * 2),
    )


def upstream_phase(qk_t, cot, w_out_half, heads):
    count = qk_t.shape[1]

    def body(qk_ref, own_ref, other_ref, w_ref, up_ref, feat_ref):
        up_ref[...] = dot(w_ref[...], either(own_ref, other_ref), (1, 1))
        query = qk_ref[...].astype(F32)
        for head in range(heads):
            feat_ref[head * FPAD : (head + 1) * FPAD, :] = features(rows_of(query, head, DK))

    return call(
        body,
        count,
        (qk_t, cot, w_out_half),
        (1, "pair", None),
        (shape((heads * DV, count), F32), shape((heads * FPAD, count), BF)),
        (1, 1),
        [],
        2 * count * w_out_half.size,
    )


def product_phase(rows_t, slabs):
    rows, count = rows_t.shape
    width = slabs[0].shape[1]

    def body(rows_ref, own_ref, other_ref, out_ref, acc):
        clear_at_first(acc)
        acc[...] += dot(rows_ref[...], either(own_ref, other_ref), (1, 0))

        @at_last
        def _():
            out_ref[...] = acc[...].T.astype(BF)

    return call(
        body,
        count,
        (rows_t, slabs),
        (1, "pair"),
        (shape((width, rows), BF),),
        (None,),
        [pltpu.VMEM((rows, width), F32)],
        2 * count * rows * width,
    )[0]


def query_phase(feats, up_t, norm, heads):
    count = up_t.shape[1]

    def body(feat_ref, up_ref, norm_ref, scale_ref, sgrad_ref, acc):
        clear_at_first(acc)
        at = lax.broadcasted_iota(jnp.int32, scale_ref.shape, 0)
        scales = jnp.zeros(scale_ref.shape, F32)
        for head in range(heads):
            feat = feat_ref[head * FPAD : (head + 1) * FPAD, :]
            parts = in_parts(head_row(norm_ref[...], head) * band_weight((1, SPAD), 1))[:, :FPAD]
            scale = 1.0 / jnp.sum(dot(parts, feat, (1, 0)), axis=0, keepdims=True)
            grad_num = (up_ref[head * DV : (head + 1) * DV, :] * scale).astype(BF)
            acc[head, :FPAD, :] += dot(feat, grad_num, (1, 1))
            scales = jnp.where(at == head, scale, scales)
        scale_ref[...] = scales

        @at_last
        def _():
            for head in range(heads):
                sgrad_ref[head * SPAD : (head + 1) * SPAD, :] = acc[head].astype(BF)

    return call(
        body,
        count,
        (feats, up_t, norm),
        (1, 1, None),
        (shape((8, count), F32), shape((heads * SPAD, DV), BF)),
        (1, None),
        [pltpu.VMEM((heads, SPAD, DV), F32)],
        2 * count * heads * FPAD * DV * 2,
    )


def attend_phase(qk_t, feats, scales, up_t, state, norm, cot, heads):
    count = up_t.shape[1]
    width = cot[0].shape[1]

    def body(
        qk_ref, feat_ref, scale_ref, up_ref, state_ref, norm_ref, own_ref, other_ref,
        att_ref, qgrad_ref, ngrad_ref, out_ref, turned, acc, out_acc,
    ):
        clear_at_first(acc, out_acc)

        @at_first
        def _():
            for head in range(heads):
                turned[head] = weighted_turned(state_ref, head)

        query = qk_ref[...].astype(F32)
        for head in range(heads):
            feat = feat_ref[head * FPAD : (head + 1) * FPAD, :]
            scale = scale_ref[head : head + 1, :]
            att = dot(turned[head, :, :FPAD], feat, (1, 0)) * scale
            grad_num = up_ref[head * DV : (head + 1) * DV, :] * scale
            grad_den = -jnp.sum(grad_num * att, axis=0, keepdims=True)
            acc[head, :, :FPAD] += dot(in_parts(grad_den), feat, (1, 1))
            fgrad = dot(state_ref[head * SPAD : head * SPAD + FPAD, :], grad_num.astype(BF), (1, 0))
            fgrad = fgrad + column(head_row(norm_ref[...], head)) * grad_den
            qgrad_ref[head * DK : (head + 1) * DK, :] = features_back(rows_of(query, head, DK), fgrad).astype(BF)
            att_ref[head * DV : (head + 1) * DV, :] = att.astype(BF)
        out_acc[...] += dot(att_ref[...], either(own_ref, other_ref), (1, 0))

        @at_last
        def _():
            ngrad_ref[...] = split_rows([jnp.sum(acc[head], axis=0, keepdims=True) for head in range(heads)])
            out_ref[...] = out_acc[...].astype(BF)

    return call(
        body,
        count,
        (qk_t, feats, scales, up_t, state, norm, cot),
        (1, 1, 1, 1, None, None, "pair"),
        (
            shape((heads * DV, count), BF),
            shape((heads * DK, count), BF),
            shape((16, 128), BF),
            shape((heads * DV, width), BF),
        ),
        (1, 1, None, None),
        [
            pltpu.VMEM((heads, DV, SPAD), BF),
            pltpu.VMEM((heads, 16, SPAD), F32),
            pltpu.VMEM((heads * DV, width), F32),
        ],
        2 * count * (heads * FPAD * DV * 4 + heads * DV * width),
    )


def mixed_phase(attended_t, w_out_half, skip, arrived, count):
    def body(att_ref, w_ref, *refs):
        part = dot(att_ref[...], w_ref[...], (0, 0))
        if len(refs) > 1:
            part = part + refs[0][...].astype(F32)
        refs[-1][...] = part.astype(BF)

    more = () if arrived is None else (arrived,)
    return call(
        body,
        count,
        (attended_t, w_out_half) + more,
        (1, None) + ("here",) * len(more),
        (shape((count, w_out_half.shape[1]), BF),),
        (0,),
        [],
        2 * count * w_out_half.size,
        skip,
    )[0]


def key_phase(qk_t, value, sgrad, ngrad, qgrad_t, tokens, heads):
    count, qk = value.shape[0], heads * DK
    width = tokens[0].shape[1]

    def body(qk_ref, value_ref, sgrad_ref, ngrad_ref, qgrad_ref, own_ref, other_ref, kgrad_ref, wgrad_ref, acc):
        clear_at_first(acc)
        keys = qk_ref[...].astype(F32)[qk:]
        found = []
        for head in range(heads):
            fgrad = dot(
                sgrad_ref[head * SPAD : head * SPAD + FPAD, :],
                value_ref[:, head * DV : (head + 1) * DV],
                (1, 1),
            )
            fgrad = fgrad + column(head_row(ngrad_ref[...], head))
            found.append(features_back(rows_of(keys, head, DK), fgrad))
        kgrad = jnp.concatenate(found, axis=0).astype(BF)
        kgrad_ref[...] = kgrad
        both = jnp.concatenate([qgrad_ref[...], kgrad], axis=0)
        acc[...] += dot(both, either(own_ref, other_ref), (1, 0))

        @at_last
        def _():
            wgrad_ref[...] = acc[...].T.astype(BF)

    return call(
        body,
        count,
        (qk_t, value, sgrad, ngrad, qgrad_t, tokens),
        (1, 0, None, None, 1, "pair"),
        (shape((qk, count), BF), shape((width, 2 * qk), BF)),
        (1, None),
        [pltpu.VMEM((2 * qk, width), F32)],
        2 * count * (heads * FPAD * DV + 2 * qk * width),
    )


def tokens_phase(qgrad_t, kgrad_t, feats, sgrad, w_qkv, heads, skip, arrived, count):
    def body(qgrad_ref, kgrad_ref, feat_ref, sgrad_ref, w_ref, *refs):
        turned = refs[-1]

        @at_first
        def _():
            for head in range(heads):
                turned[head] = weighted_turned(sgrad_ref, head)

        joined = [qgrad_ref[...], kgrad_ref[...]]
        for head in range(heads):
            feat = feat_ref[head * FPAD : (head + 1) * FPAD, :]
            joined.append(dot(turned[head, :, :FPAD], feat, (1, 0)).astype(BF))
        part = dot(jnp.concatenate(joined, axis=0), w_ref[...], (0, 1))
        if len(refs) > 2:
            part = part + refs[0][...].astype(F32)
        refs[-2][...] = part.astype(BF)

    more = () if arrived is None else (arrived,)
    return call(
        body,
        count,
        (qgrad_t, kgrad_t, feats, sgrad, w_qkv) + more,
        (1, 1, 1, None, None) + ("here",) * len(more),
        (shape((count, w_qkv.shape[0]), BF),),
        (0,),
        [pltpu.VMEM((heads, DV, SPAD), BF)],
        2 * count * (w_qkv.size + heads * FPAD * DV),
        skip,
    )[0]


def per_device(chips, tokens, w_query, w_key, w_value, w_out, cotangent):
    n = 2 * chips
    heads = H // 2
    own = tokens.shape[0]
    qk = heads * DK
    core = lax.axis_index("seq") % 2
    same_core = [[2 * p + c for p in range(chips)] for c in range(2)]
    swap = [(i, i ^ 1) for i in range(n)]
    scale_factor = (own * n) ** (-0.5)

    def exchange(x):
        return lax.ppermute(x, AXES, swap)

    def spread(x):
        return lax.all_to_all(x, AXES, 0, 0, axis_index_groups=same_core, tiled=True)

    def to_all(x):
        return jnp.broadcast_to(x[None], (chips,) + x.shape)

    def to_each(x):
        return x.reshape(chips, -1, x.shape[1])

    def add_up(x):
        return jnp.sum(x.astype(F32), axis=0)

    def fold(x):
        return jnp.concatenate([x[:, :8], x[:, 8:]], axis=2)

    def unfold(x):
        return jnp.concatenate([x[:, :, :128], x[:, :, 128:]], axis=1)

    halves = [
        jnp.concatenate(
            [
                w_query[:, c * qk : (c + 1) * qk],
                w_key[:, c * qk : (c + 1) * qk],
                w_value[:, c * heads * DV : (c + 1) * heads * DV],
            ],
            axis=1,
        )
        for c in range(2)
    ]
    to_send = jnp.broadcast_to(jnp.stack(halves)[None], (chips, 2) + halves[0].shape)
    w_qkv = lax.all_to_all(to_send.reshape((n,) + halves[0].shape), AXES, 0, 0, tiled=True)
    w_qkv = w_qkv.reshape(-1, halves[0].shape[1])
    out_rows = lax.ppermute(w_out, AXES, [(c * chips + p, 2 * p + c) for p in range(chips) for c in range(2)])
    w_out_half = spread(to_all(out_rows)).reshape(-1, out_rows.shape[1])

    tok = (tokens, exchange(tokens))
    cot = (cotangent, exchange(cotangent))

    qk_t, value, key_feat, state_part, norm_part = keys_phase(tok, w_qkv, heads)
    first = spread(jnp.concatenate([to_each(state_part), to_all(norm_part)], axis=1))
    state_own, norm = add_up(first[:, :16]).astype(BF), add_up(first[:, 16:])

    up_t, query_feat = upstream_phase(qk_t, cot, w_out_half, heads)
    moments = product_phase(key_feat, tok)
    scales, sgrad_part = query_phase(query_feat, up_t, norm, heads)
    second = spread(jnp.concatenate([to_each(sgrad_part), to_all(state_own), to_each(moments)], axis=2))
    sgrad_own = add_up(second[:, :, :128]).astype(BF)
    state = second[:, :, 128:256].reshape(-1, 128)
    moment_sum = add_up(second[:, :, 256:])

    attended_t, qgrad_t, ngrad_part, out_part = attend_phase(
        qk_t, query_feat, scales, up_t, state, norm, cot, heads
    )
    third = spread(jnp.concatenate([to_each(out_part), fold(to_all(sgrad_own)), fold(to_all(ngrad_part))], axis=2))
    width = out_part.shape[1]
    sgrad = unfold(third[:, :, width : width + 256]).reshape(-1, 128)
    ngrad = add_up(unfold(third[:, :, width + 256 :]))
    out_sum = add_up(third[:, :, :width])
    grad_out = lax.ppermute(out_sum, AXES, [(2 * p + c, c * chips + p) for p in range(chips) for c in range(2)])

    mixed_other = exchange(mixed_phase(attended_t, w_out_half, own, None, own))
    mixed = mixed_phase(attended_t, w_out_half, 0, mixed_other, own)

    kgrad_t, wgrad = key_phase(qk_t, value, sgrad, ngrad, qgrad_t, tok, heads)
    fourth = lax.all_to_all(wgrad.reshape(n, -1, wgrad.shape[1]), AXES, 0, 0, tiled=True)
    wgrad_sum = jnp.sum(fourth.reshape((chips, 2) + fourth.shape[1:]).astype(F32), axis=0) * scale_factor
    gtok_other = exchange(tokens_phase(qgrad_t, kgrad_t, key_feat, sgrad, w_qkv, heads, own, None, own))
    grad_tokens = tokens_phase(qgrad_t, kgrad_t, key_feat, sgrad, w_qkv, heads, 0, gtok_other, own)

    weight = band_weight((1, FPAD), 1)
    gvalue = jnp.concatenate(
        [
            jnp.dot(
                moment_sum[:, h * FPAD : (h + 1) * FPAD] * weight,
                sgrad[h * SPAD : h * SPAD + FPAD].astype(F32),
                precision=lax.Precision.HIGH,
            )
            for h in range(heads)
        ],
        axis=1,
    )
    rows = gvalue.shape[0] // 2
    got = exchange(lax.dynamic_slice_in_dim(gvalue, (1 - core) * rows, rows, 0))
    kept = lax.dynamic_slice_in_dim(gvalue, core * rows, rows, 0)
    low, high = jnp.where(core == 0, kept, got), jnp.where(core == 0, got, kept)
    grad_value = jnp.concatenate([low, high], axis=1) * scale_factor
    grad_query = jnp.concatenate([wgrad_sum[0, :, :qk], wgrad_sum[1, :, :qk]], axis=1)
    grad_key = jnp.concatenate([wgrad_sum[0, :, qk:], wgrad_sum[1, :, qk:]], axis=1)
    return (mixed, grad_tokens, grad_query, grad_key, grad_value, grad_out * scale_factor)


def solution(mesh):
    chips = mesh.size // 2
    placed = P(AXES, None)
    return jax.shard_map(
        lambda *args: per_device(chips, *args),
        mesh=mesh,
        in_specs=(placed,) * 6,
        out_specs=(placed,) * 6,
        check_vma=False,
    )
```

```python
import jax
import jax.numpy as jnp
from jax import lax
from jax.experimental import pallas as pl
from jax.experimental.pallas import tpu as pltpu
from jax.sharding import PartitionSpec as P

H = 8
DK = 16
DV = 128
BANDS = DK // 2 + 1
FPAD = (BANDS + 2) * DK
SPAD = 256
AXES = ("ctx", "seq")
VMEM = 60 * 2**20
BF = jnp.bfloat16
F32 = jnp.float32
SQUARE = (2.0 * DK) ** (-0.5)
LINEAR = DK ** (-0.25)


def dot(a, b, contract):
    return lax.dot_general(a, b, ((contract[:1], contract[1:]), ((), ())), preferred_element_type=F32)


def band_weight(shape, dim):
    row = lax.broadcasted_iota(jnp.int32, shape, dim)
    twice = (row >= DK) & (row < (BANDS - 1) * DK)
    return jnp.where(twice, 2.0, 1.0).astype(F32)


def shifted(u, d):
    return pltpu.roll(u, DK - d, 0) if d else u


def features(u):
    bands = [u * shifted(u, d) * SQUARE for d in range(BANDS)]
    first = lax.broadcasted_iota(jnp.int32, u.shape, 0) == 0
    return jnp.concatenate(bands + [u * LINEAR, jnp.where(first, 1.0, 0.0)], axis=0).astype(BF)


def features_back(u, fgrad):
    def band(d):
        return fgrad[d * DK : (d + 1) * DK]

    total = band(0) * u + band(BANDS - 1) * shifted(u, BANDS - 1)
    for d in range(1, BANDS - 1):
        total = total + band(d) * shifted(u, d) + shifted(band(d) * u, DK - d)
    return total * (2.0 * SQUARE) + band(BANDS) * LINEAR


def in_parts(row):
    high = row.astype(BF).astype(F32)
    rest = row - high
    mid = rest.astype(BF).astype(F32)
    at = lax.broadcasted_iota(jnp.int32, (16, row.shape[1]), 0)
    low = jnp.where(at == 2, rest - mid, 0.0)
    return jnp.where(at == 0, high, jnp.where(at == 1, mid, low)).astype(BF)


def rows_of(array, head, size):
    return array[head * size : (head + 1) * size]


def head_row(rows, head):
    first, second = rows[4 * head : 4 * head + 2, :], rows[4 * head + 2 : 4 * head + 4, :]
    both = first + second
    return jnp.concatenate([both[:1], both[1:]], axis=1)


def split_rows(per_head):
    found = []
    for row in per_head:
        high = row.astype(BF).astype(F32)
        for part in (high, row - high):
            found += [part[:, :128], part[:, 128:]]
    found += [jnp.zeros((1, 128), F32)] * (16 - len(found))
    return jnp.concatenate(found, axis=0).astype(BF)


def column(row):
    return jnp.broadcast_to(row, (8, row.shape[1])).T[:FPAD, :1]


def add_chips(ref, rows):
    total = ref[:rows, :].astype(F32)
    for at in range(rows, ref.shape[0], rows):
        total = total + ref[at : at + rows, :].astype(F32)
    return total


def lane_sums(x):
    return sum(x[:, i : i + 128] for i in range(0, x.shape[1], 128))


def weighted_turned(state_ref, head):
    whole = state_ref[head * SPAD : (head + 1) * SPAD, :].astype(F32)
    return (whole * band_weight((SPAD, DV), 0)).T.astype(BF)


def call(body, count, ins, kinds, outs, out_kinds, scratch, flops):
    block = min(512, count, count // 2 if "pair" in kinds else count)
    steps = count // block
    in_specs, args = [], []
    for x, kind in zip(ins, kinds):
        if kind is None:
            in_specs.append(pl.BlockSpec(x.shape, lambda i: (0, 0)))
        elif kind == 0:
            in_specs.append(pl.BlockSpec((block, x.shape[1]), lambda i: (i, 0)))
        elif kind == 1:
            in_specs.append(pl.BlockSpec((x.shape[0], block), lambda i: (0, i)))
        elif kind == "scalar":
            in_specs.append(pl.BlockSpec(memory_space=pltpu.SMEM))
        elif kind == "any":
            in_specs.append(pl.BlockSpec(memory_space=pl.ANY))
        elif isinstance(kind, tuple):
            width, at = kind
            in_specs.append(pl.BlockSpec((x.shape[0], width), lambda i, at=at: (0, at)))
        elif kind == "pair1":
            half = steps // 2
            in_specs.append(pl.BlockSpec((x[0].shape[0], block), lambda i: (0, jnp.minimum(i, half - 1))))
            in_specs.append(pl.BlockSpec((x[0].shape[0], block), lambda i: (0, jnp.maximum(i - half, 0))))
        else:
            half = steps // 2
            in_specs.append(pl.BlockSpec((block, x[0].shape[1]), lambda i: (jnp.minimum(i, half - 1), 0)))
            in_specs.append(pl.BlockSpec((block, x[0].shape[1]), lambda i: (jnp.maximum(i - half, 0), 0)))
        args += list(x) if kind in ("pair", "pair1") else [x]
    out_specs = []
    for x, kind in zip(outs, out_kinds):
        half = steps // 2
        if kind == "first":
            out_specs.append(pl.BlockSpec((x.shape[0], block), lambda i: (0, jnp.minimum(i, half - 1))))
            continue
        if kind == "second":
            out_specs.append(pl.BlockSpec((x.shape[0], block), lambda i: (0, jnp.maximum(i - half, 0))))
            continue
        if kind is None:
            out_specs.append(pl.BlockSpec(x.shape, lambda i: (0, 0)))
        elif kind == 0:
            out_specs.append(pl.BlockSpec((block, x.shape[1]), lambda i: (i, 0)))
        else:
            out_specs.append(pl.BlockSpec((x.shape[0], block), lambda i: (0, i)))
    nbytes = sum(x.size * x.dtype.itemsize for x in args + list(outs))
    return pl.pallas_call(
        body,
        grid=(steps,),
        in_specs=in_specs,
        out_specs=out_specs,
        out_shape=outs,
        scratch_shapes=scratch,
        compiler_params=pltpu.CompilerParams(dimension_semantics=("arbitrary",), vmem_limit_bytes=VMEM),
        cost_estimate=pl.CostEstimate(flops=flops, bytes_accessed=nbytes, transcendentals=0),
    )(*args)


def either(first_ref, second_ref):
    return jnp.where(pl.program_id(0) < pl.num_programs(0) // 2, first_ref[...], second_ref[...])


def store_half(first_ref, second_ref, value):
    @pl.when(pl.program_id(0) < pl.num_programs(0) // 2)
    def _():
        first_ref[...] = value

    @pl.when(pl.program_id(0) >= pl.num_programs(0) // 2)
    def _():
        second_ref[...] = value


def shape(dims, dtype):
    return jax.ShapeDtypeStruct(dims, dtype)


def clear_at_first(*refs):
    @pl.when(pl.program_id(0) == 0)
    def _():
        for ref in refs:
            ref[...] = jnp.zeros(ref.shape, ref.dtype)


def at_first(fn):
    pl.when(pl.program_id(0) == 0)(fn)


def at_last(fn):
    pl.when(pl.program_id(0) == pl.num_programs(0) - 1)(fn)


def weights_phase(w_query, w_key, w_value, w_out, chips, heads):
    qk, cols, half = heads * DK, heads * DV, w_out.shape[1] // 2

    def body(q_ref, k_ref, v_ref, o_ref, out_ref):
        query, key, value, rest = (ref[...].astype(F32) for ref in (q_ref, k_ref, v_ref, o_ref))
        halves = [
            jnp.concatenate(
                [
                    query[:, c * qk : (c + 1) * qk],
                    key[:, c * qk : (c + 1) * qk],
                    value[:, c * cols : (c + 1) * cols],
                    rest[:, c * half : (c + 1) * half],
                ],
                axis=1,
            )
            for c in range(2)
        ]
        pair = jnp.concatenate(halves, axis=0).astype(BF)
        for p in range(chips):
            out_ref[p * pair.shape[0] : (p + 1) * pair.shape[0], :] = pair

    rows = w_query.shape[0]
    return pl.pallas_call(
        body,
        out_shape=shape((2 * chips * rows, 2 * qk + cols + half), BF),
        compiler_params=pltpu.CompilerParams(vmem_limit_bytes=VMEM),
        cost_estimate=pl.CostEstimate(flops=0, bytes_accessed=2 * 2 * chips * rows * (2 * qk + cols + half), transcendentals=0),
    )(w_query, w_key, w_value, w_out)


def keys_phase(tokens, w_qkv, chips, heads):
    qk = heads * DK

    def body(own_ref, other_ref, w_ref, qk_ref, value_ref, feat_ref, feat_other_ref, sent_ref, state_acc, norm_acc):
        clear_at_first(state_acc, norm_acc)
        joined = dot(either(own_ref, other_ref), w_ref[:, : 2 * qk + heads * DV], (1, 0))
        qk_t = joined[:, : 2 * qk].T.astype(BF)
        value = joined[:, 2 * qk :].astype(BF)
        qk_ref[...] = qk_t
        value_ref[...] = value
        keys = qk_t.astype(F32)[qk:]
        found = []
        for head in range(heads):
            feat = features(rows_of(keys, head, DK))
            found.append(feat)
            state_acc[head, :FPAD, :] += dot(feat, value[:, head * DV : (head + 1) * DV], (1, 0))
            norm_acc[head, :FPAD, :] += lane_sums(feat.astype(F32))
        store_half(feat_ref, feat_other_ref, jnp.concatenate(found, axis=0))

        @at_last
        def _():
            norm = split_rows([jnp.sum(norm_acc[head], axis=1)[None] for head in range(heads)])
            state = state_acc[...].reshape(heads * SPAD, DV).astype(BF)
            part = heads * SPAD // chips
            for p in range(chips):
                sent_ref[2 * part * p : 2 * part * p + part, :] = state[part * p : part * (p + 1)]
                sent_ref[2 * part * p + part : 2 * part * (p + 1), :] = norm

    count = 2 * tokens[0].shape[0]
    return call(
        body,
        count,
        (tokens, w_qkv),
        ("pair", None),
        (
            shape((2 * qk, count), BF),
            shape((count, heads * DV), BF),
            shape((heads * FPAD, count // 2), BF),
            shape((heads * FPAD, count // 2), BF),
            shape((2 * heads * SPAD, DV), BF),
        ),
        (1, 0, "first", "second", None),
        [pltpu.VMEM((heads, SPAD, DV), F32), pltpu.VMEM((heads, SPAD, 128), F32)],
        2 * count * heads * (w_qkv.shape[0] * (2 * DK + DV) + FPAD * DV * 2),
    )


def upstream_phase(core, qk_t, cot, weights, other_weights, heads):
    count, width = qk_t.shape[1], cot[0].shape[1]
    rows, half = heads * DV, width // 2
    joined = 2 * heads * DK + heads * DV

    def body(core_ref, qk_ref, own_ref, other_ref, mine_ref, theirs_ref, up_ref, feat_ref, w_ref):
        at = core_ref[0, 0]

        @at_first
        def _():
            mine, theirs = mine_ref[:, joined:], theirs_ref[:, joined:]
            w_ref[:, :half] = jnp.where(at == 0, mine, theirs)
            w_ref[:, half:] = jnp.where(at == 0, theirs, mine)

        here = w_ref[pl.ds(pl.multiple_of(at * rows, rows), rows), :]
        up_ref[...] = dot(here, either(own_ref, other_ref), (1, 1))
        query = qk_ref[...].astype(F32)
        for head in range(heads):
            feat_ref[head * FPAD : (head + 1) * FPAD, :] = features(rows_of(query, head, DK))

    return call(
        body,
        count,
        (core, qk_t, cot, weights, other_weights),
        ("scalar", 1, "pair", None, None),
        (shape((rows, count), F32), shape((heads * FPAD, count), BF), shape((2 * rows, width), BF)),
        (1, 1, None),
        [],
        2 * count * rows * width,
    )


def product_phase(rows_t, slabs, after, parts):
    rows, count = rows_t[0].shape[0], 2 * rows_t[0].shape[1]
    size = rows // parts
    width = slabs[0].shape[1]

    def body(rows_ref, rows_other_ref, own_ref, other_ref, after_ref, out_ref, acc):
        clear_at_first(acc)
        acc[...] += dot(either(rows_ref, rows_other_ref), either(own_ref, other_ref), (1, 0))

        @at_last
        def _():
            for part in range(parts):
                out_ref[part * width : (part + 1) * width, :] = acc[part * size : (part + 1) * size, :].T.astype(BF)

    return call(
        body,
        count,
        (rows_t, slabs, after),
        ("pair1", "pair", "any"),
        (shape((parts * width, size), BF),),
        (None,),
        [pltpu.VMEM((rows, width), F32)],
        2 * count * rows * width,
    )[0]


def query_phase(feats, up_t, first, chips, heads):
    count = up_t.shape[1]
    part = heads * SPAD // chips

    def body(feat_ref, up_ref, first_ref, scale_ref, norm_ref, sent_ref, acc, state_own):
        clear_at_first(acc)

        @at_first
        def _():
            total = add_chips(first_ref, 2 * part)
            state_own[...] = total[:part].astype(BF)
            norm_ref[...] = total[part:]

        at = lax.broadcasted_iota(jnp.int32, scale_ref.shape, 0)
        scales = jnp.zeros(scale_ref.shape, F32)
        for head in range(heads):
            feat = feat_ref[head * FPAD : (head + 1) * FPAD, :]
            parts = in_parts(head_row(norm_ref[...], head) * band_weight((1, SPAD), 1))[:, :FPAD]
            scale = 1.0 / jnp.sum(dot(parts, feat, (1, 0)), axis=0, keepdims=True)
            grad_num = (up_ref[head * DV : (head + 1) * DV, :] * scale).astype(BF)
            acc[head, :FPAD, :] += dot(feat, grad_num, (1, 1))
            scales = jnp.where(at == head, scale, scales)
        scale_ref[...] = scales

        @at_last
        def _():
            sent_ref[:, :DV] = acc[...].reshape(heads * SPAD, DV).astype(BF)
            for p in range(chips):
                sent_ref[p * part : (p + 1) * part, DV:] = state_own[...]

    return call(
        body,
        count,
        (feats, up_t, first),
        (1, 1, None),
        (shape((8, count), F32), shape((16, 128), F32), shape((heads * SPAD, 2 * DV), BF)),
        (1, None, None),
        [pltpu.VMEM((heads, SPAD, DV), F32), pltpu.VMEM((part, DV), BF)],
        2 * count * heads * FPAD * DV * 2,
    )


def attend_phase(feats, scales, up_t, second, cot, moments, chips, heads):
    count = up_t.shape[1]
    width = cot[0].shape[1]
    quarter = width // 4

    def body(
        feat_ref, scale_ref, up_ref, state_ref, sgrad_ref, own_ref, other_ref, moment_ref,
        att_ref, att_other_ref, den_ref, out_ref, sent_ref, turned, acc, out_acc,
    ):
        clear_at_first(acc, out_acc)

        @at_first
        def _():
            for head in range(heads):
                turned[head] = weighted_turned(state_ref, head)

        at = lax.broadcasted_iota(jnp.int32, den_ref.shape, 0)
        dens = jnp.zeros(den_ref.shape, F32)
        found = []
        for head in range(heads):
            feat = feat_ref[head * FPAD : (head + 1) * FPAD, :]
            scale = scale_ref[head : head + 1, :]
            att = dot(turned[head, :, :FPAD], feat, (1, 0)) * scale
            grad_num = up_ref[head * DV : (head + 1) * DV, :] * scale
            grad_den = -jnp.sum(grad_num * att, axis=0, keepdims=True)
            acc[head, :FPAD, :] += lane_sums(feat.astype(F32) * grad_den)
            found.append(att.astype(BF))
            dens = jnp.where(at == head, grad_den, dens)
        den_ref[...] = dens
        attended = jnp.concatenate(found, axis=0)
        store_half(att_ref, att_other_ref, attended)
        out_acc[...] += dot(attended, either(own_ref, other_ref), (1, 0))

        @at_last
        def _():
            ngrad = split_rows([jnp.sum(acc[head], axis=1)[None] for head in range(heads)])
            sgrad_own = add_chips(sgrad_ref, ngrad.shape[0]).astype(BF)
            both = jnp.concatenate([sgrad_own, ngrad], axis=1)
            for p in range(chips):
                sent_ref[p * both.shape[0] : (p + 1) * both.shape[0], :] = both
            for k in range(4):
                rows = slice(k * heads * DV, (k + 1) * heads * DV)
                out_ref[rows, :quarter] = out_acc[:, k * quarter : (k + 1) * quarter].astype(BF)
                for j in range(2):
                    part = moment_ref[(2 * k + j) * heads * DV : (2 * k + j + 1) * heads * DV, :]
                    out_ref[rows, quarter + j * FPAD : quarter + (j + 1) * FPAD] = part

    return call(
        body,
        count,
        (feats, scales, up_t, second, second, cot, moments),
        (1, 1, 1, (DV, 1), (DV, 0), "pair", None),
        (
            shape((heads * DV, count // 2), BF),
            shape((heads * DV, count // 2), BF),
            shape((8, count), F32),
            shape((4 * heads * DV, quarter + 2 * FPAD), BF),
            shape(second.shape, BF),
        ),
        ("first", "second", 1, None, None),
        [
            pltpu.VMEM((heads, DV, SPAD), BF),
            pltpu.VMEM((heads, SPAD, 128), F32),
            pltpu.VMEM((heads * DV, width), F32),
        ],
        2 * count * (heads * FPAD * DV * 2 + heads * DV * width),
    )


def query_back_phase(qk_t, scales, dens, up_t, second, norm, heads):
    count = up_t.shape[1]

    def body(qk_ref, scale_ref, den_ref, up_ref, state_ref, norm_ref, qgrad_ref, qgrad_other_ref):
        query = qk_ref[...].astype(F32)
        found = []
        for head in range(heads):
            grad_num = (up_ref[head * DV : (head + 1) * DV, :] * scale_ref[head : head + 1, :]).astype(BF)
            fgrad = dot(state_ref[head * SPAD : head * SPAD + FPAD, :], grad_num, (1, 0))
            fgrad = fgrad + column(head_row(norm_ref[...], head)) * den_ref[head : head + 1, :]
            found.append(features_back(rows_of(query, head, DK), fgrad).astype(BF))
        store_half(qgrad_ref, qgrad_other_ref, jnp.concatenate(found, axis=0))

    return call(
        body,
        count,
        (qk_t, scales, dens, up_t, second, norm),
        (1, 1, 1, 1, (DV, 1), None),
        (shape((heads * DK, count // 2), BF), shape((heads * DK, count // 2), BF)),
        ("first", "second"),
        [],
        2 * count * heads * FPAD * DV,
    )


def key_phase(qk_t, value, third, qgrads, tokens, after, heads):
    count, qk = value.shape[0], heads * DK
    width = tokens[0].shape[1]

    def body(
        qk_ref, value_ref, sgrad_ref, rows_ref, qgrad_ref, qgrad_other_ref, own_ref, other_ref, after_ref,
        kgrad_ref, kgrad_other_ref, copy_ref, sent_ref, acc, ngrad_ref,
    ):
        clear_at_first(acc)

        @at_first
        def _():
            ngrad_ref[...] = add_chips(rows_ref, 16)
            copy_ref[...] = sgrad_ref[...]

        keys = qk_ref[...].astype(F32)[qk:]
        found = []
        for head in range(heads):
            fgrad = dot(
                sgrad_ref[head * SPAD : head * SPAD + FPAD, :],
                value_ref[:, head * DV : (head + 1) * DV],
                (1, 1),
            )
            fgrad = fgrad + column(head_row(ngrad_ref[...], head))
            found.append(features_back(rows_of(keys, head, DK), fgrad))
        kgrad = jnp.concatenate(found, axis=0).astype(BF)
        store_half(kgrad_ref, kgrad_other_ref, kgrad)
        both = jnp.concatenate([either(qgrad_ref, qgrad_other_ref), kgrad], axis=0)
        acc[...] += dot(both, either(own_ref, other_ref), (1, 0))

        @at_last
        def _():
            sent_ref[...] = acc[...].T.astype(BF)

    return call(
        body,
        count,
        (qk_t, value, third, third, qgrads, tokens, after),
        (1, 0, (DV, 0), (DV, 1), "pair1", "pair", "any"),
        (
            shape((qk, count // 2), BF),
            shape((qk, count // 2), BF),
            shape((third.shape[0], DV), BF),
            shape((width, 2 * qk), BF),
        ),
        ("first", "second", None, None),
        [pltpu.VMEM((2 * qk, width), F32), pltpu.VMEM((16, DV), F32)],
        2 * count * (heads * FPAD * DV + 2 * qk * width),
    )


def last_payload(core, wgrad, along_x):
    rows, cols = wgrad.shape
    half = along_x.shape[0]
    quarter = along_x.shape[1] - 2 * FPAD

    def body(core_ref, wgrad_ref, terms_ref, sent_ref):
        first = core_ref[0, 0] == 0
        sent_ref[:, :cols] = wgrad_ref[...]
        for j in range(2):
            here = slice(j * half, (j + 1) * half)
            sent_ref[here, cols : cols + FPAD] = terms_ref[:, quarter + j * FPAD : quarter + (j + 1) * FPAD]
            out = terms_ref[:, :quarter]
            sent_ref[here, cols + FPAD :] = jnp.where(first == (j == 0), out, jnp.zeros_like(out))

    vmem = pl.BlockSpec(memory_space=pltpu.VMEM)
    return pl.pallas_call(
        body,
        in_specs=[pl.BlockSpec(memory_space=pltpu.SMEM)] + [vmem] * 2,
        out_specs=vmem,
        out_shape=shape((rows, cols + FPAD + quarter), BF),
        compiler_params=pltpu.CompilerParams(vmem_limit_bytes=VMEM),
        cost_estimate=pl.CostEstimate(flops=0, bytes_accessed=4 * rows * cols, transcendentals=0),
    )(core, wgrad, along_x)


def outputs_phase(core, attended, qgrads, kgrads, feats, sgrads, weights, w_out, heads):
    count, width = attended[0].shape[1], w_out.shape[1]
    rows, joined = heads * DV, 2 * heads * DK + heads * DV

    def body(core_ref, *refs):
        atts, qs, ks, fs, ss, ws = (refs[2 * i : 2 * i + 2] for i in range(6))
        out_ref, mixed_ref, gtok_ref, turned = refs[12:]
        at = core_ref[0, 0]

        @at_first
        def _():
            for c in range(2):
                for head in range(heads):
                    turned[c, head] = weighted_turned(ss[c], head)

        mixed, gtok = 0.0, 0.0
        for c in range(2):
            first = pl.multiple_of((at if c == 0 else 1 - at) * rows, rows)
            mixed = mixed + dot(atts[c][...], out_ref[pl.ds(first, rows), :], (0, 0))
            parts = [qs[c][...], ks[c][...]]
            for head in range(heads):
                feat = fs[c][head * FPAD : (head + 1) * FPAD, :]
                parts.append(dot(turned[c, head, :, :FPAD], feat, (1, 0)).astype(BF))
            gtok = gtok + dot(jnp.concatenate(parts, axis=0), ws[c][:, :joined], (0, 1))
        mixed_ref[...] = mixed.astype(BF)
        gtok_ref[...] = gtok.astype(BF)

    return call(
        body,
        count,
        (core, *attended, *qgrads, *kgrads, *feats, *sgrads, *weights, w_out),
        ("scalar",) + (1,) * 8 + (None,) * 5,
        (shape((count, width), BF), shape((count, width), BF)),
        (0, 0),
        [pltpu.VMEM((2, heads, DV, SPAD), BF)],
        2 * count * 2 * (joined * width + rows * width + heads * FPAD * DV),
    )


def finish_phase(core, fourth, sgrads, after, heads, scale_factor):
    rows, qk, n = 8, heads * DK, fourth.shape[0] // 8
    quarter = fourth.shape[1] - 2 * qk - FPAD

    def body(core_ref, recv_ref, mine_ref, other_ref, *refs):
        query_ref, key_ref, value_ref, out_ref = refs[-4:]
        first = core_ref[0, 0] == 0
        wgrad = jnp.zeros((2 * rows, 2 * qk), F32)
        moment = [jnp.zeros((2 * rows, FPAD), F32) for _ in range(heads)]
        out = [jnp.zeros((2 * rows, quarter), F32) for _ in range(4)]
        for p in range(n // 2):
            both = recv_ref[2 * rows * p : 2 * rows * (p + 1), :].astype(F32)
            x = 2 * ((p // 8) % 2) + p % 2
            wgrad = wgrad + both[:, : 2 * qk]
            moment[x] = moment[x] + both[:, 2 * qk : 2 * qk + FPAD]
            out[x] = out[x] + both[:, 2 * qk + FPAD :]
        for x in range(4):
            out_ref[:, x * quarter : (x + 1) * quarter] = (out[x][:rows] + out[x][rows:]) * scale_factor
        wgrad = wgrad * scale_factor
        query_ref[...] = jnp.concatenate([wgrad[:rows, :qk], wgrad[rows:, :qk]], axis=1)
        key_ref[...] = jnp.concatenate([wgrad[:rows, qk:], wgrad[rows:, qk:]], axis=1)
        weight = band_weight((1, FPAD), 1) * scale_factor
        found = [[], []]
        for head in range(heads):
            whole = moment[head] * weight
            high = whole.astype(BF)
            parts = jnp.concatenate([high, (whole - high.astype(F32)).astype(BF)], axis=0)
            for which, ref in enumerate((mine_ref, other_ref)):
                both = dot(parts, ref[head * SPAD : head * SPAD + FPAD, :], (1, 0))
                both = both[: 2 * rows] + both[2 * rows :]
                low, up = both[:rows], both[rows:]
                found[which].append(jnp.where(first, low, up) if which == 0 else jnp.where(first, up, low))
        mine, other = (jnp.concatenate(part, axis=1) for part in found)
        value_ref[:, : heads * DV] = jnp.where(first, mine, other)
        value_ref[:, heads * DV :] = jnp.where(first, other, mine)

    vmem = pl.BlockSpec(memory_space=pltpu.VMEM)
    return pl.pallas_call(
        body,
        in_specs=[pl.BlockSpec(memory_space=pltpu.SMEM)] + [vmem] * 3 + [pl.BlockSpec(memory_space=pl.ANY)] * len(after),
        out_specs=[vmem] * 4,
        out_shape=(
            shape((rows, 2 * qk), F32),
            shape((rows, 2 * qk), F32),
            shape((rows, 2 * heads * DV), F32),
            shape((rows, 4 * quarter), F32),
        ),
        compiler_params=pltpu.CompilerParams(vmem_limit_bytes=VMEM),
        cost_estimate=pl.CostEstimate(flops=0, bytes_accessed=fourth.size * 2, transcendentals=0),
    )(core, fourth, *sgrads, *after)


def per_device(chips, tokens, w_query, w_key, w_value, w_out, cotangent):
    n = 2 * chips
    heads = H // 2
    own, width = tokens.shape
    qk = heads * DK
    core = lax.axis_index("seq") % 2
    core_at = core.astype(jnp.int32).reshape(1, 1)
    same_core = [[2 * p + c for p in range(chips)] for c in range(2)]
    swap = [(i, i ^ 1) for i in range(n)]
    scale_factor = (own * n) ** (-0.5)

    def exchange(x):
        return lax.ppermute(x, AXES, swap)

    def spread(x):
        return lax.all_to_all(x, AXES, 0, 0, axis_index_groups=same_core, tiled=True)

    def add_along_x(x):
        quarters = x.reshape((4, -1) + x.shape[1:])
        total = lax.dynamic_index_in_dim(quarters, me_x, 0, keepdims=False).astype(F32)
        for step in (1, 2, 3):
            moves = []
            for i in range(n):
                y, at, z, c = place(i)
                moves.append((i, device(y, (at + step) % 4, z, c)))
            there = lax.dynamic_index_in_dim(quarters, (me_x + step) % 4, 0, keepdims=False)
            total = total + lax.ppermute(there, AXES, moves).astype(F32)
        return total.astype(BF)

    def place(i):
        return (i // 32, 2 * (i // 16 % 2) + i // 2 % 2, i // 4 % 4, i % 2)

    def device(y, x, z, c):
        return (((y * 2 + x // 2) * 4 + z) * 2 + x % 2) * 2 + c

    def to_each(x):
        return x.reshape(chips, -1, x.shape[1])

    ctx, seq = lax.axis_index("ctx"), lax.axis_index("seq")
    me_x = 2 * (ctx // 4 % 2) + seq // 2
    along_x = [[device(y, x, z, c) for x in range(4)] for y in range(4) for z in range(4) for c in range(2)]

    to_send = weights_phase(w_query, w_key, w_value, w_out, chips, heads)
    weights = lax.all_to_all(to_send.reshape(n, -1, to_send.shape[1]), AXES, 0, 0, tiled=True)
    weights = weights.reshape(-1, to_send.shape[1])
    tok = (tokens, exchange(tokens))
    cot = (cotangent, exchange(cotangent))
    other_weights = exchange(weights)

    qk_t, value, key_feat, key_feat_sent, sent = keys_phase(tok, weights, chips, heads)
    first = spread(to_each(sent)).reshape(sent.shape)
    key_feats = (key_feat, exchange(key_feat_sent))

    up_t, query_feat, w_out_whole = upstream_phase(core_at, qk_t, cot, weights, other_weights, heads)
    scales, norm, sent = query_phase(query_feat, up_t, first, chips, heads)
    second = spread(to_each(sent)).reshape(sent.shape)
    moments = product_phase((key_feat, key_feat_sent), tok, sent, heads)

    attended, attended_sent, dens, terms, sent = attend_phase(
        query_feat, scales, up_t, second, cot, moments, chips, heads
    )
    third = spread(to_each(sent)).reshape(sent.shape)
    terms = add_along_x(terms)
    attendeds = (attended, exchange(attended_sent))
    qgrad, qgrad_sent = query_back_phase(qk_t, scales, dens, up_t, second, norm, heads)
    qgrads = (qgrad, exchange(qgrad_sent))

    kgrad, kgrad_sent, sgrad, wgrad = key_phase(qk_t, value, third, (qgrad, qgrad_sent), tok, terms, heads)
    sent = last_payload(core_at, wgrad, terms)
    fourth = lax.all_to_all(sent.reshape(n, -1, sent.shape[1]), AXES, 0, 0, tiled=True).reshape(sent.shape)
    kgrads, sgrads = (kgrad, exchange(kgrad_sent)), (sgrad, exchange(sgrad))
    mixed, grad_tokens = outputs_phase(
        core_at, attendeds, qgrads, kgrads, key_feats, sgrads, (weights, other_weights), w_out_whole, heads
    )
    grad_query, grad_key, grad_value, grad_out = finish_phase(
        core_at, fourth, sgrads, (grad_tokens, mixed), heads, scale_factor
    )
    return (mixed, grad_tokens, grad_query, grad_key, grad_value, grad_out)


def solution(mesh):
    chips = mesh.size // 2
    placed = P(AXES, None)
    return jax.shard_map(
        lambda *args: per_device(chips, *args),
        mesh=mesh,
        in_specs=(placed,) * 6,
        out_specs=(placed,) * 6,
        check_vma=False,
    )
```

```python
import jax
import jax.numpy as jnp
from jax import lax
from jax.experimental import pallas as pl
from jax.experimental.pallas import tpu as pltpu
from jax.sharding import PartitionSpec as P

H = 8
DK = 16
DV = 128
BANDS = DK // 2 + 1
FPAD = (BANDS + 2) * DK
SPAD = 256
AXES = ("ctx", "seq")
BLOCK = 512
VMEM = 60 * 2**20
BF = jnp.bfloat16
F32 = jnp.float32
SQUARE = (2.0 * DK) ** (-0.5)
LINEAR = DK ** (-0.25)


def dot(a, b, contract):
    return lax.dot_general(a, b, ((contract[:1], contract[1:]), ((), ())), preferred_element_type=F32)


def band_weight(shape, dim):
    row = lax.broadcasted_iota(jnp.int32, shape, dim)
    twice = (row >= DK) & (row < (BANDS - 1) * DK)
    return jnp.where(twice, 2.0, 1.0).astype(F32)


def shifted(u, d):
    return pltpu.roll(u, DK - d, 0) if d else u


def features(u):
    bands = [u * shifted(u, d) * SQUARE for d in range(BANDS)]
    first = lax.broadcasted_iota(jnp.int32, u.shape, 0) == 0
    return jnp.concatenate(bands + [u * LINEAR, jnp.where(first, 1.0, 0.0)], axis=0).astype(BF)


def features_back(u, fgrad):
    def band(d):
        return fgrad[d * DK : (d + 1) * DK]

    total = band(0) * u + band(BANDS - 1) * shifted(u, BANDS - 1)
    for d in range(1, BANDS - 1):
        total = total + band(d) * shifted(u, d) + shifted(band(d) * u, DK - d)
    return total * (2.0 * SQUARE) + band(BANDS) * LINEAR


def in_parts(row):
    high = row.astype(BF).astype(F32)
    rest = row - high
    mid = rest.astype(BF).astype(F32)
    at = lax.broadcasted_iota(jnp.int32, (16, row.shape[1]), 0)
    low = jnp.where(at == 2, rest - mid, 0.0)
    return jnp.where(at == 0, high, jnp.where(at == 1, mid, low)).astype(BF)


def rows_of(array, head, size):
    return array[head * size : (head + 1) * size]


def head_row(rows, head):
    first, second = rows[4 * head : 4 * head + 2, :], rows[4 * head + 2 : 4 * head + 4, :]
    both = first + second
    return jnp.concatenate([both[:1], both[1:]], axis=1)


def split_rows(per_head):
    found = []
    for row in per_head:
        high = row.astype(BF).astype(F32)
        for part in (high, row - high):
            found += [part[:, :128], part[:, 128:]]
    found += [jnp.zeros((1, 128), F32)] * (16 - len(found))
    return jnp.concatenate(found, axis=0).astype(BF)


def column(row):
    return jnp.broadcast_to(row, (8, row.shape[1])).T[:FPAD, :1]


def add_chips(ref, rows):
    total = ref[:rows, :].astype(F32)
    for at in range(rows, ref.shape[0], rows):
        total = total + ref[at : at + rows, :].astype(F32)
    return total


def lane_sums(x):
    return sum(x[:, i : i + 128] for i in range(0, x.shape[1], 128))


def weighted_turned(state_ref, head):
    whole = state_ref[head * SPAD : (head + 1) * SPAD, :].astype(F32)
    return (whole * band_weight((SPAD, DV), 0)).T.astype(BF)


def call(body, count, ins, kinds, outs, out_kinds, scratch, flops):
    block = min(BLOCK, count // 2 if "pair" in kinds or "pair1" in out_kinds else count)
    steps = count // block

    def pieces(x, kind):
        if kind in ("pair", "pair1"):
            half = steps // 2
            return pieces_of(0, half, x[0].shape, kind) + pieces_of(1, half, x[1].shape, kind)
        if kind in (0, 1):
            return pieces_of(0, steps, x.shape, kind)
        if kind is not None and kind[0] == "from":
            return [(0, pl.ds(0, x.shape[0]), pl.ds(kind[1], x.shape[1] - kind[1]))]
        if kind is not None:
            return [(0, pl.ds(0, x.shape[0]), pl.ds(kind[0] * kind[1], kind[0]))]
        return [(0, pl.ds(0, x.shape[0]), pl.ds(0, x.shape[1]))]

    def pieces_of(which, number, dims, kind):
        if kind in (0, "pair"):
            return [(which, pl.ds(i * block, block), pl.ds(0, dims[1])) for i in range(number)]
        return [(which, pl.ds(0, dims[0]), pl.ds(i * block, block)) for i in range(number)]

    def members(x, kind):
        return list(x) if kind in ("pair", "pair1") else [x]

    plans = [[] if kind in ("scalar", "any") else pieces(x, kind) for x, kind in zip(ins, kinds)]
    out_plans = [pieces(x, kind) for x, kind in zip(outs, out_kinds)]
    buffers = [
        pltpu.VMEM((rows.size, cols.size), members(x, kind)[0].dtype)
        for x, kind, plan in zip(tuple(ins) + tuple(outs), tuple(kinds) + tuple(out_kinds), plans + out_plans)
        for _, rows, cols in plan
    ]

    def kernel(*refs):
        refs = list(refs)

        def take(number):
            found = refs[:number]
            del refs[:number]
            return found

        given = [take(len(members(x, kind))) for x, kind in zip(ins, kinds)]
        made = [take(len(members(x, kind))) for x, kind in zip(outs, out_kinds)]
        held, sent = [take(len(plan)) for plan in plans], [take(len(plan)) for plan in out_plans]
        arrived, left = take(2)
        own = refs

        reads, at = [[] for _ in range(steps)], 0
        for source, buffer, plan in zip(given, held, plans):
            for i, (which, rows, cols) in enumerate(plan):
                reads[i].append(pltpu.make_async_copy(source[which].at[rows, cols], buffer[i], arrived.at[at]))
                at += 1
        writes, at = [], 0
        for target, buffer, plan in zip(made, sent, out_plans):
            writes.append([])
            for i, (which, rows, cols) in enumerate(plan):
                writes[-1].append(pltpu.make_async_copy(buffer[i], target[which].at[rows, cols], left.at[at]))
                at += 1
        for step in reads:
            for copy in step:
                copy.start()
        for i in range(steps):
            for copy in reads[i]:
                copy.wait()
            body(
                lambda fn: fn() if i == 0 else None,
                lambda fn: fn() if i == steps - 1 else None,
                *[buffer[min(i, len(buffer) - 1)] if buffer else source[0] for buffer, source in zip(held, given)],
                *[buffer[min(i, len(buffer) - 1)] for buffer in sent],
                *own,
            )
            for copies in writes:
                if len(copies) == steps:
                    copies[i].start()
                elif i == steps - 1:
                    copies[0].start()
        for copies in writes:
            for copy in copies:
                copy.wait()

    args = [y for x, kind in zip(ins, kinds) for y in members(x, kind)]
    results = [y for x, kind in zip(outs, out_kinds) for y in members(x, kind)]
    spaces = [pltpu.SMEM if kind == "scalar" else pl.ANY for x, kind in zip(ins, kinds) for _ in members(x, kind)]
    nbytes = sum(x.size * x.dtype.itemsize for x in args + results)
    return pl.pallas_call(
        kernel,
        in_specs=[pl.BlockSpec(memory_space=space) for space in spaces],
        out_specs=[pl.BlockSpec(memory_space=pl.ANY)] * len(results),
        out_shape=results,
        scratch_shapes=buffers
        + [
            pltpu.SemaphoreType.DMA((sum(len(plan) for plan in plans),)),
            pltpu.SemaphoreType.DMA((sum(len(plan) for plan in out_plans),)),
        ]
        + list(scratch),
        compiler_params=pltpu.CompilerParams(vmem_limit_bytes=VMEM),
        cost_estimate=pl.CostEstimate(flops=flops, bytes_accessed=nbytes, transcendentals=0),
    )(*args)


def shape(dims, dtype):
    return jax.ShapeDtypeStruct(dims, dtype)


def clear(*refs):
    for ref in refs:
        ref[...] = jnp.zeros(ref.shape, ref.dtype)


def weights_phase(w_query, w_key, w_value, w_out, chips, heads):
    qk, cols, half = heads * DK, heads * DV, w_out.shape[1] // 2

    def body(q_ref, k_ref, v_ref, o_ref, out_ref):
        query, key, value, rest = (ref[...].astype(F32) for ref in (q_ref, k_ref, v_ref, o_ref))
        halves = [
            jnp.concatenate(
                [
                    query[:, c * qk : (c + 1) * qk],
                    key[:, c * qk : (c + 1) * qk],
                    value[:, c * cols : (c + 1) * cols],
                    rest[:, c * half : (c + 1) * half],
                ],
                axis=1,
            )
            for c in range(2)
        ]
        pair = jnp.concatenate(halves, axis=0).astype(BF)
        for p in range(chips):
            out_ref[p * pair.shape[0] : (p + 1) * pair.shape[0], :] = pair

    rows = w_query.shape[0]
    return pl.pallas_call(
        body,
        out_shape=shape((2 * chips * rows, 2 * qk + cols + half), BF),
        compiler_params=pltpu.CompilerParams(vmem_limit_bytes=VMEM),
        cost_estimate=pl.CostEstimate(flops=0, bytes_accessed=2 * 2 * chips * rows * (2 * qk + cols + half), transcendentals=0),
    )(w_query, w_key, w_value, w_out)


def keys_phase(tokens, w_qkv, chips, heads):
    qk = heads * DK

    def body(at_first, at_last, slab_ref, w_ref, qk_ref, value_ref, feat_ref, sent_ref, state_acc, norm_acc):
        at_first(lambda: clear(state_acc, norm_acc))
        joined = dot(slab_ref[...], w_ref[...], (1, 0))
        qk_t = joined[:, : 2 * qk].T.astype(BF)
        value = joined[:, 2 * qk :].astype(BF)
        qk_ref[...] = qk_t
        value_ref[...] = value
        keys = qk_t.astype(F32)[qk:]
        found = []
        for head in range(heads):
            feat = features(rows_of(keys, head, DK))
            found.append(feat)
            state_acc[head, :FPAD, :] += dot(feat, value[:, head * DV : (head + 1) * DV], (1, 0))
            norm_acc[head, :FPAD, :] += lane_sums(feat.astype(F32))
        feat_ref[...] = jnp.concatenate(found, axis=0)

        @at_last
        def _():
            norm = split_rows([jnp.sum(norm_acc[head], axis=1)[None] for head in range(heads)])
            state = state_acc[...].reshape(heads * SPAD, DV).astype(BF)
            part = heads * SPAD // chips
            for p in range(chips):
                sent_ref[2 * part * p : 2 * part * p + part, :] = state[part * p : part * (p + 1)]
                sent_ref[2 * part * p + part : 2 * part * (p + 1), :] = norm

    count = 2 * tokens[0].shape[0]
    return call(
        body,
        count,
        (tokens, w_qkv),
        ("pair", (2 * qk + heads * DV, 0)),
        (
            shape((2 * qk, count), BF),
            shape((count, heads * DV), BF),
            (shape((heads * FPAD, count // 2), BF),) * 2,
            shape((2 * heads * SPAD, DV), BF),
        ),
        (1, 0, "pair1", None),
        [pltpu.VMEM((heads, SPAD, DV), F32), pltpu.VMEM((heads, SPAD, 128), F32)],
        2 * count * heads * (w_qkv.shape[0] * (2 * DK + DV) + FPAD * DV * 2),
    )


def upstream_phase(core, qk_t, cot, weights, other_weights, heads):
    count, width = qk_t.shape[1], cot[0].shape[1]
    rows, half = heads * DV, width // 2
    joined = 2 * heads * DK + heads * DV

    def body(at_first, at_last, core_ref, qk_ref, slab_ref, mine_ref, theirs_ref, up_ref, feat_ref, w_ref):
        at = core_ref[0, 0]

        @at_first
        def _():
            mine, theirs = mine_ref[...], theirs_ref[...]
            w_ref[:, :half] = jnp.where(at == 0, mine, theirs)
            w_ref[:, half:] = jnp.where(at == 0, theirs, mine)

        here = w_ref[pl.ds(pl.multiple_of(at * rows, rows), rows), :]
        up_ref[...] = dot(here, slab_ref[...], (1, 1))
        query = qk_ref[...].astype(F32)
        for head in range(heads):
            feat_ref[head * FPAD : (head + 1) * FPAD, :] = features(rows_of(query, head, DK))

    return call(
        body,
        count,
        (core, qk_t, cot, weights, other_weights),
        ("scalar", 1, "pair", ("from", joined), ("from", joined)),
        (shape((rows, count), F32), shape((heads * FPAD, count), BF), shape((2 * rows, width), BF)),
        (1, 1, None),
        [],
        2 * count * rows * width,
    )


def product_phase(rows_t, slabs, after, parts):
    rows, count = rows_t[0].shape[0], 2 * rows_t[0].shape[1]
    size = rows // parts
    width = slabs[0].shape[1]

    def body(at_first, at_last, rows_ref, slab_ref, after_ref, out_ref, acc):
        at_first(lambda: clear(acc))
        acc[...] += dot(rows_ref[...], slab_ref[...], (1, 0))

        @at_last
        def _():
            for part in range(parts):
                out_ref[part * width : (part + 1) * width, :] = acc[part * size : (part + 1) * size, :].T.astype(BF)

    return call(
        body,
        count,
        (rows_t, slabs, after),
        ("pair1", "pair", "any"),
        (shape((parts * width, size), BF),),
        (None,),
        [pltpu.VMEM((rows, width), F32)],
        2 * count * rows * width,
    )[0]


def query_phase(feats, up_t, first, chips, heads):
    count = up_t.shape[1]
    part = heads * SPAD // chips

    def body(at_first, at_last, feat_ref, up_ref, first_ref, scale_ref, norm_ref, sent_ref, acc, state_own):
        at_first(lambda: clear(acc))

        @at_first
        def _():
            total = add_chips(first_ref, 2 * part)
            state_own[...] = total[:part].astype(BF)
            norm_ref[...] = total[part:]

        at = lax.broadcasted_iota(jnp.int32, scale_ref.shape, 0)
        scales = jnp.zeros(scale_ref.shape, F32)
        for head in range(heads):
            feat = feat_ref[head * FPAD : (head + 1) * FPAD, :]
            parts = in_parts(head_row(norm_ref[...], head) * band_weight((1, SPAD), 1))[:, :FPAD]
            scale = 1.0 / jnp.sum(dot(parts, feat, (1, 0)), axis=0, keepdims=True)
            grad_num = (up_ref[head * DV : (head + 1) * DV, :] * scale).astype(BF)
            acc[head, :FPAD, :] += dot(feat, grad_num, (1, 1))
            scales = jnp.where(at == head, scale, scales)
        scale_ref[...] = scales

        @at_last
        def _():
            sent_ref[:, :DV] = acc[...].reshape(heads * SPAD, DV).astype(BF)
            for p in range(chips):
                sent_ref[p * part : (p + 1) * part, DV:] = state_own[...]

    return call(
        body,
        count,
        (feats, up_t, first),
        (1, 1, None),
        (shape((8, count), F32), shape((16, 128), F32), shape((heads * SPAD, 2 * DV), BF)),
        (1, None, None),
        [pltpu.VMEM((heads, SPAD, DV), F32), pltpu.VMEM((part, DV), BF)],
        2 * count * heads * FPAD * DV * 2,
    )


def attend_phase(feats, scales, up_t, second, cot, moments, chips, heads):
    count = up_t.shape[1]
    width = cot[0].shape[1]
    quarter = width // 4

    def body(
        at_first, at_last, feat_ref, scale_ref, up_ref, state_ref, sgrad_ref, slab_ref, moment_ref,
        att_ref, den_ref, out_ref, sent_ref, turned, acc, out_acc,
    ):
        at_first(lambda: clear(acc, out_acc))

        @at_first
        def _():
            for head in range(heads):
                turned[head] = weighted_turned(state_ref, head)

        at = lax.broadcasted_iota(jnp.int32, den_ref.shape, 0)
        dens = jnp.zeros(den_ref.shape, F32)
        found = []
        for head in range(heads):
            feat = feat_ref[head * FPAD : (head + 1) * FPAD, :]
            scale = scale_ref[head : head + 1, :]
            att = dot(turned[head, :, :FPAD], feat, (1, 0)) * scale
            grad_num = up_ref[head * DV : (head + 1) * DV, :] * scale
            grad_den = -jnp.sum(grad_num * att, axis=0, keepdims=True)
            acc[head, :FPAD, :] += lane_sums(feat.astype(F32) * grad_den)
            found.append(att.astype(BF))
            dens = jnp.where(at == head, grad_den, dens)
        den_ref[...] = dens
        attended = jnp.concatenate(found, axis=0)
        att_ref[...] = attended
        out_acc[...] += dot(attended, slab_ref[...], (1, 0))

        @at_last
        def _():
            ngrad = split_rows([jnp.sum(acc[head], axis=1)[None] for head in range(heads)])
            sgrad_own = add_chips(sgrad_ref, ngrad.shape[0]).astype(BF)
            both = jnp.concatenate([sgrad_own, ngrad], axis=1)
            for p in range(chips):
                sent_ref[p * both.shape[0] : (p + 1) * both.shape[0], :] = both
            for k in range(4):
                rows = slice(k * heads * DV, (k + 1) * heads * DV)
                out_ref[rows, :quarter] = out_acc[:, k * quarter : (k + 1) * quarter].astype(BF)
                for j in range(2):
                    part = moment_ref[(2 * k + j) * heads * DV : (2 * k + j + 1) * heads * DV, :]
                    out_ref[rows, quarter + j * FPAD : quarter + (j + 1) * FPAD] = part

    return call(
        body,
        count,
        (feats, scales, up_t, second, second, cot, moments),
        (1, 1, 1, (DV, 1), (DV, 0), "pair", None),
        (
            (shape((heads * DV, count // 2), BF),) * 2,
            shape((8, count), F32),
            shape((4 * heads * DV, quarter + 2 * FPAD), BF),
            shape(second.shape, BF),
        ),
        ("pair1", 1, None, None),
        [
            pltpu.VMEM((heads, DV, SPAD), BF),
            pltpu.VMEM((heads, SPAD, 128), F32),
            pltpu.VMEM((heads * DV, width), F32),
        ],
        2 * count * (heads * FPAD * DV * 2 + heads * DV * width),
    )


def query_back_phase(qk_t, scales, dens, up_t, second, norm, heads):
    count = up_t.shape[1]

    def body(at_first, at_last, qk_ref, scale_ref, den_ref, up_ref, state_ref, norm_ref, qgrad_ref):
        query = qk_ref[...].astype(F32)
        found = []
        for head in range(heads):
            grad_num = (up_ref[head * DV : (head + 1) * DV, :] * scale_ref[head : head + 1, :]).astype(BF)
            fgrad = dot(state_ref[head * SPAD : head * SPAD + FPAD, :], grad_num, (1, 0))
            fgrad = fgrad + column(head_row(norm_ref[...], head)) * den_ref[head : head + 1, :]
            found.append(features_back(rows_of(query, head, DK), fgrad).astype(BF))
        qgrad_ref[...] = jnp.concatenate(found, axis=0)

    return call(
        body,
        count,
        (qk_t, scales, dens, up_t, second, norm),
        (1, 1, 1, 1, (DV, 1), None),
        ((shape((heads * DK, count // 2), BF),) * 2,),
        ("pair1",),
        [],
        2 * count * heads * FPAD * DV,
    )


def key_phase(qk_t, value, third, qgrads, tokens, after, heads):
    count, qk = value.shape[0], heads * DK
    width = tokens[0].shape[1]

    def body(
        at_first, at_last, qk_ref, value_ref, sgrad_ref, rows_ref, qgrad_ref, slab_ref, after_ref,
        kgrad_ref, copy_ref, sent_ref, acc, ngrad_ref,
    ):
        at_first(lambda: clear(acc))

        @at_first
        def _():
            ngrad_ref[...] = add_chips(rows_ref, 16)
            copy_ref[...] = sgrad_ref[...]

        keys = qk_ref[...].astype(F32)[qk:]
        found = []
        for head in range(heads):
            fgrad = dot(
                sgrad_ref[head * SPAD : head * SPAD + FPAD, :],
                value_ref[:, head * DV : (head + 1) * DV],
                (1, 1),
            )
            fgrad = fgrad + column(head_row(ngrad_ref[...], head))
            found.append(features_back(rows_of(keys, head, DK), fgrad))
        kgrad = jnp.concatenate(found, axis=0).astype(BF)
        kgrad_ref[...] = kgrad
        both = jnp.concatenate([qgrad_ref[...], kgrad], axis=0)
        acc[...] += dot(both, slab_ref[...], (1, 0))

        @at_last
        def _():
            sent_ref[...] = acc[...].T.astype(BF)

    return call(
        body,
        count,
        (qk_t, value, third, third, qgrads, tokens, after),
        (1, 0, (DV, 0), (DV, 1), "pair1", "pair", "any"),
        (
            (shape((qk, count // 2), BF),) * 2,
            shape((third.shape[0], DV), BF),
            shape((width, 2 * qk), BF),
        ),
        ("pair1", None, None),
        [pltpu.VMEM((2 * qk, width), F32), pltpu.VMEM((16, DV), F32)],
        2 * count * (heads * FPAD * DV + 2 * qk * width),
    )


def last_payload(core, wgrad, along_x):
    rows, cols = wgrad.shape
    half = along_x.shape[0]
    quarter = along_x.shape[1] - 2 * FPAD

    def body(core_ref, wgrad_ref, terms_ref, sent_ref):
        first = core_ref[0, 0] == 0
        sent_ref[:, :cols] = wgrad_ref[...]
        for j in range(2):
            here = slice(j * half, (j + 1) * half)
            sent_ref[here, cols : cols + FPAD] = terms_ref[:, quarter + j * FPAD : quarter + (j + 1) * FPAD]
            out = terms_ref[:, :quarter]
            sent_ref[here, cols + FPAD :] = jnp.where(first == (j == 0), out, jnp.zeros_like(out))

    vmem = pl.BlockSpec(memory_space=pltpu.VMEM)
    return pl.pallas_call(
        body,
        in_specs=[pl.BlockSpec(memory_space=pltpu.SMEM)] + [vmem] * 2,
        out_specs=vmem,
        out_shape=shape((rows, cols + FPAD + quarter), BF),
        compiler_params=pltpu.CompilerParams(vmem_limit_bytes=VMEM),
        cost_estimate=pl.CostEstimate(flops=0, bytes_accessed=4 * rows * cols, transcendentals=0),
    )(core, wgrad, along_x)


def outputs_phase(core, attended, qgrads, kgrads, feats, sgrads, weights, w_out, heads):
    count, width = attended[0].shape[1], w_out.shape[1]
    rows, joined = heads * DV, 2 * heads * DK + heads * DV

    def body(at_first, at_last, core_ref, *refs):
        atts, qs, ks, fs, ss, ws = (refs[2 * i : 2 * i + 2] for i in range(6))
        out_ref, mixed_ref, gtok_ref, turned = refs[12:]
        at = core_ref[0, 0]

        @at_first
        def _():
            for c in range(2):
                for head in range(heads):
                    turned[c, head] = weighted_turned(ss[c], head)

        mixed, gtok = 0.0, 0.0
        for c in range(2):
            first = pl.multiple_of((at if c == 0 else 1 - at) * rows, rows)
            mixed = mixed + dot(atts[c][...], out_ref[pl.ds(first, rows), :], (0, 0))
            parts = [qs[c][...], ks[c][...]]
            for head in range(heads):
                feat = fs[c][head * FPAD : (head + 1) * FPAD, :]
                parts.append(dot(turned[c, head, :, :FPAD], feat, (1, 0)).astype(BF))
            gtok = gtok + dot(jnp.concatenate(parts, axis=0), ws[c][...], (0, 1))
        mixed_ref[...] = mixed.astype(BF)
        gtok_ref[...] = gtok.astype(BF)

    return call(
        body,
        count,
        (core, *attended, *qgrads, *kgrads, *feats, *sgrads, *weights, w_out),
        ("scalar",) + (1,) * 8 + (None,) * 2 + ((joined, 0),) * 2 + (None,),
        (shape((count, width), BF), shape((count, width), BF)),
        (0, 0),
        [pltpu.VMEM((2, heads, DV, SPAD), BF)],
        2 * count * 2 * (joined * width + rows * width + heads * FPAD * DV),
    )


def finish_phase(core, fourth, sgrads, after, heads, scale_factor):
    rows, qk, n = 8, heads * DK, fourth.shape[0] // 8
    quarter = fourth.shape[1] - 2 * qk - FPAD

    def body(core_ref, recv_ref, mine_ref, other_ref, *refs):
        query_ref, key_ref, value_ref, out_ref = refs[-4:]
        first = core_ref[0, 0] == 0
        wgrad = jnp.zeros((2 * rows, 2 * qk), F32)
        moment = [jnp.zeros((2 * rows, FPAD), F32) for _ in range(heads)]
        out = [jnp.zeros((2 * rows, quarter), F32) for _ in range(4)]
        for p in range(n // 2):
            both = recv_ref[2 * rows * p : 2 * rows * (p + 1), :].astype(F32)
            x = 2 * ((p // 8) % 2) + p % 2
            wgrad = wgrad + both[:, : 2 * qk]
            moment[x] = moment[x] + both[:, 2 * qk : 2 * qk + FPAD]
            out[x] = out[x] + both[:, 2 * qk + FPAD :]
        for x in range(4):
            out_ref[:, x * quarter : (x + 1) * quarter] = (out[x][:rows] + out[x][rows:]) * scale_factor
        wgrad = wgrad * scale_factor
        query_ref[...] = jnp.concatenate([wgrad[:rows, :qk], wgrad[rows:, :qk]], axis=1)
        key_ref[...] = jnp.concatenate([wgrad[:rows, qk:], wgrad[rows:, qk:]], axis=1)
        weight = band_weight((1, FPAD), 1) * scale_factor
        found = [[], []]
        for head in range(heads):
            whole = moment[head] * weight
            high = whole.astype(BF)
            parts = jnp.concatenate([high, (whole - high.astype(F32)).astype(BF)], axis=0)
            for which, ref in enumerate((mine_ref, other_ref)):
                both = dot(parts, ref[head * SPAD : head * SPAD + FPAD, :], (1, 0))
                both = both[: 2 * rows] + both[2 * rows :]
                low, up = both[:rows], both[rows:]
                found[which].append(jnp.where(first, low, up) if which == 0 else jnp.where(first, up, low))
        mine, other = (jnp.concatenate(part, axis=1) for part in found)
        value_ref[:, : heads * DV] = jnp.where(first, mine, other)
        value_ref[:, heads * DV :] = jnp.where(first, other, mine)

    vmem = pl.BlockSpec(memory_space=pltpu.VMEM)
    return pl.pallas_call(
        body,
        in_specs=[pl.BlockSpec(memory_space=pltpu.SMEM)] + [vmem] * 3 + [pl.BlockSpec(memory_space=pl.ANY)] * len(after),
        out_specs=[vmem] * 4,
        out_shape=(
            shape((rows, 2 * qk), F32),
            shape((rows, 2 * qk), F32),
            shape((rows, 2 * heads * DV), F32),
            shape((rows, 4 * quarter), F32),
        ),
        compiler_params=pltpu.CompilerParams(vmem_limit_bytes=VMEM),
        cost_estimate=pl.CostEstimate(flops=0, bytes_accessed=fourth.size * 2, transcendentals=0),
    )(core, fourth, *sgrads, *after)


def per_device(chips, tokens, w_query, w_key, w_value, w_out, cotangent):
    n = 2 * chips
    heads = H // 2
    own, width = tokens.shape
    qk = heads * DK
    core = lax.axis_index("seq") % 2
    core_at = core.astype(jnp.int32).reshape(1, 1)
    same_core = [[2 * p + c for p in range(chips)] for c in range(2)]
    swap = [(i, i ^ 1) for i in range(n)]
    scale_factor = (own * n) ** (-0.5)

    def exchange(x):
        return lax.ppermute(x, AXES, swap)

    def spread(x):
        return lax.all_to_all(x, AXES, 0, 0, axis_index_groups=same_core, tiled=True)

    def add_along_x(x):
        quarters = x.reshape((4, -1) + x.shape[1:])
        total = lax.dynamic_index_in_dim(quarters, me_x, 0, keepdims=False).astype(F32)
        for step in (1, 2, 3):
            moves = []
            for i in range(n):
                y, at, z, c = place(i)
                moves.append((i, device(y, (at + step) % 4, z, c)))
            there = lax.dynamic_index_in_dim(quarters, (me_x + step) % 4, 0, keepdims=False)
            total = total + lax.ppermute(there, AXES, moves).astype(F32)
        return total.astype(BF)

    def place(i):
        return (i // 32, 2 * (i // 16 % 2) + i // 2 % 2, i // 4 % 4, i % 2)

    def device(y, x, z, c):
        return (((y * 2 + x // 2) * 4 + z) * 2 + x % 2) * 2 + c

    def to_each(x):
        return x.reshape(chips, -1, x.shape[1])

    ctx, seq = lax.axis_index("ctx"), lax.axis_index("seq")
    me_x = 2 * (ctx // 4 % 2) + seq // 2
    along_x = [[device(y, x, z, c) for x in range(4)] for y in range(4) for z in range(4) for c in range(2)]

    to_send = weights_phase(w_query, w_key, w_value, w_out, chips, heads)
    weights = lax.all_to_all(to_send.reshape(n, -1, to_send.shape[1]), AXES, 0, 0, tiled=True)
    weights = weights.reshape(-1, to_send.shape[1])
    tok = (tokens, exchange(tokens))
    cot = (cotangent, exchange(cotangent))
    other_weights = exchange(weights)

    qk_t, value, key_feat, key_feat_sent, sent = keys_phase(tok, weights, chips, heads)
    first = spread(to_each(sent)).reshape(sent.shape)
    key_feats = (key_feat, exchange(key_feat_sent))

    up_t, query_feat, w_out_whole = upstream_phase(core_at, qk_t, cot, weights, other_weights, heads)
    scales, norm, sent = query_phase(query_feat, up_t, first, chips, heads)
    second = spread(to_each(sent)).reshape(sent.shape)
    moments = product_phase((key_feat, key_feat_sent), tok, sent, heads)

    attended, attended_sent, dens, terms, sent = attend_phase(
        query_feat, scales, up_t, second, cot, moments, chips, heads
    )
    third = spread(to_each(sent)).reshape(sent.shape)
    terms = add_along_x(terms)
    attendeds = (attended, exchange(attended_sent))
    qgrad, qgrad_sent = query_back_phase(qk_t, scales, dens, up_t, second, norm, heads)
    qgrads = (qgrad, exchange(qgrad_sent))

    kgrad, kgrad_sent, sgrad, wgrad = key_phase(qk_t, value, third, (qgrad, qgrad_sent), tok, terms, heads)
    sent = last_payload(core_at, wgrad, terms)
    fourth = lax.all_to_all(sent.reshape(n, -1, sent.shape[1]), AXES, 0, 0, tiled=True).reshape(sent.shape)
    kgrads, sgrads = (kgrad, exchange(kgrad_sent)), (sgrad, exchange(sgrad))
    mixed, grad_tokens = outputs_phase(
        core_at, attendeds, qgrads, kgrads, key_feats, sgrads, (weights, other_weights), w_out_whole, heads
    )
    grad_query, grad_key, grad_value, grad_out = finish_phase(
        core_at, fourth, sgrads, (grad_tokens, mixed), heads, scale_factor
    )
    return (mixed, grad_tokens, grad_query, grad_key, grad_value, grad_out)


def solution(mesh):
    chips = mesh.size // 2
    placed = P(AXES, None)
    return jax.shard_map(
        lambda *args: per_device(chips, *args),
        mesh=mesh,
        in_specs=(placed,) * 6,
        out_specs=(placed,) * 6,
        check_vma=False,
    )
```

```python
import jax
import jax.numpy as jnp
from jax import lax
from jax.experimental import pallas as pl
from jax.experimental.pallas import tpu as pltpu
from jax.sharding import PartitionSpec as P

H = 8
DK = 16
DV = 128
BANDS = DK // 2 + 1
FPAD = (BANDS + 2) * DK
SPAD = 256
AXES = ("ctx", "seq")
BLOCK = 512
VMEM = 60 * 2**20
BF = jnp.bfloat16
F32 = jnp.float32
SQUARE = (2.0 * DK) ** (-0.5)
LINEAR = DK ** (-0.25)


def dot(a, b, contract):
    return lax.dot_general(a, b, ((contract[:1], contract[1:]), ((), ())), preferred_element_type=F32)


def band_weight(shape, dim):
    row = lax.broadcasted_iota(jnp.int32, shape, dim)
    twice = (row >= DK) & (row < (BANDS - 1) * DK)
    return jnp.where(twice, 2.0, 1.0).astype(F32)


def shifted(u, d):
    return pltpu.roll(u, DK - d, 0) if d else u


def features(u):
    bands = [u * shifted(u, d) * SQUARE for d in range(BANDS)]
    first = lax.broadcasted_iota(jnp.int32, u.shape, 0) == 0
    return jnp.concatenate(bands + [u * LINEAR, jnp.where(first, 1.0, 0.0)], axis=0).astype(BF)


def features_back(u, fgrad):
    def band(d):
        return fgrad[d * DK : (d + 1) * DK]

    total = band(0) * u + band(BANDS - 1) * shifted(u, BANDS - 1)
    for d in range(1, BANDS - 1):
        total = total + band(d) * shifted(u, d) + shifted(band(d) * u, DK - d)
    return total * (2.0 * SQUARE) + band(BANDS) * LINEAR


def in_parts(row):
    high = row.astype(BF).astype(F32)
    rest = row - high
    mid = rest.astype(BF).astype(F32)
    at = lax.broadcasted_iota(jnp.int32, (16, row.shape[1]), 0)
    low = jnp.where(at == 2, rest - mid, 0.0)
    return jnp.where(at == 0, high, jnp.where(at == 1, mid, low)).astype(BF)


def rows_of(array, head, size):
    return array[head * size : (head + 1) * size]


def head_row(rows, head):
    first, second = rows[4 * head : 4 * head + 2, :], rows[4 * head + 2 : 4 * head + 4, :]
    both = first + second
    return jnp.concatenate([both[:1], both[1:]], axis=1)


def split_rows(per_head):
    found = []
    for row in per_head:
        high = row.astype(BF).astype(F32)
        for part in (high, row - high):
            found += [part[:, :128], part[:, 128:]]
    found += [jnp.zeros((1, 128), F32)] * (16 - len(found))
    return jnp.concatenate(found, axis=0).astype(BF)


def column(row):
    return jnp.broadcast_to(row, (8, row.shape[1])).T[:FPAD, :1]


def add_chips(ref, rows):
    total = ref[:rows, :].astype(F32)
    for at in range(rows, ref.shape[0], rows):
        total = total + ref[at : at + rows, :].astype(F32)
    return total


def lane_sums(x):
    return sum(x[:, i : i + 128] for i in range(0, x.shape[1], 128))


def weighted_turned(state_ref, head):
    whole = state_ref[head * SPAD : (head + 1) * SPAD, :].astype(F32)
    return (whole * band_weight((SPAD, DV), 0)).T.astype(BF)


def call(body, count, ins, kinds, outs, out_kinds, scratch, flops, size=BLOCK):
    block = min(size, count // 2 if "pair" in kinds or "pair1" in out_kinds else count)
    steps = count // block

    def pieces(x, kind):
        if kind in ("pair", "pair1"):
            half = steps // 2
            return pieces_of(0, half, x[0].shape, kind) + pieces_of(1, half, x[1].shape, kind)
        if kind in (0, 1):
            return pieces_of(0, steps, x.shape, kind)
        if kind is not None and kind[0] == "from":
            return [(0, pl.ds(0, x.shape[0]), pl.ds(kind[1], x.shape[1] - kind[1]))]
        if kind is not None:
            return [(0, pl.ds(0, x.shape[0]), pl.ds(kind[0] * kind[1], kind[0]))]
        return [(0, pl.ds(0, x.shape[0]), pl.ds(0, x.shape[1]))]

    def pieces_of(which, number, dims, kind):
        if kind in (0, "pair"):
            return [(which, pl.ds(i * block, block), pl.ds(0, dims[1])) for i in range(number)]
        return [(which, pl.ds(0, dims[0]), pl.ds(i * block, block)) for i in range(number)]

    def members(x, kind):
        return list(x) if kind in ("pair", "pair1") else [x]

    plans = [[] if kind in ("scalar", "any") else pieces(x, kind) for x, kind in zip(ins, kinds)]
    out_plans = [pieces(x, kind) for x, kind in zip(outs, out_kinds)]
    buffers = [
        pltpu.VMEM((rows.size, cols.size), members(x, kind)[0].dtype)
        for x, kind, plan in zip(tuple(ins) + tuple(outs), tuple(kinds) + tuple(out_kinds), plans + out_plans)
        for _, rows, cols in plan
    ]

    def kernel(*refs):
        refs = list(refs)

        def take(number):
            found = refs[:number]
            del refs[:number]
            return found

        given = [take(len(members(x, kind))) for x, kind in zip(ins, kinds)]
        made = [take(len(members(x, kind))) for x, kind in zip(outs, out_kinds)]
        held, sent = [take(len(plan)) for plan in plans], [take(len(plan)) for plan in out_plans]
        arrived, left = take(2)
        own = refs

        reads, at = [[] for _ in range(steps)], 0
        for source, buffer, plan in zip(given, held, plans):
            for i, (which, rows, cols) in enumerate(plan):
                reads[i].append(pltpu.make_async_copy(source[which].at[rows, cols], buffer[i], arrived.at[at]))
                at += 1
        writes, at = [], 0
        for target, buffer, plan in zip(made, sent, out_plans):
            writes.append([])
            for i, (which, rows, cols) in enumerate(plan):
                writes[-1].append(pltpu.make_async_copy(buffer[i], target[which].at[rows, cols], left.at[at]))
                at += 1
        for step in reads:
            for copy in step:
                copy.start()
        for i in range(steps):
            for copy in reads[i]:
                copy.wait()
            body(
                lambda fn: fn() if i == 0 else None,
                lambda fn: fn() if i == steps - 1 else None,
                *[buffer[min(i, len(buffer) - 1)] if buffer else source[0] for buffer, source in zip(held, given)],
                *[buffer[min(i, len(buffer) - 1)] for buffer in sent],
                *own,
            )
            for copies in writes:
                if len(copies) == steps:
                    copies[i].start()
                elif i == steps - 1:
                    copies[0].start()
        for copies in writes:
            for copy in copies:
                copy.wait()

    args = [y for x, kind in zip(ins, kinds) for y in members(x, kind)]
    results = [y for x, kind in zip(outs, out_kinds) for y in members(x, kind)]
    spaces = [pltpu.SMEM if kind == "scalar" else pl.ANY for x, kind in zip(ins, kinds) for _ in members(x, kind)]
    nbytes = sum(x.size * x.dtype.itemsize for x in args + results)
    return pl.pallas_call(
        kernel,
        in_specs=[pl.BlockSpec(memory_space=space) for space in spaces],
        out_specs=[pl.BlockSpec(memory_space=pl.ANY)] * len(results),
        out_shape=results,
        scratch_shapes=buffers
        + [
            pltpu.SemaphoreType.DMA((sum(len(plan) for plan in plans),)),
            pltpu.SemaphoreType.DMA((sum(len(plan) for plan in out_plans),)),
        ]
        + list(scratch),
        compiler_params=pltpu.CompilerParams(vmem_limit_bytes=VMEM),
        cost_estimate=pl.CostEstimate(flops=flops, bytes_accessed=nbytes, transcendentals=0),
    )(*args)


def shape(dims, dtype):
    return jax.ShapeDtypeStruct(dims, dtype)


def clear(*refs):
    for ref in refs:
        ref[...] = jnp.zeros(ref.shape, ref.dtype)


def weights_phase(w_query, w_key, w_value, w_out, chips, heads):
    qk, cols, half = heads * DK, heads * DV, w_out.shape[1] // 2

    def body(q_ref, k_ref, v_ref, o_ref, out_ref, pair_ref, sems):
        query, key, value, rest = (ref[...].astype(F32) for ref in (q_ref, k_ref, v_ref, o_ref))
        halves = [
            jnp.concatenate(
                [
                    query[:, c * qk : (c + 1) * qk],
                    key[:, c * qk : (c + 1) * qk],
                    value[:, c * cols : (c + 1) * cols],
                    rest[:, c * half : (c + 1) * half],
                ],
                axis=1,
            )
            for c in range(2)
        ]
        pair_ref[...] = jnp.concatenate(halves, axis=0).astype(BF)
        copies = [
            pltpu.make_async_copy(pair_ref, out_ref.at[pl.ds(2 * rows * p, 2 * rows), :], sems.at[p]) for p in range(chips)
        ]
        for copy in copies:
            copy.start()
        for copy in copies:
            copy.wait()

    rows = w_query.shape[0]
    return pl.pallas_call(
        body,
        out_specs=pl.BlockSpec(memory_space=pl.ANY),
        out_shape=shape((2 * chips * rows, 2 * qk + cols + half), BF),
        scratch_shapes=[pltpu.VMEM((2 * rows, 2 * qk + cols + half), BF), pltpu.SemaphoreType.DMA((chips,))],
        compiler_params=pltpu.CompilerParams(vmem_limit_bytes=VMEM),
        cost_estimate=pl.CostEstimate(flops=0, bytes_accessed=2 * 2 * chips * rows * (2 * qk + cols + half), transcendentals=0),
    )(w_query, w_key, w_value, w_out)


def keys_phase(tokens, w_qkv, chips, heads):
    qk = heads * DK

    def body(at_first, at_last, slab_ref, w_ref, qk_ref, value_ref, feat_ref, sent_ref, state_acc, norm_acc):
        at_first(lambda: clear(state_acc, norm_acc))
        joined = dot(slab_ref[...], w_ref[...], (1, 0))
        qk_t = joined[:, : 2 * qk].T.astype(BF)
        value = joined[:, 2 * qk :].astype(BF)
        qk_ref[...] = qk_t
        value_ref[...] = value
        keys = qk_t.astype(F32)[qk:]
        found = []
        for head in range(heads):
            feat = features(rows_of(keys, head, DK))
            found.append(feat)
            state_acc[head, :FPAD, :] += dot(feat, value[:, head * DV : (head + 1) * DV], (1, 0))
            norm_acc[head, :FPAD, :] += lane_sums(feat.astype(F32))
        feat_ref[...] = jnp.concatenate(found, axis=0)

        @at_last
        def _():
            norm = split_rows([jnp.sum(norm_acc[head], axis=1)[None] for head in range(heads)])
            state = state_acc[...].reshape(heads * SPAD, DV).astype(BF)
            part = heads * SPAD // chips
            for p in range(chips):
                sent_ref[2 * part * p : 2 * part * p + part, :] = state[part * p : part * (p + 1)]
                sent_ref[2 * part * p + part : 2 * part * (p + 1), :] = norm

    count = 2 * tokens[0].shape[0]
    return call(
        body,
        count,
        (tokens, w_qkv),
        ("pair", (2 * qk + heads * DV, 0)),
        (
            shape((2 * qk, count), BF),
            shape((count, heads * DV), BF),
            (shape((heads * FPAD, count // 2), BF),) * 2,
            shape((2 * heads * SPAD, DV), BF),
        ),
        (1, 0, "pair1", None),
        [pltpu.VMEM((heads, SPAD, DV), F32), pltpu.VMEM((heads, SPAD, 128), F32)],
        2 * count * heads * (w_qkv.shape[0] * (2 * DK + DV) + FPAD * DV * 2),
    )


def upstream_phase(core, qk_t, cot, weights, other_weights, heads):
    count, width = qk_t.shape[1], cot[0].shape[1]
    rows, half = heads * DV, width // 2
    joined = 2 * heads * DK + heads * DV

    def body(at_first, at_last, core_ref, qk_ref, slab_ref, mine_ref, theirs_ref, up_ref, feat_ref, w_ref):
        at = core_ref[0, 0]

        @at_first
        def _():
            mine, theirs = mine_ref[...], theirs_ref[...]
            w_ref[:, :half] = jnp.where(at == 0, mine, theirs)
            w_ref[:, half:] = jnp.where(at == 0, theirs, mine)

        here = w_ref[pl.ds(pl.multiple_of(at * rows, rows), rows), :]
        up_ref[...] = dot(here, slab_ref[...], (1, 1))
        query = qk_ref[...].astype(F32)
        for head in range(heads):
            feat_ref[head * FPAD : (head + 1) * FPAD, :] = features(rows_of(query, head, DK))

    return call(
        body,
        count,
        (core, qk_t, cot, weights, other_weights),
        ("scalar", 1, "pair", ("from", joined), ("from", joined)),
        (shape((rows, count), F32), shape((heads * FPAD, count), BF), shape((2 * rows, width), BF)),
        (1, 1, None),
        [],
        2 * count * rows * width,
    )


def product_phase(turn, rows_t, slabs, after, parts):
    rows, count = rows_t[0].shape[0], 2 * rows_t[0].shape[1]
    size = rows // parts
    width = slabs[0].shape[1]

    def body(at_first, at_last, turn_ref, rows_ref, slab_ref, after_ref, *refs):
        out_refs, acc = refs[:parts], refs[parts]
        at_first(lambda: clear(acc))
        acc[...] += dot(rows_ref[...], slab_ref[...], (1, 0))

        @at_last
        def _():
            for k in range(parts):
                part = turn_ref[0, 0] ^ k
                out_refs[k][...] = acc[pl.ds(pl.multiple_of(part * size, 16), size), :].T.astype(BF)

    return call(
        body,
        count,
        (turn, rows_t, slabs, after),
        ("scalar", "pair1", "pair", "any"),
        (shape((width, size), BF),) * parts,
        (None,) * parts,
        [pltpu.VMEM((rows, width), F32)],
        2 * count * rows * width,
    )


def query_phase(feats, up_t, first, chips, heads):
    count = up_t.shape[1]
    part = heads * SPAD // chips

    def body(at_first, at_last, feat_ref, up_ref, first_ref, scale_ref, norm_ref, sent_ref, acc, state_own):
        at_first(lambda: clear(acc))

        @at_first
        def _():
            total = add_chips(first_ref, 2 * part)
            state_own[...] = total[:part].astype(BF)
            norm_ref[...] = total[part:]

        at = lax.broadcasted_iota(jnp.int32, scale_ref.shape, 0)
        scales = jnp.zeros(scale_ref.shape, F32)
        for head in range(heads):
            feat = feat_ref[head * FPAD : (head + 1) * FPAD, :]
            parts = in_parts(head_row(norm_ref[...], head) * band_weight((1, SPAD), 1))[:, :FPAD]
            scale = 1.0 / jnp.sum(dot(parts, feat, (1, 0)), axis=0, keepdims=True)
            grad_num = (up_ref[head * DV : (head + 1) * DV, :] * scale).astype(BF)
            acc[head, :FPAD, :] += dot(feat, grad_num, (1, 1))
            scales = jnp.where(at == head, scale, scales)
        scale_ref[...] = scales

        @at_last
        def _():
            sent_ref[:, :DV] = acc[...].reshape(heads * SPAD, DV).astype(BF)
            for p in range(chips):
                sent_ref[p * part : (p + 1) * part, DV:] = state_own[...]

    return call(
        body,
        count,
        (feats, up_t, first),
        (1, 1, None),
        (shape((8, count), F32), shape((16, 128), F32), shape((heads * SPAD, 2 * DV), BF)),
        (1, None, None),
        [pltpu.VMEM((heads, SPAD, DV), F32), pltpu.VMEM((part, DV), BF)],
        2 * count * heads * FPAD * DV * 2,
    )


def attend_phase(turn, feats, scales, up_t, second, cot, chips, heads):
    count = up_t.shape[1]
    width = cot[0].shape[1]
    quarter = width // 4

    def body(
        at_first, at_last, turn_ref, feat_ref, scale_ref, up_ref, state_ref, sgrad_ref, slab_ref,
        att_ref, den_ref, sent_ref, out0, out1, out2, out3, turned, acc, out_acc,
    ):
        at_first(lambda: clear(acc, out_acc))

        @at_first
        def _():
            for head in range(heads):
                turned[head] = weighted_turned(state_ref, head)

        at = lax.broadcasted_iota(jnp.int32, den_ref.shape, 0)
        dens = jnp.zeros(den_ref.shape, F32)
        found = []
        for head in range(heads):
            feat = feat_ref[head * FPAD : (head + 1) * FPAD, :]
            scale = scale_ref[head : head + 1, :]
            att = dot(turned[head, :, :FPAD], feat, (1, 0)) * scale
            grad_num = up_ref[head * DV : (head + 1) * DV, :] * scale
            grad_den = -jnp.sum(grad_num * att, axis=0, keepdims=True)
            acc[head, :FPAD, :] += lane_sums(feat.astype(F32) * grad_den)
            found.append(att.astype(BF))
            dens = jnp.where(at == head, grad_den, dens)
        den_ref[...] = dens
        attended = jnp.concatenate(found, axis=0)
        att_ref[...] = attended
        out_acc[...] += dot(attended, slab_ref[...], (1, 0))

        @at_last
        def _():
            ngrad = split_rows([jnp.sum(acc[head], axis=1)[None] for head in range(heads)])
            sgrad_own = add_chips(sgrad_ref, ngrad.shape[0]).astype(BF)
            both = jnp.concatenate([sgrad_own, ngrad], axis=1)
            for p in range(chips):
                sent_ref[p * both.shape[0] : (p + 1) * both.shape[0], :] = both
            for k, out_ref in enumerate((out0, out1, out2, out3)):
                part = turn_ref[0, 0] ^ k
                out_ref[...] = out_acc[:, pl.ds(pl.multiple_of(part * quarter, 128), quarter)].astype(BF)

    return call(
        body,
        count,
        (turn, feats, scales, up_t, second, second, cot),
        ("scalar", 1, 1, 1, (DV, 1), (DV, 0), "pair"),
        (
            (shape((heads * DV, count // 2), BF),) * 2,
            shape((8, count), F32),
            shape(second.shape, BF),
        )
        + (shape((heads * DV, quarter), BF),) * 4,
        ("pair1", 1) + (None,) * 5,
        [
            pltpu.VMEM((heads, DV, SPAD), BF),
            pltpu.VMEM((heads, SPAD, 128), F32),
            pltpu.VMEM((heads * DV, width), F32),
        ],
        2 * count * (heads * FPAD * DV * 2 + heads * DV * width),
    )


def query_back_phase(qk_t, scales, dens, up_t, second, norm, heads):
    count = up_t.shape[1]

    def body(at_first, at_last, qk_ref, scale_ref, den_ref, up_ref, state_ref, norm_ref, qgrad_ref):
        query = qk_ref[...].astype(F32)
        found = []
        for head in range(heads):
            grad_num = (up_ref[head * DV : (head + 1) * DV, :] * scale_ref[head : head + 1, :]).astype(BF)
            fgrad = dot(state_ref[head * SPAD : head * SPAD + FPAD, :], grad_num, (1, 0))
            fgrad = fgrad + column(head_row(norm_ref[...], head)) * den_ref[head : head + 1, :]
            found.append(features_back(rows_of(query, head, DK), fgrad).astype(BF))
        qgrad_ref[...] = jnp.concatenate(found, axis=0)

    return call(
        body,
        count,
        (qk_t, scales, dens, up_t, second, norm),
        (1, 1, 1, 1, (DV, 1), None),
        ((shape((heads * DK, count // 2), BF),) * 2,),
        ("pair1",),
        [],
        2 * count * heads * FPAD * DV,
    )


def key_phase(qk_t, value, third, qgrads, tokens, terms, heads):
    count, qk = value.shape[0], heads * DK
    width = tokens[0].shape[1]

    def body(
        at_first, at_last, qk_ref, value_ref, sgrad_ref, rows_ref, qgrad_ref, slab_ref, terms_ref,
        kgrad_ref, copy_ref, sent_ref, acc, ngrad_ref,
    ):
        at_first(lambda: clear(acc))

        @at_first
        def _():
            ngrad_ref[...] = add_chips(rows_ref, 16)
            copy_ref[...] = sgrad_ref[...]

        keys = qk_ref[...].astype(F32)[qk:]
        found = []
        for head in range(heads):
            fgrad = dot(
                sgrad_ref[head * SPAD : head * SPAD + FPAD, :],
                value_ref[:, head * DV : (head + 1) * DV],
                (1, 1),
            )
            fgrad = fgrad + column(head_row(ngrad_ref[...], head))
            found.append(features_back(rows_of(keys, head, DK), fgrad))
        kgrad = jnp.concatenate(found, axis=0).astype(BF)
        kgrad_ref[...] = kgrad
        both = jnp.concatenate([qgrad_ref[...], kgrad], axis=0)
        acc[...] += dot(both, slab_ref[...], (1, 0))

        @at_last
        def _():
            sent_ref[:, : 2 * qk] = acc[...].T.astype(BF)
            sent_ref[:, 2 * qk :] = terms_ref[...]

    return call(
        body,
        count,
        (qk_t, value, third, third, qgrads, tokens, terms),
        (1, 0, (DV, 0), (DV, 1), "pair1", "pair", None),
        (
            (shape((qk, count // 2), BF),) * 2,
            shape((third.shape[0], DV), BF),
            shape((width, 2 * qk + terms.shape[1]), BF),
        ),
        ("pair1", None, None),
        [pltpu.VMEM((2 * qk, width), F32), pltpu.VMEM((16, DV), F32)],
        2 * count * (heads * FPAD * DV + 2 * qk * width),
    )


def terms_phase(core, moments, outs):
    rows = moments[0].shape[0]
    half, quarter = outs[0].shape

    def body(at_first, at_last, core_ref, m0, m1, m2, m3, o0, o1, o2, o3, sent_ref):
        first = core_ref[0, 0] == 0
        sent_ref[:, :FPAD] = sum(ref[...].astype(F32) for ref in (m0, m1, m2, m3)).astype(BF)

        def put(here):
            out = sum(ref[...].astype(F32) for ref in (o0, o1, o2, o3))
            sent_ref[:, FPAD:] = jnp.where(here, out, 0.0).astype(BF)

        at_first(lambda: put(first))
        at_last(lambda: put(jnp.logical_not(first)))

    return call(
        body,
        rows,
        (core, *moments, *outs),
        ("scalar",) + (0,) * 4 + (None,) * 4,
        (shape((rows, FPAD + quarter), BF),),
        (0,),
        [],
        0,
        half,
    )[0]


def outputs_phase(core, attended, qgrads, kgrads, feats, sgrads, weights, w_out, heads):
    count, width = attended[0].shape[1], w_out.shape[1]
    rows, joined = heads * DV, 2 * heads * DK + heads * DV

    def body(at_first, at_last, core_ref, *refs):
        atts, qs, ks, fs, ss, ws = (refs[2 * i : 2 * i + 2] for i in range(6))
        out_ref, mixed_ref, gtok_ref, turned = refs[12:]
        at = core_ref[0, 0]

        @at_first
        def _():
            for c in range(2):
                for head in range(heads):
                    turned[c, head] = weighted_turned(ss[c], head)

        mixed, gtok = 0.0, 0.0
        for c in range(2):
            first = pl.multiple_of((at if c == 0 else 1 - at) * rows, rows)
            mixed = mixed + dot(atts[c][...], out_ref[pl.ds(first, rows), :], (0, 0))
            parts = [qs[c][...], ks[c][...]]
            for head in range(heads):
                feat = fs[c][head * FPAD : (head + 1) * FPAD, :]
                parts.append(dot(turned[c, head, :, :FPAD], feat, (1, 0)).astype(BF))
            gtok = gtok + dot(jnp.concatenate(parts, axis=0), ws[c][...], (0, 1))
        mixed_ref[...] = mixed.astype(BF)
        gtok_ref[...] = gtok.astype(BF)

    return call(
        body,
        count,
        (core, *attended, *qgrads, *kgrads, *feats, *sgrads, *weights, w_out),
        ("scalar",) + (1,) * 8 + (None,) * 2 + ((joined, 0),) * 2 + (None,),
        (shape((count, width), BF), shape((count, width), BF)),
        (0, 0),
        [pltpu.VMEM((2, heads, DV, SPAD), BF)],
        2 * count * 2 * (joined * width + rows * width + heads * FPAD * DV),
    )


def finish_phase(core, fourth, sgrads, after, heads, scale_factor):
    rows, qk, n = 8, heads * DK, fourth.shape[0] // 8
    quarter = fourth.shape[1] - 2 * qk - FPAD

    def body(core_ref, recv_ref, mine_ref, other_ref, *refs):
        query_ref, key_ref, value_ref, out_ref = refs[-4:]
        first = core_ref[0, 0] == 0
        wgrad = jnp.zeros((2 * rows, 2 * qk), F32)
        moment = [jnp.zeros((2 * rows, FPAD), F32) for _ in range(heads)]
        out = [jnp.zeros((2 * rows, quarter), F32) for _ in range(4)]
        for p in range(n // 2):
            both = recv_ref[2 * rows * p : 2 * rows * (p + 1), :].astype(F32)
            y = p // 16
            in_yz, in_xy = 2 * (y % 2) + p // 2 % 2, 2 * (p % 2) + 1 - y % 2
            wgrad = wgrad + both[:, : 2 * qk]
            moment[in_yz] = moment[in_yz] + both[:, 2 * qk : 2 * qk + FPAD]
            out[in_xy] = out[in_xy] + both[:, 2 * qk + FPAD :]
        for x in range(4):
            out_ref[:, x * quarter : (x + 1) * quarter] = (out[x][:rows] + out[x][rows:]) * scale_factor
        wgrad = wgrad * scale_factor
        query_ref[...] = jnp.concatenate([wgrad[:rows, :qk], wgrad[rows:, :qk]], axis=1)
        key_ref[...] = jnp.concatenate([wgrad[:rows, qk:], wgrad[rows:, qk:]], axis=1)
        weight = band_weight((1, FPAD), 1) * scale_factor
        found = [[], []]
        for head in range(heads):
            whole = moment[head] * weight
            high = whole.astype(BF)
            parts = jnp.concatenate([high, (whole - high.astype(F32)).astype(BF)], axis=0)
            for which, ref in enumerate((mine_ref, other_ref)):
                both = dot(parts, ref[head * SPAD : head * SPAD + FPAD, :], (1, 0))
                both = both[: 2 * rows] + both[2 * rows :]
                low, up = both[:rows], both[rows:]
                found[which].append(jnp.where(first, low, up) if which == 0 else jnp.where(first, up, low))
        mine, other = (jnp.concatenate(part, axis=1) for part in found)
        value_ref[:, : heads * DV] = jnp.where(first, mine, other)
        value_ref[:, heads * DV :] = jnp.where(first, other, mine)

    vmem = pl.BlockSpec(memory_space=pltpu.VMEM)
    return pl.pallas_call(
        body,
        in_specs=[pl.BlockSpec(memory_space=pltpu.SMEM)] + [vmem] * 3 + [pl.BlockSpec(memory_space=pl.ANY)] * len(after),
        out_specs=[vmem] * 4,
        out_shape=(
            shape((rows, 2 * qk), F32),
            shape((rows, 2 * qk), F32),
            shape((rows, 2 * heads * DV), F32),
            shape((rows, 4 * quarter), F32),
        ),
        compiler_params=pltpu.CompilerParams(vmem_limit_bytes=VMEM),
        cost_estimate=pl.CostEstimate(flops=0, bytes_accessed=fourth.size * 2, transcendentals=0),
    )(core, fourth, *sgrads, *after)


def per_device(chips, tokens, w_query, w_key, w_value, w_out, cotangent):
    n = 2 * chips
    heads = H // 2
    own, width = tokens.shape
    qk = heads * DK
    core = lax.axis_index("seq") % 2
    core_at = core.astype(jnp.int32).reshape(1, 1)
    same_core = [[2 * p + c for p in range(chips)] for c in range(2)]
    swap = [(i, i ^ 1) for i in range(n)]
    scale_factor = (own * n) ** (-0.5)

    def exchange(x):
        return lax.ppermute(x, AXES, swap)

    def spread(x):
        return lax.all_to_all(x, AXES, 0, 0, axis_index_groups=same_core, tiled=True)

    def among_four(flips, parts):
        found = [parts[0]]
        for step in (1, 2, 3):
            moves = []
            for i in range(n):
                at = place(i)
                for bit in (0, 1):
                    at = flips[bit](*at) if step >> bit & 1 else at
                moves.append((i, device(*at)))
            found.append(lax.ppermute(parts[step], AXES, moves))
        return found

    yz = (lambda y, x, z, c: (y, x, z ^ 1, c), lambda y, x, z, c: (y ^ 1, x, z, c))
    xy = (lambda y, x, z, c: ((y + 2 * (y % 2) - 1) % 4, x, z, c), lambda y, x, z, c: (y, x ^ 1, z, c))

    def place(i):
        return (i // 32, 2 * (i // 16 % 2) + i // 2 % 2, i // 4 % 4, i % 2)

    def device(y, x, z, c):
        return (((y * 2 + x // 2) * 4 + z) * 2 + x % 2) * 2 + c

    def to_each(x):
        return x.reshape(chips, -1, x.shape[1])

    ctx, seq = lax.axis_index("ctx"), lax.axis_index("seq")
    in_yz, in_xy = (
        v.astype(jnp.int32).reshape(1, 1)
        for v in (2 * (ctx // 8 % 2) + ctx % 2, 2 * (seq // 2) + 1 - ctx // 8 % 2)
    )

    to_send = weights_phase(w_query, w_key, w_value, w_out, chips, heads)
    weights = lax.all_to_all(to_send.reshape(n, -1, to_send.shape[1]), AXES, 0, 0, tiled=True)
    weights = weights.reshape(-1, to_send.shape[1])
    tok = (tokens, exchange(tokens))
    cot = (cotangent, exchange(cotangent))
    other_weights = exchange(weights)

    qk_t, value, key_feat, key_feat_sent, sent = keys_phase(tok, weights, chips, heads)
    first = spread(to_each(sent)).reshape(sent.shape)
    key_feats = (key_feat, exchange(key_feat_sent))

    up_t, query_feat, w_out_whole = upstream_phase(core_at, qk_t, cot, weights, other_weights, heads)
    moments = among_four(yz, product_phase(in_yz, (key_feat, key_feat_sent), tok, up_t, heads))
    scales, norm, sent = query_phase(query_feat, up_t, first, chips, heads)
    second = spread(to_each(sent)).reshape(sent.shape)

    attended, attended_sent, dens, sent, *outs = attend_phase(
        in_xy, query_feat, scales, up_t, second, cot, chips, heads
    )
    third = spread(to_each(sent)).reshape(sent.shape)
    terms = terms_phase(core_at, moments, among_four(xy, outs))
    attendeds = (attended, exchange(attended_sent))
    qgrad, qgrad_sent = query_back_phase(qk_t, scales, dens, up_t, second, norm, heads)
    qgrads = (qgrad, exchange(qgrad_sent))

    kgrad, kgrad_sent, sgrad, sent = key_phase(qk_t, value, third, (qgrad, qgrad_sent), tok, terms, heads)
    fourth = lax.all_to_all(sent.reshape(n, -1, sent.shape[1]), AXES, 0, 0, tiled=True).reshape(sent.shape)
    kgrads, sgrads = (kgrad, exchange(kgrad_sent)), (sgrad, exchange(sgrad))
    mixed, grad_tokens = outputs_phase(
        core_at, attendeds, qgrads, kgrads, key_feats, sgrads, (weights, other_weights), w_out_whole, heads
    )
    grad_query, grad_key, grad_value, grad_out = finish_phase(
        core_at, fourth, sgrads, (grad_tokens, mixed), heads, scale_factor
    )
    return (mixed, grad_tokens, grad_query, grad_key, grad_value, grad_out)


def solution(mesh):
    chips = mesh.size // 2
    placed = P(AXES, None)
    return jax.shard_map(
        lambda *args: per_device(chips, *args),
        mesh=mesh,
        in_specs=(placed,) * 6,
        out_specs=(placed,) * 6,
        check_vma=False,
    )
```

```python
import jax
import jax.numpy as jnp
from jax import lax
from jax.experimental import pallas as pl
from jax.experimental.pallas import tpu as pltpu
from jax.sharding import PartitionSpec as P

H = 8
DK = 16
DV = 128
BANDS = DK // 2 + 1
FPAD = (BANDS + 2) * DK
SPAD = 256
AXES = ("ctx", "seq")
BLOCK = 512
VMEM = 60 * 2**20
BF = jnp.bfloat16
F32 = jnp.float32
SQUARE = (2.0 * DK) ** (-0.5)
LINEAR = DK ** (-0.25)


def dot(a, b, contract):
    return lax.dot_general(a, b, ((contract[:1], contract[1:]), ((), ())), preferred_element_type=F32)


def band_weight(shape, dim):
    row = lax.broadcasted_iota(jnp.int32, shape, dim)
    twice = (row >= DK) & (row < (BANDS - 1) * DK)
    return jnp.where(twice, 2.0, 1.0).astype(F32)


def shifted(u, d):
    return pltpu.roll(u, DK - d, 0) if d else u


def features(u):
    bands = [u * shifted(u, d) * SQUARE for d in range(BANDS)]
    first = lax.broadcasted_iota(jnp.int32, u.shape, 0) == 0
    return jnp.concatenate(bands + [u * LINEAR, jnp.where(first, 1.0, 0.0)], axis=0).astype(BF)


def features_back(u, fgrad):
    def band(d):
        return fgrad[d * DK : (d + 1) * DK]

    total = band(0) * u + band(BANDS - 1) * shifted(u, BANDS - 1)
    for d in range(1, BANDS - 1):
        total = total + band(d) * shifted(u, d) + shifted(band(d) * u, DK - d)
    return total * (2.0 * SQUARE) + band(BANDS) * LINEAR


def in_parts(row):
    high = row.astype(BF).astype(F32)
    rest = row - high
    mid = rest.astype(BF).astype(F32)
    at = lax.broadcasted_iota(jnp.int32, (16, row.shape[1]), 0)
    low = jnp.where(at == 2, rest - mid, 0.0)
    return jnp.where(at == 0, high, jnp.where(at == 1, mid, low)).astype(BF)


def rows_of(array, head, size):
    return array[head * size : (head + 1) * size]


def head_row(rows, head):
    first, second = rows[4 * head : 4 * head + 2, :], rows[4 * head + 2 : 4 * head + 4, :]
    both = first + second
    return jnp.concatenate([both[:1], both[1:]], axis=1)


def split_rows(per_head):
    found = []
    for row in per_head:
        high = row.astype(BF).astype(F32)
        for part in (high, row - high):
            found += [part[:, :128], part[:, 128:]]
    found += [jnp.zeros((1, 128), F32)] * (16 - len(found))
    return jnp.concatenate(found, axis=0).astype(BF)


def column(row):
    return jnp.broadcast_to(row, (8, row.shape[1])).T[:FPAD, :1]


def add_chips(ref, rows):
    total = ref[:rows, :].astype(F32)
    for at in range(rows, ref.shape[0], rows):
        total = total + ref[at : at + rows, :].astype(F32)
    return total


def lane_sums(x):
    return sum(x[:, i : i + 128] for i in range(0, x.shape[1], 128))


def weighted_turned(state_ref, head):
    whole = state_ref[head * SPAD : (head + 1) * SPAD, :].astype(F32)
    return (whole * band_weight((SPAD, DV), 0)).T.astype(BF)


def call(body, count, ins, kinds, outs, out_kinds, scratch, flops, size=BLOCK):
    block = min(size, count // 2 if "pair" in kinds or "pair1" in out_kinds else count)
    steps = count // block

    def pieces(x, kind):
        if kind in ("pair", "pair1"):
            half = steps // 2
            return pieces_of(0, half, x[0].shape, kind) + pieces_of(1, half, x[1].shape, kind)
        if kind in (0, 1):
            return pieces_of(0, steps, x.shape, kind)
        if kind == "late":
            return [(0, pl.ds(0, x.shape[0]), pl.ds(0, x.shape[1]))]
        if kind is not None and kind[0] == "from":
            return [(0, pl.ds(0, x.shape[0]), pl.ds(kind[1], x.shape[1] - kind[1]))]
        if kind is not None:
            return [(0, pl.ds(0, x.shape[0]), pl.ds(kind[0] * kind[1], kind[0]))]
        return [(0, pl.ds(0, x.shape[0]), pl.ds(0, x.shape[1]))]

    def pieces_of(which, number, dims, kind):
        if kind in (0, "pair"):
            return [(which, pl.ds(i * block, block), pl.ds(0, dims[1])) for i in range(number)]
        return [(which, pl.ds(0, dims[0]), pl.ds(i * block, block)) for i in range(number)]

    def members(x, kind):
        return list(x) if kind in ("pair", "pair1") else [x]

    plans = [[] if kind in ("scalar", "any") else pieces(x, kind) for x, kind in zip(ins, kinds)]
    out_plans = [pieces(x, kind) for x, kind in zip(outs, out_kinds)]
    buffers = [
        pltpu.VMEM((rows.size, cols.size), members(x, kind)[0].dtype)
        for x, kind, plan in zip(tuple(ins) + tuple(outs), tuple(kinds) + tuple(out_kinds), plans + out_plans)
        for _, rows, cols in plan
    ]

    def kernel(*refs):
        refs = list(refs)

        def take(number):
            found = refs[:number]
            del refs[:number]
            return found

        given = [take(len(members(x, kind))) for x, kind in zip(ins, kinds)]
        made = [take(len(members(x, kind))) for x, kind in zip(outs, out_kinds)]
        held, sent = [take(len(plan)) for plan in plans], [take(len(plan)) for plan in out_plans]
        arrived, left = take(2)
        own = refs

        reads, at = [[] for _ in range(steps)], 0
        for source, buffer, plan, kind in zip(given, held, plans, kinds):
            for i, (which, rows, cols) in enumerate(plan):
                reads[steps - 1 if kind == "late" else i].append(pltpu.make_async_copy(source[which].at[rows, cols], buffer[i], arrived.at[at]))
                at += 1
        writes, at = [], 0
        for target, buffer, plan in zip(made, sent, out_plans):
            writes.append([])
            for i, (which, rows, cols) in enumerate(plan):
                writes[-1].append(pltpu.make_async_copy(buffer[i], target[which].at[rows, cols], left.at[at]))
                at += 1
        for step in reads:
            for copy in step:
                copy.start()
        for i in range(steps):
            for copy in reads[i]:
                copy.wait()
            at_first = lambda fn, i=i: fn() if i == 0 else None
            at_first.block = i
            body(
                at_first,
                lambda fn, i=i: fn() if i == steps - 1 else None,
                *[buffer[min(i, len(buffer) - 1)] if buffer else source[0] for buffer, source in zip(held, given)],
                *[buffer[min(i, len(buffer) - 1)] for buffer in sent],
                *own,
            )
            for copies in writes:
                if len(copies) == steps:
                    copies[i].start()
                elif i == steps - 1:
                    copies[0].start()
        for copies in writes:
            for copy in copies:
                copy.wait()

    args = [y for x, kind in zip(ins, kinds) for y in members(x, kind)]
    results = [y for x, kind in zip(outs, out_kinds) for y in members(x, kind)]
    spaces = [pltpu.SMEM if kind == "scalar" else pl.ANY for x, kind in zip(ins, kinds) for _ in members(x, kind)]
    nbytes = sum(x.size * x.dtype.itemsize for x in args + results)
    return pl.pallas_call(
        kernel,
        in_specs=[pl.BlockSpec(memory_space=space) for space in spaces],
        out_specs=[pl.BlockSpec(memory_space=pl.ANY)] * len(results),
        out_shape=results,
        scratch_shapes=buffers
        + [
            pltpu.SemaphoreType.DMA((sum(len(plan) for plan in plans),)),
            pltpu.SemaphoreType.DMA((sum(len(plan) for plan in out_plans),)),
        ]
        + list(scratch),
        compiler_params=pltpu.CompilerParams(vmem_limit_bytes=VMEM),
        cost_estimate=pl.CostEstimate(flops=flops, bytes_accessed=nbytes, transcendentals=0),
    )(*args)


def shape(dims, dtype):
    return jax.ShapeDtypeStruct(dims, dtype)


def clear(*refs):
    for ref in refs:
        ref[...] = jnp.zeros(ref.shape, ref.dtype)


def weights_phase(w_query, w_key, w_value, w_out, chips, heads):
    qk, cols, half = heads * DK, heads * DV, w_out.shape[1] // 2

    def body(q_ref, k_ref, v_ref, o_ref, out_ref, pair_ref, sems):
        query, key, value, rest = (ref[...].astype(F32) for ref in (q_ref, k_ref, v_ref, o_ref))
        halves = [
            jnp.concatenate(
                [
                    query[:, c * qk : (c + 1) * qk],
                    key[:, c * qk : (c + 1) * qk],
                    value[:, c * cols : (c + 1) * cols],
                    rest[:, c * half : (c + 1) * half],
                ],
                axis=1,
            )
            for c in range(2)
        ]
        pair = jnp.concatenate(halves, axis=0).astype(BF)
        for p in range(chips // 8):
            pair_ref[2 * rows * p : 2 * rows * (p + 1), :] = pair
        part = pair_ref.shape[0]
        copies = [pltpu.make_async_copy(pair_ref, out_ref.at[pl.ds(part * k, part), :], sems.at[k]) for k in range(8)]
        for copy in copies:
            copy.start()
        for copy in copies:
            copy.wait()

    rows = w_query.shape[0]
    return pl.pallas_call(
        body,
        out_specs=pl.BlockSpec(memory_space=pl.ANY),
        out_shape=shape((2 * chips * rows, 2 * qk + cols + half), BF),
        scratch_shapes=[pltpu.VMEM((2 * rows * (chips // 8), 2 * qk + cols + half), BF), pltpu.SemaphoreType.DMA((8,))],
        compiler_params=pltpu.CompilerParams(vmem_limit_bytes=VMEM),
        cost_estimate=pl.CostEstimate(flops=0, bytes_accessed=2 * 2 * chips * rows * (2 * qk + cols + half), transcendentals=0),
    )(w_query, w_key, w_value, w_out)


def keys_phase(tokens, w_qkv, chips, heads):
    qk = heads * DK

    def body(at_first, at_last, slab_ref, w_ref, qk_ref, value_ref, feat_ref, sent_ref, state_acc, norm_acc):
        at_first(lambda: clear(state_acc, norm_acc))
        joined = dot(slab_ref[...], w_ref[...], (1, 0))
        qk_t = joined[:, : 2 * qk].T.astype(BF)
        value = joined[:, 2 * qk :].astype(BF)
        qk_ref[...] = qk_t
        value_ref[...] = value
        keys = qk_t.astype(F32)[qk:]
        found = []
        for head in range(heads):
            feat = features(rows_of(keys, head, DK))
            found.append(feat)
            state_acc[head, :FPAD, :] += dot(feat, value[:, head * DV : (head + 1) * DV], (1, 0))
            norm_acc[head, :FPAD, :] += lane_sums(feat.astype(F32))
        feat_ref[...] = jnp.concatenate(found, axis=0)

        @at_last
        def _():
            norm = split_rows([jnp.sum(norm_acc[head], axis=1)[None] for head in range(heads)])
            state = state_acc[...].reshape(heads * SPAD, DV).astype(BF)
            part = heads * SPAD // chips
            for p in range(chips):
                sent_ref[2 * part * p : 2 * part * p + part, :] = state[part * p : part * (p + 1)]
                sent_ref[2 * part * p + part : 2 * part * (p + 1), :] = norm

    count = 2 * tokens[0].shape[0]
    return call(
        body,
        count,
        (tokens, w_qkv),
        ("pair", (2 * qk + heads * DV, 0)),
        (
            shape((2 * qk, count), BF),
            shape((count, heads * DV), BF),
            (shape((heads * FPAD, count // 2), BF),) * 2,
            shape((2 * heads * SPAD, DV), BF),
        ),
        (1, 0, "pair1", None),
        [pltpu.VMEM((heads, SPAD, DV), F32), pltpu.VMEM((heads, SPAD, 128), F32)],
        2 * count * heads * (w_qkv.shape[0] * (2 * DK + DV) + FPAD * DV * 2),
    )


def upstream_phase(core, qk_t, cot, weights, other_weights, heads):
    count, width = qk_t.shape[1], cot[0].shape[1]
    rows, half = heads * DV, width // 2
    joined = 2 * heads * DK + heads * DV

    def body(at_first, at_last, core_ref, qk_ref, slab_ref, mine_ref, theirs_ref, up_ref, feat_ref, w_ref):
        at = core_ref[0, 0]

        @at_first
        def _():
            mine, theirs = mine_ref[...], theirs_ref[...]
            w_ref[:, :half] = jnp.where(at == 0, mine, theirs)
            w_ref[:, half:] = jnp.where(at == 0, theirs, mine)

        here = w_ref[pl.ds(pl.multiple_of(at * rows, rows), rows), :]
        up_ref[...] = dot(here, slab_ref[...], (1, 1))
        query = qk_ref[...].astype(F32)
        for head in range(heads):
            feat_ref[head * FPAD : (head + 1) * FPAD, :] = features(rows_of(query, head, DK))

    return call(
        body,
        count,
        (core, qk_t, cot, weights, other_weights),
        ("scalar", 1, "pair", ("from", joined), ("from", joined)),
        (shape((rows, count), F32), shape((heads * FPAD, count), BF), shape((2 * rows, width), BF)),
        (1, 1, None),
        [],
        2 * count * rows * width,
    )


def product_phase(turn, rows_t, slabs, after, parts):
    rows, count = rows_t[0].shape[0], 2 * rows_t[0].shape[1]
    size = rows // parts
    width = slabs[0].shape[1]

    def body(at_first, at_last, turn_ref, rows_ref, slab_ref, after_ref, *refs):
        out_refs, acc = refs[:parts], refs[parts]
        at_first(lambda: clear(acc))
        acc[...] += dot(rows_ref[...], slab_ref[...], (1, 0))

        @at_last
        def _():
            for k in range(parts):
                part = turn_ref[0, 0] ^ k
                out_refs[k][...] = acc[pl.ds(pl.multiple_of(part * size, 16), size), :].T.astype(BF)

    return call(
        body,
        count,
        (turn, rows_t, slabs, after),
        ("scalar", "pair1", "pair", "any"),
        (shape((width, size), BF),) * parts,
        (None,) * parts,
        [pltpu.VMEM((rows, width), F32)],
        2 * count * rows * width,
    )


def query_phase(feats, up_t, first, chips, heads):
    count = up_t.shape[1]
    part = heads * SPAD // chips

    def body(at_first, at_last, feat_ref, up_ref, first_ref, scale_ref, norm_ref, sent_ref, acc, state_own):
        at_first(lambda: clear(acc))

        @at_first
        def _():
            total = add_chips(first_ref, 2 * part)
            state_own[...] = total[:part].astype(BF)
            norm_ref[...] = total[part:]

        at = lax.broadcasted_iota(jnp.int32, scale_ref.shape, 0)
        scales = jnp.zeros(scale_ref.shape, F32)
        for head in range(heads):
            feat = feat_ref[head * FPAD : (head + 1) * FPAD, :]
            parts = in_parts(head_row(norm_ref[...], head) * band_weight((1, SPAD), 1))[:, :FPAD]
            scale = 1.0 / jnp.sum(dot(parts, feat, (1, 0)), axis=0, keepdims=True)
            grad_num = (up_ref[head * DV : (head + 1) * DV, :] * scale).astype(BF)
            acc[head, :FPAD, :] += dot(feat, grad_num, (1, 1))
            scales = jnp.where(at == head, scale, scales)
        scale_ref[...] = scales

        @at_last
        def _():
            sent_ref[:, :DV] = acc[...].reshape(heads * SPAD, DV).astype(BF)
            for p in range(chips):
                sent_ref[p * part : (p + 1) * part, DV:] = state_own[...]

    return call(
        body,
        count,
        (feats, up_t, first),
        (1, 1, None),
        (shape((8, count), F32), shape((16, 128), F32), shape((heads * SPAD, 2 * DV), BF)),
        (1, None, None),
        [pltpu.VMEM((heads, SPAD, DV), F32), pltpu.VMEM((part, DV), BF)],
        2 * count * heads * FPAD * DV * 2,
    )


def attend_phase(turn, feats, scales, up_t, second, cot, chips, heads):
    count = up_t.shape[1]
    width = cot[0].shape[1]
    quarter = width // 4

    def body(
        at_first, at_last, turn_ref, feat_ref, scale_ref, up_ref, state_ref, sgrad_ref, slab_ref,
        att_ref, den_ref, sent_ref, out0, out1, out2, out3, turned, acc, out_acc,
    ):
        at_first(lambda: clear(acc, out_acc))

        @at_first
        def _():
            for head in range(heads):
                turned[head] = weighted_turned(state_ref, head)

        at = lax.broadcasted_iota(jnp.int32, den_ref.shape, 0)
        dens = jnp.zeros(den_ref.shape, F32)
        found = []
        for head in range(heads):
            feat = feat_ref[head * FPAD : (head + 1) * FPAD, :]
            scale = scale_ref[head : head + 1, :]
            att = dot(turned[head, :, :FPAD], feat, (1, 0)) * scale
            grad_num = up_ref[head * DV : (head + 1) * DV, :] * scale
            grad_den = -jnp.sum(grad_num * att, axis=0, keepdims=True)
            acc[head, :FPAD, :] += lane_sums(feat.astype(F32) * grad_den)
            found.append(att.astype(BF))
            dens = jnp.where(at == head, grad_den, dens)
        den_ref[...] = dens
        attended = jnp.concatenate(found, axis=0)
        att_ref[...] = attended
        out_acc[...] += dot(attended, slab_ref[...], (1, 0))

        @at_last
        def _():
            ngrad = split_rows([jnp.sum(acc[head], axis=1)[None] for head in range(heads)])
            sgrad_own = add_chips(sgrad_ref, ngrad.shape[0]).astype(BF)
            both = jnp.concatenate([sgrad_own, ngrad], axis=1)
            for p in range(chips):
                sent_ref[p * both.shape[0] : (p + 1) * both.shape[0], :] = both
            for k, out_ref in enumerate((out0, out1, out2, out3)):
                part = turn_ref[0, 0] ^ k
                out_ref[...] = out_acc[:, pl.ds(pl.multiple_of(part * quarter, 128), quarter)].astype(BF)

    return call(
        body,
        count,
        (turn, feats, scales, up_t, second, second, cot),
        ("scalar", 1, 1, 1, (DV, 1), (DV, 0), "pair"),
        (
            (shape((heads * DV, count // 2), BF),) * 2,
            shape((8, count), F32),
            shape(second.shape, BF),
        )
        + (shape((heads * DV, quarter), BF),) * 4,
        ("pair1", 1) + (None,) * 5,
        [
            pltpu.VMEM((heads, DV, SPAD), BF),
            pltpu.VMEM((heads, SPAD, 128), F32),
            pltpu.VMEM((heads * DV, width), F32),
        ],
        2 * count * (heads * FPAD * DV * 2 + heads * DV * width),
    )


def query_back_phase(qk_t, scales, dens, up_t, second, norm, heads):
    count = up_t.shape[1]

    def body(at_first, at_last, qk_ref, scale_ref, den_ref, up_ref, state_ref, norm_ref, qgrad_ref):
        query = qk_ref[...].astype(F32)
        found = []
        for head in range(heads):
            grad_num = (up_ref[head * DV : (head + 1) * DV, :] * scale_ref[head : head + 1, :]).astype(BF)
            fgrad = dot(state_ref[head * SPAD : head * SPAD + FPAD, :], grad_num, (1, 0))
            fgrad = fgrad + column(head_row(norm_ref[...], head)) * den_ref[head : head + 1, :]
            found.append(features_back(rows_of(query, head, DK), fgrad).astype(BF))
        qgrad_ref[...] = jnp.concatenate(found, axis=0)

    return call(
        body,
        count,
        (qk_t, scales, dens, up_t, second, norm),
        (1, 1, 1, 1, (DV, 1), None),
        ((shape((heads * DK, count // 2), BF),) * 2,),
        ("pair1",),
        [],
        2 * count * heads * FPAD * DV,
    )


def key_phase(qk_t, value, third, qgrads, tokens, core, moments, outs, heads):
    count, qk = value.shape[0], heads * DK
    width = tokens[0].shape[1]

    def body(
        at_first, at_last, qk_ref, value_ref, sgrad_ref, rows_ref, qgrad_ref, slab_ref, core_ref, m0, m1, m2, m3, o0, o1, o2, o3,
        kgrad_ref, copy_ref, sent_ref, acc, ngrad_ref,
    ):
        at_first(lambda: clear(acc))

        @at_first
        def _():
            ngrad_ref[...] = add_chips(rows_ref, 16)
            copy_ref[...] = sgrad_ref[...]

        keys = qk_ref[...].astype(F32)[qk:]
        found = []
        for head in range(heads):
            fgrad = dot(
                sgrad_ref[head * SPAD : head * SPAD + FPAD, :],
                value_ref[:, head * DV : (head + 1) * DV],
                (1, 1),
            )
            fgrad = fgrad + column(head_row(ngrad_ref[...], head))
            found.append(features_back(rows_of(keys, head, DK), fgrad))
        kgrad = jnp.concatenate(found, axis=0).astype(BF)
        kgrad_ref[...] = kgrad
        both = jnp.concatenate([qgrad_ref[...], kgrad], axis=0)
        acc[...] += dot(both, slab_ref[...], (1, 0))

        @at_last
        def _():
            sent_ref[:, : 2 * qk] = acc[...].T.astype(BF)
            sent_ref[:, 2 * qk : 2 * qk + FPAD] = sum(ref[...].astype(F32) for ref in (m0, m1, m2, m3)).astype(BF)
            first = core_ref[0, 0] == 0
            out = sum(ref[...].astype(F32) for ref in (o0, o1, o2, o3))
            half = out.shape[0]
            for j in range(2):
                sent_ref[j * half : (j + 1) * half, 2 * qk + FPAD :] = jnp.where(first == (j == 0), out, 0.0).astype(BF)

    return call(
        body,
        count,
        (qk_t, value, third, third, qgrads, tokens, core, *moments, *outs),
        (1, 0, (DV, 0), (DV, 1), "pair1", "pair", "scalar") + ("late",) * 8,
        (
            (shape((qk, count // 2), BF),) * 2,
            shape((third.shape[0], DV), BF),
            shape((width, 2 * qk + FPAD + outs[0].shape[1]), BF),
        ),
        ("pair1", None, None),
        [pltpu.VMEM((2 * qk, width), F32), pltpu.VMEM((16, DV), F32)],
        2 * count * (heads * FPAD * DV + 2 * qk * width),
    )


def outputs_phase(core, attended, qgrads, kgrads, feats, sgrads, weights, w_out, heads):
    count, width = attended[0].shape[1], w_out.shape[1]
    rows, joined = heads * DV, 2 * heads * DK + heads * DV

    def body(at_first, at_last, core_ref, *refs):
        atts, qs, ks, fs, ss, ws = (refs[2 * i : 2 * i + 2] for i in range(6))
        out_ref, mixed_ref, gtok_ref, turned = refs[12:]
        at = core_ref[0, 0]

        @at_first
        def _():
            for c in range(2):
                for head in range(heads):
                    turned[c, head] = weighted_turned(ss[c], head)

        mixed, gtok = 0.0, 0.0
        for c in range(2):
            first = pl.multiple_of((at if c == 0 else 1 - at) * rows, rows)
            mixed = mixed + dot(atts[c][...], out_ref[pl.ds(first, rows), :], (0, 0))
            parts = [qs[c][...], ks[c][...]]
            for head in range(heads):
                feat = fs[c][head * FPAD : (head + 1) * FPAD, :]
                parts.append(dot(turned[c, head, :, :FPAD], feat, (1, 0)).astype(BF))
            gtok = gtok + dot(jnp.concatenate(parts, axis=0), ws[c][...], (0, 1))
        mixed_ref[...] = mixed.astype(BF)
        gtok_ref[...] = gtok.astype(BF)

    return call(
        body,
        count,
        (core, *attended, *qgrads, *kgrads, *feats, *sgrads, *weights, w_out),
        ("scalar",) + (1,) * 8 + (None,) * 2 + ((joined, 0),) * 2 + (None,),
        (shape((count, width), BF), shape((count, width), BF)),
        (0, 0),
        [pltpu.VMEM((2, heads, DV, SPAD), BF)],
        2 * count * 2 * (joined * width + rows * width + heads * FPAD * DV),
    )


def finish_phase(core, fourth, sgrads, after, heads, scale_factor):
    rows, qk = 8, heads * DK
    quarter = fourth.shape[1] - 2 * qk - FPAD

    def body(at_first, at_last, core_ref, recv_ref, mine_ref, other_ref, *refs):
        query_ref, key_ref, value_ref, out_ref, wgrad, moment, out = refs[-7:]

        at_first(lambda: clear(wgrad, moment, out))
        odd = at_first.block % 2
        wgrad[...] += add_chips(recv_ref.at[:, pl.ds(0, 2 * qk)], 2 * rows)
        parts = recv_ref.shape[0] // (2 * rows)
        for which in range(2):
            some = [p for p in range(parts) if p // 2 % 2 == which]
            moment[2 * odd + which] += sum(
                recv_ref[2 * rows * p : 2 * rows * (p + 1), 2 * qk : 2 * qk + FPAD].astype(F32) for p in some
            )
            some = [p for p in range(parts) if p % 2 == which]
            out[2 * which + 1 - odd] += sum(
                recv_ref[2 * rows * p : 2 * rows * (p + 1), 2 * qk + FPAD :].astype(F32) for p in some
            )
        @at_last
        def _():
            for x in range(4):
                out_ref[:, x * quarter : (x + 1) * quarter] = (out[x, :rows] + out[x, rows:]) * scale_factor
            first = core_ref[0, 0] == 0
            both = wgrad[...] * scale_factor
            query_ref[...] = jnp.concatenate([both[:rows, :qk], both[rows:, :qk]], axis=1)
            key_ref[...] = jnp.concatenate([both[:rows, qk:], both[rows:, qk:]], axis=1)
            weight = band_weight((1, FPAD), 1) * scale_factor
            found = [[], []]
            for head in range(heads):
                whole = moment[head] * weight
                high = whole.astype(BF)
                split = jnp.concatenate([high, (whole - high.astype(F32)).astype(BF)], axis=0)
                for which, ref in enumerate((mine_ref, other_ref)):
                    both = dot(split, ref[head * SPAD : head * SPAD + FPAD, :], (1, 0))
                    both = both[: 2 * rows] + both[2 * rows :]
                    low, up = both[:rows], both[rows:]
                    found[which].append(jnp.where(first, low, up) if which == 0 else jnp.where(first, up, low))
            mine, other = (jnp.concatenate(part, axis=1) for part in found)
            value_ref[:, : heads * DV] = jnp.where(first, mine, other)
            value_ref[:, heads * DV :] = jnp.where(first, other, mine)

    return call(
        body,
        fourth.shape[0],
        (core, fourth, *sgrads, *after),
        ("scalar", 0, "late", "late") + ("any",) * len(after),
        (
            shape((rows, 2 * qk), F32),
            shape((rows, 2 * qk), F32),
            shape((rows, 2 * heads * DV), F32),
            shape((rows, 4 * quarter), F32),
        ),
        (None,) * 4,
        [
            pltpu.VMEM((2 * rows, 2 * qk), F32),
            pltpu.VMEM((heads, 2 * rows, FPAD), F32),
            pltpu.VMEM((4, 2 * rows, quarter), F32),
        ],
        0,
        fourth.shape[0] // 4,
    )


def per_device(chips, tokens, w_query, w_key, w_value, w_out, cotangent):
    n = 2 * chips
    heads = H // 2
    own, width = tokens.shape
    qk = heads * DK
    core = lax.axis_index("seq") % 2
    core_at = core.astype(jnp.int32).reshape(1, 1)
    same_core = [[2 * p + c for p in range(chips)] for c in range(2)]
    swap = [(i, i ^ 1) for i in range(n)]
    scale_factor = (own * n) ** (-0.5)

    def exchange(x):
        return lax.ppermute(x, AXES, swap)

    def spread(x):
        return lax.all_to_all(x, AXES, 0, 0, axis_index_groups=same_core, tiled=True)

    def among_four(flips, parts):
        found = [parts[0]]
        for step in (1, 2, 3):
            moves = []
            for i in range(n):
                at = place(i)
                for bit in (0, 1):
                    at = flips[bit](*at) if step >> bit & 1 else at
                moves.append((i, device(*at)))
            found.append(lax.ppermute(parts[step], AXES, moves))
        return found

    yz = (lambda y, x, z, c: (y, x, z ^ 1, c), lambda y, x, z, c: (y ^ 1, x, z, c))
    xy = (lambda y, x, z, c: ((y + 2 * (y % 2) - 1) % 4, x, z, c), lambda y, x, z, c: (y, x ^ 1, z, c))

    def place(i):
        return (i // 32, 2 * (i // 16 % 2) + i // 2 % 2, i // 4 % 4, i % 2)

    def device(y, x, z, c):
        return (((y * 2 + x // 2) * 4 + z) * 2 + x % 2) * 2 + c

    def to_each(x):
        return x.reshape(chips, -1, x.shape[1])

    ctx, seq = lax.axis_index("ctx"), lax.axis_index("seq")
    in_yz, in_xy = (
        v.astype(jnp.int32).reshape(1, 1)
        for v in (2 * (ctx // 8 % 2) + ctx % 2, 2 * (seq // 2) + 1 - ctx // 8 % 2)
    )

    to_send = weights_phase(w_query, w_key, w_value, w_out, chips, heads)
    weights = lax.all_to_all(to_send.reshape(n, -1, to_send.shape[1]), AXES, 0, 0, tiled=True)
    weights = weights.reshape(-1, to_send.shape[1])
    tok = (tokens, exchange(tokens))
    cot = (cotangent, exchange(cotangent))
    other_weights = exchange(weights)

    qk_t, value, key_feat, key_feat_sent, sent = keys_phase(tok, weights, chips, heads)
    first = spread(to_each(sent)).reshape(sent.shape)
    key_feats = (key_feat, exchange(key_feat_sent))

    up_t, query_feat, w_out_whole = upstream_phase(core_at, qk_t, cot, weights, other_weights, heads)
    moments = among_four(yz, product_phase(in_yz, (key_feat, key_feat_sent), tok, up_t, heads))
    scales, norm, sent = query_phase(query_feat, up_t, first, chips, heads)
    second = spread(to_each(sent)).reshape(sent.shape)

    attended, attended_sent, dens, sent, *outs = attend_phase(
        in_xy, query_feat, scales, up_t, second, cot, chips, heads
    )
    third = spread(to_each(sent)).reshape(sent.shape)
    outs = among_four(xy, outs)
    attendeds = (attended, exchange(attended_sent))
    qgrad, qgrad_sent = query_back_phase(qk_t, scales, dens, up_t, second, norm, heads)
    qgrads = (qgrad, exchange(qgrad_sent))

    kgrad, kgrad_sent, sgrad, sent = key_phase(qk_t, value, third, (qgrad, qgrad_sent), tok, core_at, moments, outs, heads)
    fourth = lax.all_to_all(sent.reshape(n, -1, sent.shape[1]), AXES, 0, 0, tiled=True).reshape(sent.shape)
    kgrads, sgrads = (kgrad, exchange(kgrad_sent)), (sgrad, exchange(sgrad))
    mixed, grad_tokens = outputs_phase(
        core_at, attendeds, qgrads, kgrads, key_feats, sgrads, (weights, other_weights), w_out_whole, heads
    )
    grad_query, grad_key, grad_value, grad_out = finish_phase(
        core_at, fourth, sgrads, (grad_tokens, mixed), heads, scale_factor
    )
    return (mixed, grad_tokens, grad_query, grad_key, grad_value, grad_out)


def solution(mesh):
    chips = mesh.size // 2
    placed = P(AXES, None)
    return jax.shard_map(
        lambda *args: per_device(chips, *args),
        mesh=mesh,
        in_specs=(placed,) * 6,
        out_specs=(placed,) * 6,
        check_vma=False,
    )
```

```python
import jax
import jax.numpy as jnp
from jax import lax
from jax.experimental import pallas as pl
from jax.experimental.pallas import tpu as pltpu
from jax.sharding import PartitionSpec as P

H = 8
DK = 16
DV = 128
BANDS = DK // 2 + 1
FPAD = (BANDS + 2) * DK
SPAD = 256
AXES = ("ctx", "seq")
BLOCK = 512
VMEM = 60 * 2**20
BF = jnp.bfloat16
F32 = jnp.float32
SQUARE = (2.0 * DK) ** (-0.5)
LINEAR = DK ** (-0.25)


def dot(a, b, contract):
    return lax.dot_general(a, b, ((contract[:1], contract[1:]), ((), ())), preferred_element_type=F32)


def band_weight(shape, dim):
    row = lax.broadcasted_iota(jnp.int32, shape, dim)
    twice = (row >= DK) & (row < (BANDS - 1) * DK)
    return jnp.where(twice, 2.0, 1.0).astype(F32)


def shifted(u, d):
    return pltpu.roll(u, DK - d, 0) if d else u


def features(u):
    bands = [u * shifted(u, d) * SQUARE for d in range(BANDS)]
    first = lax.broadcasted_iota(jnp.int32, u.shape, 0) == 0
    return jnp.concatenate(bands + [u * LINEAR, jnp.where(first, 1.0, 0.0)], axis=0).astype(BF)


def features_back(u, fgrad):
    def band(d):
        return fgrad[d * DK : (d + 1) * DK]

    total = band(0) * u + band(BANDS - 1) * shifted(u, BANDS - 1)
    for d in range(1, BANDS - 1):
        total = total + band(d) * shifted(u, d) + shifted(band(d) * u, DK - d)
    return total * (2.0 * SQUARE) + band(BANDS) * LINEAR


def in_parts(row):
    high = row.astype(BF).astype(F32)
    rest = row - high
    mid = rest.astype(BF).astype(F32)
    at = lax.broadcasted_iota(jnp.int32, (16, row.shape[1]), 0)
    low = jnp.where(at == 2, rest - mid, 0.0)
    return jnp.where(at == 0, high, jnp.where(at == 1, mid, low)).astype(BF)


def rows_of(array, head, size):
    return array[head * size : (head + 1) * size]


def head_row(rows, head):
    first, second = rows[4 * head : 4 * head + 2, :], rows[4 * head + 2 : 4 * head + 4, :]
    both = first + second
    return jnp.concatenate([both[:1], both[1:]], axis=1)


def split_rows(per_head):
    found = []
    for row in per_head:
        high = row.astype(BF).astype(F32)
        for part in (high, row - high):
            found += [part[:, :128], part[:, 128:]]
    found += [jnp.zeros((1, 128), F32)] * (16 - len(found))
    return jnp.concatenate(found, axis=0).astype(BF)


def column(row):
    return jnp.broadcast_to(row, (8, row.shape[1])).T[:FPAD, :1]


def add_chips(ref, rows):
    total = ref[:rows, :].astype(F32)
    for at in range(rows, ref.shape[0], rows):
        total = total + ref[at : at + rows, :].astype(F32)
    return total


def lane_sums(x):
    return sum(x[:, i : i + 128] for i in range(0, x.shape[1], 128))


def weighted_turned(state_ref, head):
    whole = state_ref[head * SPAD : (head + 1) * SPAD, :].astype(F32)
    return (whole * band_weight((SPAD, DV), 0)).T.astype(BF)


def call(body, count, ins, kinds, outs, out_kinds, scratch, flops, size=BLOCK):
    block = min(size, count // 2 if "pair" in kinds or "pair1" in out_kinds else count)
    steps = count // block

    def pieces(x, kind):
        if kind in ("pair", "pair1"):
            half = steps // 2
            return pieces_of(0, half, x[0].shape, kind) + pieces_of(1, half, x[1].shape, kind)
        if kind in (0, 1):
            return pieces_of(0, steps, x.shape, kind)
        if kind == "late":
            return [(0, pl.ds(0, x.shape[0]), pl.ds(0, x.shape[1]))]
        if kind is not None and kind[0] == "from":
            return [(0, pl.ds(0, x.shape[0]), pl.ds(kind[1], x.shape[1] - kind[1]))]
        if kind is not None:
            return [(0, pl.ds(0, x.shape[0]), pl.ds(kind[0] * kind[1], kind[0]))]
        return [(0, pl.ds(0, x.shape[0]), pl.ds(0, x.shape[1]))]

    def pieces_of(which, number, dims, kind):
        if kind in (0, "pair"):
            return [(which, pl.ds(i * block, block), pl.ds(0, dims[1])) for i in range(number)]
        return [(which, pl.ds(0, dims[0]), pl.ds(i * block, block)) for i in range(number)]

    def members(x, kind):
        return list(x) if kind in ("pair", "pair1") else [x]

    plans = [[] if kind in ("scalar", "any") else pieces(x, kind) for x, kind in zip(ins, kinds)]
    out_plans = [pieces(x, kind) for x, kind in zip(outs, out_kinds)]
    buffers = [
        pltpu.VMEM((rows.size, cols.size), members(x, kind)[0].dtype)
        for x, kind, plan in zip(tuple(ins) + tuple(outs), tuple(kinds) + tuple(out_kinds), plans + out_plans)
        for _, rows, cols in plan
    ]

    def kernel(*refs):
        refs = list(refs)

        def take(number):
            found = refs[:number]
            del refs[:number]
            return found

        given = [take(len(members(x, kind))) for x, kind in zip(ins, kinds)]
        made = [take(len(members(x, kind))) for x, kind in zip(outs, out_kinds)]
        held, sent = [take(len(plan)) for plan in plans], [take(len(plan)) for plan in out_plans]
        arrived, left = take(2)
        own = refs

        reads, at = [[] for _ in range(steps)], 0
        for source, buffer, plan, kind in zip(given, held, plans, kinds):
            for i, (which, rows, cols) in enumerate(plan):
                reads[steps - 1 if kind == "late" else i].append(pltpu.make_async_copy(source[which].at[rows, cols], buffer[i], arrived.at[at]))
                at += 1
        writes, at = [], 0
        for target, buffer, plan in zip(made, sent, out_plans):
            writes.append([])
            for i, (which, rows, cols) in enumerate(plan):
                writes[-1].append(pltpu.make_async_copy(buffer[i], target[which].at[rows, cols], left.at[at]))
                at += 1
        for step in reads:
            for copy in step:
                copy.start()
        for i in range(steps):
            for copy in reads[i]:
                copy.wait()
            at_first = lambda fn, i=i: fn() if i == 0 else None
            at_first.block = i
            body(
                at_first,
                lambda fn, i=i: fn() if i == steps - 1 else None,
                *[buffer[min(i, len(buffer) - 1)] if buffer else source[0] for buffer, source in zip(held, given)],
                *[buffer[min(i, len(buffer) - 1)] for buffer in sent],
                *own,
            )
            for copies in writes:
                if len(copies) == steps:
                    copies[i].start()
                elif i == steps - 1:
                    copies[0].start()
        for copies in writes:
            for copy in copies:
                copy.wait()

    args = [y for x, kind in zip(ins, kinds) for y in members(x, kind)]
    results = [y for x, kind in zip(outs, out_kinds) for y in members(x, kind)]
    spaces = [pltpu.SMEM if kind == "scalar" else pl.ANY for x, kind in zip(ins, kinds) for _ in members(x, kind)]
    nbytes = sum(x.size * x.dtype.itemsize for x in args + results)
    return pl.pallas_call(
        kernel,
        in_specs=[pl.BlockSpec(memory_space=space) for space in spaces],
        out_specs=[pl.BlockSpec(memory_space=pl.ANY)] * len(results),
        out_shape=results,
        scratch_shapes=buffers
        + [
            pltpu.SemaphoreType.DMA((sum(len(plan) for plan in plans),)),
            pltpu.SemaphoreType.DMA((sum(len(plan) for plan in out_plans),)),
        ]
        + list(scratch),
        compiler_params=pltpu.CompilerParams(vmem_limit_bytes=VMEM),
        cost_estimate=pl.CostEstimate(flops=flops, bytes_accessed=nbytes, transcendentals=0),
    )(*args)


def shape(dims, dtype):
    return jax.ShapeDtypeStruct(dims, dtype)


def clear(*refs):
    for ref in refs:
        ref[...] = jnp.zeros(ref.shape, ref.dtype)


def weights_phase(w_query, w_key, w_value, w_out, chips, heads):
    qk, cols, half = heads * DK, heads * DV, w_out.shape[1] // 2

    def body(q_ref, k_ref, v_ref, o_ref, out_ref, pair_ref, sems):
        query, key, value, rest = (ref[...].astype(F32) for ref in (q_ref, k_ref, v_ref, o_ref))
        halves = [
            jnp.concatenate(
                [
                    query[:, c * qk : (c + 1) * qk],
                    key[:, c * qk : (c + 1) * qk],
                    value[:, c * cols : (c + 1) * cols],
                    rest[:, c * half : (c + 1) * half],
                ],
                axis=1,
            )
            for c in range(2)
        ]
        pair = jnp.concatenate(halves, axis=0).astype(BF)
        for p in range(chips // 8):
            pair_ref[2 * rows * p : 2 * rows * (p + 1), :] = pair
        part = pair_ref.shape[0]
        copies = [pltpu.make_async_copy(pair_ref, out_ref.at[pl.ds(part * k, part), :], sems.at[k]) for k in range(8)]
        for copy in copies:
            copy.start()
        for copy in copies:
            copy.wait()

    rows = w_query.shape[0]
    return pl.pallas_call(
        body,
        out_specs=pl.BlockSpec(memory_space=pl.ANY),
        out_shape=shape((2 * chips * rows, 2 * qk + cols + half), BF),
        scratch_shapes=[pltpu.VMEM((2 * rows * (chips // 8), 2 * qk + cols + half), BF), pltpu.SemaphoreType.DMA((8,))],
        compiler_params=pltpu.CompilerParams(vmem_limit_bytes=VMEM),
        cost_estimate=pl.CostEstimate(flops=0, bytes_accessed=2 * 2 * chips * rows * (2 * qk + cols + half), transcendentals=0),
    )(w_query, w_key, w_value, w_out)


def keys_phase(tokens, w_qkv, chips, heads):
    qk = heads * DK

    def body(at_first, at_last, slab_ref, w_ref, qk_ref, value_ref, feat_ref, sent_ref, state_acc, norm_acc):
        at_first(lambda: clear(state_acc, norm_acc))
        joined = dot(slab_ref[...], w_ref[...], (1, 0))
        qk_t = joined[:, : 2 * qk].T.astype(BF)
        value = joined[:, 2 * qk :].astype(BF)
        qk_ref[...] = qk_t
        value_ref[...] = value
        keys = qk_t.astype(F32)[qk:]
        found = []
        for head in range(heads):
            feat = features(rows_of(keys, head, DK))
            found.append(feat)
            state_acc[head, :FPAD, :] += dot(feat, value[:, head * DV : (head + 1) * DV], (1, 0))
            norm_acc[head, :FPAD, :] += lane_sums(feat.astype(F32))
        feat_ref[...] = jnp.concatenate(found, axis=0)

        @at_last
        def _():
            norm = split_rows([jnp.sum(norm_acc[head], axis=1)[None] for head in range(heads)])
            state = state_acc[...].reshape(heads * SPAD, DV).astype(BF)
            part = heads * SPAD // chips
            for p in range(chips):
                sent_ref[2 * part * p : 2 * part * p + part, :] = state[part * p : part * (p + 1)]
                sent_ref[2 * part * p + part : 2 * part * (p + 1), :] = norm

    count = 2 * tokens[0].shape[0]
    return call(
        body,
        count,
        (tokens, w_qkv),
        ("pair", (2 * qk + heads * DV, 0)),
        (
            shape((2 * qk, count), BF),
            shape((count, heads * DV), BF),
            (shape((heads * FPAD, count // 2), BF),) * 2,
            shape((2 * heads * SPAD, DV), BF),
        ),
        (1, 0, "pair1", None),
        [pltpu.VMEM((heads, SPAD, DV), F32), pltpu.VMEM((heads, SPAD, 128), F32)],
        2 * count * heads * (w_qkv.shape[0] * (2 * DK + DV) + FPAD * DV * 2),
    )


def upstream_phase(core, qk_t, cot, weights, other_weights, heads):
    count, width = qk_t.shape[1], cot[0].shape[1]
    rows, half = heads * DV, width // 2
    joined = 2 * heads * DK + heads * DV

    def body(at_first, at_last, core_ref, qk_ref, slab_ref, mine_ref, theirs_ref, up_ref, feat_ref, w_ref):
        at = core_ref[0, 0]

        @at_first
        def _():
            mine, theirs = mine_ref[...], theirs_ref[...]
            w_ref[:, :half] = jnp.where(at == 0, mine, theirs)
            w_ref[:, half:] = jnp.where(at == 0, theirs, mine)

        here = w_ref[pl.ds(pl.multiple_of(at * rows, rows), rows), :]
        up_ref[...] = dot(here, slab_ref[...], (1, 1))
        query = qk_ref[...].astype(F32)
        for head in range(heads):
            feat_ref[head * FPAD : (head + 1) * FPAD, :] = features(rows_of(query, head, DK))

    return call(
        body,
        count,
        (core, qk_t, cot, weights, other_weights),
        ("scalar", 1, "pair", ("from", joined), ("from", joined)),
        (shape((rows, count), F32), shape((heads * FPAD, count), BF), shape((2 * rows, width), BF)),
        (1, 1, None),
        [],
        2 * count * rows * width,
    )


def product_phase(turn, rows_t, slabs, after, parts):
    rows, count = rows_t[0].shape[0], 2 * rows_t[0].shape[1]
    size = rows // parts
    width = slabs[0].shape[1]

    def body(at_first, at_last, turn_ref, rows_ref, slab_ref, after_ref, *refs):
        out_refs, acc = refs[:parts], refs[parts]
        at_first(lambda: clear(acc))
        acc[...] += dot(rows_ref[...], slab_ref[...], (1, 0))

        @at_last
        def _():
            for k in range(parts):
                part = turn_ref[0, 0] ^ k
                out_refs[k][...] = acc[pl.ds(pl.multiple_of(part * size, 16), size), :].astype(BF)

    return call(
        body,
        count,
        (turn, rows_t, slabs, after),
        ("scalar", "pair1", "pair", "any"),
        (shape((size, width), BF),) * parts,
        (None,) * parts,
        [pltpu.VMEM((rows, width), F32)],
        2 * count * rows * width,
    )


def query_phase(feats, up_t, first, chips, heads):
    count = up_t.shape[1]
    part = heads * SPAD // chips

    def body(at_first, at_last, feat_ref, up_ref, first_ref, scale_ref, norm_ref, sent_ref, acc, state_own):
        at_first(lambda: clear(acc))

        @at_first
        def _():
            total = add_chips(first_ref, 2 * part)
            state_own[...] = total[:part].astype(BF)
            norm_ref[...] = total[part:]

        at = lax.broadcasted_iota(jnp.int32, scale_ref.shape, 0)
        scales = jnp.zeros(scale_ref.shape, F32)
        for head in range(heads):
            feat = feat_ref[head * FPAD : (head + 1) * FPAD, :]
            parts = in_parts(head_row(norm_ref[...], head) * band_weight((1, SPAD), 1))[:, :FPAD]
            scale = 1.0 / jnp.sum(dot(parts, feat, (1, 0)), axis=0, keepdims=True)
            grad_num = (up_ref[head * DV : (head + 1) * DV, :] * scale).astype(BF)
            acc[head, :FPAD, :] += dot(feat, grad_num, (1, 1))
            scales = jnp.where(at == head, scale, scales)
        scale_ref[...] = scales

        @at_last
        def _():
            sent_ref[:, :DV] = acc[...].reshape(heads * SPAD, DV).astype(BF)
            for p in range(chips):
                sent_ref[p * part : (p + 1) * part, DV:] = state_own[...]

    return call(
        body,
        count,
        (feats, up_t, first),
        (1, 1, None),
        (shape((8, count), F32), shape((16, 128), F32), shape((heads * SPAD, 2 * DV), BF)),
        (1, None, None),
        [pltpu.VMEM((heads, SPAD, DV), F32), pltpu.VMEM((part, DV), BF)],
        2 * count * heads * FPAD * DV * 2,
    )


def attend_phase(turn, feats, scales, up_t, second, cot, chips, heads):
    count = up_t.shape[1]
    width = cot[0].shape[1]
    quarter = width // 4

    def body(
        at_first, at_last, turn_ref, feat_ref, scale_ref, up_ref, state_ref, sgrad_ref, slab_ref,
        att_ref, den_ref, sent_ref, out0, out1, out2, out3, turned, acc, out_acc,
    ):
        at_first(lambda: clear(acc, out_acc))

        @at_first
        def _():
            for head in range(heads):
                turned[head] = weighted_turned(state_ref, head)

        at = lax.broadcasted_iota(jnp.int32, den_ref.shape, 0)
        dens = jnp.zeros(den_ref.shape, F32)
        found = []
        for head in range(heads):
            feat = feat_ref[head * FPAD : (head + 1) * FPAD, :]
            scale = scale_ref[head : head + 1, :]
            att = dot(turned[head, :, :FPAD], feat, (1, 0)) * scale
            grad_num = up_ref[head * DV : (head + 1) * DV, :] * scale
            grad_den = -jnp.sum(grad_num * att, axis=0, keepdims=True)
            acc[head, :FPAD, :] += lane_sums(feat.astype(F32) * grad_den)
            found.append(att.astype(BF))
            dens = jnp.where(at == head, grad_den, dens)
        den_ref[...] = dens
        attended = jnp.concatenate(found, axis=0)
        att_ref[...] = attended
        out_acc[...] += dot(attended, slab_ref[...], (1, 0))

        @at_last
        def _():
            ngrad = split_rows([jnp.sum(acc[head], axis=1)[None] for head in range(heads)])
            sgrad_own = add_chips(sgrad_ref, ngrad.shape[0]).astype(BF)
            both = jnp.concatenate([sgrad_own, ngrad], axis=1)
            for p in range(chips):
                sent_ref[p * both.shape[0] : (p + 1) * both.shape[0], :] = both
            for k, out_ref in enumerate((out0, out1, out2, out3)):
                part = turn_ref[0, 0] ^ k
                out_ref[...] = out_acc[:, pl.ds(pl.multiple_of(part * quarter, 128), quarter)].astype(BF)

    return call(
        body,
        count,
        (turn, feats, scales, up_t, second, second, cot),
        ("scalar", 1, 1, 1, (DV, 1), (DV, 0), "pair"),
        (
            (shape((heads * DV, count // 2), BF),) * 2,
            shape((8, count), F32),
            shape(second.shape, BF),
        )
        + (shape((heads * DV, quarter), BF),) * 4,
        ("pair1", 1) + (None,) * 5,
        [
            pltpu.VMEM((heads, DV, SPAD), BF),
            pltpu.VMEM((heads, SPAD, 128), F32),
            pltpu.VMEM((heads * DV, width), F32),
        ],
        2 * count * (heads * FPAD * DV * 2 + heads * DV * width),
    )


def query_back_phase(qk_t, scales, dens, up_t, second, norm, heads):
    count = up_t.shape[1]

    def body(at_first, at_last, qk_ref, scale_ref, den_ref, up_ref, state_ref, norm_ref, qgrad_ref):
        query = qk_ref[...].astype(F32)
        found = []
        for head in range(heads):
            grad_num = (up_ref[head * DV : (head + 1) * DV, :] * scale_ref[head : head + 1, :]).astype(BF)
            fgrad = dot(state_ref[head * SPAD : head * SPAD + FPAD, :], grad_num, (1, 0))
            fgrad = fgrad + column(head_row(norm_ref[...], head)) * den_ref[head : head + 1, :]
            found.append(features_back(rows_of(query, head, DK), fgrad).astype(BF))
        qgrad_ref[...] = jnp.concatenate(found, axis=0)

    return call(
        body,
        count,
        (qk_t, scales, dens, up_t, second, norm),
        (1, 1, 1, 1, (DV, 1), None),
        ((shape((heads * DK, count // 2), BF),) * 2,),
        ("pair1",),
        [],
        2 * count * heads * FPAD * DV,
    )


def key_phase(qk_t, value, third, qgrads, tokens, core, moments, outs, heads):
    count, qk = value.shape[0], heads * DK
    width = tokens[0].shape[1]

    def body(
        at_first, at_last, qk_ref, value_ref, sgrad_ref, rows_ref, qgrad_ref, slab_ref, core_ref, m0, m1, m2, m3, o0, o1, o2, o3,
        kgrad_ref, copy_ref, sent_ref, acc, ngrad_ref,
    ):
        at_first(lambda: clear(acc))

        @at_first
        def _():
            ngrad_ref[...] = add_chips(rows_ref, 16)
            copy_ref[...] = sgrad_ref[...]

        keys = qk_ref[...].astype(F32)[qk:]
        found = []
        for head in range(heads):
            fgrad = dot(
                sgrad_ref[head * SPAD : head * SPAD + FPAD, :],
                value_ref[:, head * DV : (head + 1) * DV],
                (1, 1),
            )
            fgrad = fgrad + column(head_row(ngrad_ref[...], head))
            found.append(features_back(rows_of(keys, head, DK), fgrad))
        kgrad = jnp.concatenate(found, axis=0).astype(BF)
        kgrad_ref[...] = kgrad
        both = jnp.concatenate([qgrad_ref[...], kgrad], axis=0)
        acc[...] += dot(both, slab_ref[...], (1, 0))

        @at_last
        def _():
            sent_ref[:, : 2 * qk] = acc[...].T.astype(BF)
            sent_ref[:, 2 * qk : 2 * qk + FPAD] = sum(ref[...].astype(F32) for ref in (m0, m1, m2, m3)).T.astype(BF)
            first = core_ref[0, 0] == 0
            out = sum(ref[...].astype(F32) for ref in (o0, o1, o2, o3))
            half = out.shape[0]
            for j in range(2):
                sent_ref[j * half : (j + 1) * half, 2 * qk + FPAD :] = jnp.where(first == (j == 0), out, 0.0).astype(BF)

    return call(
        body,
        count,
        (qk_t, value, third, third, qgrads, tokens, core, *moments, *outs),
        (1, 0, (DV, 0), (DV, 1), "pair1", "pair", "scalar") + ("late",) * 8,
        (
            (shape((qk, count // 2), BF),) * 2,
            shape((third.shape[0], DV), BF),
            shape((width, 2 * qk + FPAD + outs[0].shape[1]), BF),
        ),
        ("pair1", None, None),
        [pltpu.VMEM((2 * qk, width), F32), pltpu.VMEM((16, DV), F32)],
        2 * count * (heads * FPAD * DV + 2 * qk * width),
    )


def outputs_phase(core, attended, qgrads, kgrads, feats, sgrads, weights, w_out, heads):
    count, width = attended[0].shape[1], w_out.shape[1]
    rows, joined = heads * DV, 2 * heads * DK + heads * DV

    def body(at_first, at_last, core_ref, *refs):
        atts, qs, ks, fs, ss, ws = (refs[2 * i : 2 * i + 2] for i in range(6))
        out_ref, mixed_ref, gtok_ref, turned = refs[12:]
        at = core_ref[0, 0]

        @at_first
        def _():
            for c in range(2):
                for head in range(heads):
                    turned[c, head] = weighted_turned(ss[c], head)

        mixed, gtok = 0.0, 0.0
        for c in range(2):
            first = pl.multiple_of((at if c == 0 else 1 - at) * rows, rows)
            mixed = mixed + dot(atts[c][...], out_ref[pl.ds(first, rows), :], (0, 0))
            parts = [qs[c][...], ks[c][...]]
            for head in range(heads):
                feat = fs[c][head * FPAD : (head + 1) * FPAD, :]
                parts.append(dot(turned[c, head, :, :FPAD], feat, (1, 0)).astype(BF))
            gtok = gtok + dot(jnp.concatenate(parts, axis=0), ws[c][...], (0, 1))
        mixed_ref[...] = mixed.astype(BF)
        gtok_ref[...] = gtok.astype(BF)

    return call(
        body,
        count,
        (core, *attended, *qgrads, *kgrads, *feats, *sgrads, *weights, w_out),
        ("scalar",) + (1,) * 8 + (None,) * 2 + ((joined, 0),) * 2 + (None,),
        (shape((count, width), BF), shape((count, width), BF)),
        (0, 0),
        [pltpu.VMEM((2, heads, DV, SPAD), BF)],
        2 * count * 2 * (joined * width + rows * width + heads * FPAD * DV),
    )


def finish_phase(core, fourth, sgrads, after, heads, scale_factor):
    rows, qk = 8, heads * DK
    quarter = fourth.shape[1] - 2 * qk - FPAD

    def body(at_first, at_last, core_ref, recv_ref, mine_ref, other_ref, *refs):
        query_ref, key_ref, value_ref, out_ref, wgrad, moment, out = refs[-7:]

        at_first(lambda: clear(wgrad, moment, out))
        odd = at_first.block % 2
        wgrad[...] += add_chips(recv_ref.at[:, pl.ds(0, 2 * qk)], 2 * rows)
        parts = recv_ref.shape[0] // (2 * rows)
        for which in range(2):
            some = [p for p in range(parts) if p // 2 % 2 == which]
            moment[2 * odd + which] += sum(
                recv_ref[2 * rows * p : 2 * rows * (p + 1), 2 * qk : 2 * qk + FPAD].astype(F32) for p in some
            )
            some = [p for p in range(parts) if p % 2 == which]
            out[2 * which + 1 - odd] += sum(
                recv_ref[2 * rows * p : 2 * rows * (p + 1), 2 * qk + FPAD :].astype(F32) for p in some
            )
        @at_last
        def _():
            for x in range(4):
                out_ref[:, x * quarter : (x + 1) * quarter] = (out[x, :rows] + out[x, rows:]) * scale_factor
            first = core_ref[0, 0] == 0
            both = wgrad[...] * scale_factor
            query_ref[...] = jnp.concatenate([both[:rows, :qk], both[rows:, :qk]], axis=1)
            key_ref[...] = jnp.concatenate([both[:rows, qk:], both[rows:, qk:]], axis=1)
            weight = band_weight((1, FPAD), 1) * scale_factor
            found = [[], []]
            for head in range(heads):
                whole = moment[head] * weight
                high = whole.astype(BF)
                split = jnp.concatenate([high, (whole - high.astype(F32)).astype(BF)], axis=0)
                for which, ref in enumerate((mine_ref, other_ref)):
                    both = dot(split, ref[head * SPAD : head * SPAD + FPAD, :], (1, 0))
                    both = both[: 2 * rows] + both[2 * rows :]
                    low, up = both[:rows], both[rows:]
                    found[which].append(jnp.where(first, low, up) if which == 0 else jnp.where(first, up, low))
            mine, other = (jnp.concatenate(part, axis=1) for part in found)
            value_ref[:, : heads * DV] = jnp.where(first, mine, other)
            value_ref[:, heads * DV :] = jnp.where(first, other, mine)

    return call(
        body,
        fourth.shape[0],
        (core, fourth, *sgrads, *after),
        ("scalar", 0, "late", "late") + ("any",) * len(after),
        (
            shape((rows, 2 * qk), F32),
            shape((rows, 2 * qk), F32),
            shape((rows, 2 * heads * DV), F32),
            shape((rows, 4 * quarter), F32),
        ),
        (None,) * 4,
        [
            pltpu.VMEM((2 * rows, 2 * qk), F32),
            pltpu.VMEM((heads, 2 * rows, FPAD), F32),
            pltpu.VMEM((4, 2 * rows, quarter), F32),
        ],
        0,
        fourth.shape[0] // 4,
    )


def per_device(chips, tokens, w_query, w_key, w_value, w_out, cotangent):
    n = 2 * chips
    heads = H // 2
    own, width = tokens.shape
    qk = heads * DK
    core = lax.axis_index("seq") % 2
    core_at = core.astype(jnp.int32).reshape(1, 1)
    same_core = [[2 * p + c for p in range(chips)] for c in range(2)]
    swap = [(i, i ^ 1) for i in range(n)]
    scale_factor = (own * n) ** (-0.5)

    def exchange(x):
        return lax.ppermute(x, AXES, swap)

    def spread(x):
        return lax.all_to_all(x, AXES, 0, 0, axis_index_groups=same_core, tiled=True)

    def among_four(flips, parts):
        found = [parts[0]]
        for step in (1, 2, 3):
            moves = []
            for i in range(n):
                at = place(i)
                for bit in (0, 1):
                    at = flips[bit](*at) if step >> bit & 1 else at
                moves.append((i, device(*at)))
            found.append(lax.ppermute(parts[step], AXES, moves))
        return found

    yz = (lambda y, x, z, c: (y, x, z ^ 1, c), lambda y, x, z, c: (y ^ 1, x, z, c))
    xy = (lambda y, x, z, c: ((y + 2 * (y % 2) - 1) % 4, x, z, c), lambda y, x, z, c: (y, x ^ 1, z, c))

    def place(i):
        return (i // 32, 2 * (i // 16 % 2) + i // 2 % 2, i // 4 % 4, i % 2)

    def device(y, x, z, c):
        return (((y * 2 + x // 2) * 4 + z) * 2 + x % 2) * 2 + c

    def to_each(x):
        return x.reshape(chips, -1, x.shape[1])

    ctx, seq = lax.axis_index("ctx"), lax.axis_index("seq")
    in_yz, in_xy = (
        v.astype(jnp.int32).reshape(1, 1)
        for v in (2 * (ctx // 8 % 2) + ctx % 2, 2 * (seq // 2) + 1 - ctx // 8 % 2)
    )

    to_send = weights_phase(w_query, w_key, w_value, w_out, chips, heads)
    weights = lax.all_to_all(to_send.reshape(n, -1, to_send.shape[1]), AXES, 0, 0, tiled=True)
    weights = weights.reshape(-1, to_send.shape[1])
    tok = (tokens, exchange(tokens))
    cot = (cotangent, exchange(cotangent))
    other_weights = exchange(weights)

    qk_t, value, key_feat, key_feat_sent, sent = keys_phase(tok, weights, chips, heads)
    first = spread(to_each(sent)).reshape(sent.shape)
    key_feats = (key_feat, exchange(key_feat_sent))

    up_t, query_feat, w_out_whole = upstream_phase(core_at, qk_t, cot, weights, other_weights, heads)
    moments = among_four(yz, product_phase(in_yz, (key_feat, key_feat_sent), tok, up_t, heads))
    scales, norm, sent = query_phase(query_feat, up_t, first, chips, heads)
    second = spread(to_each(sent)).reshape(sent.shape)

    attended, attended_sent, dens, sent, *outs = attend_phase(
        in_xy, query_feat, scales, up_t, second, cot, chips, heads
    )
    third = spread(to_each(sent)).reshape(sent.shape)
    outs = among_four(xy, outs)
    attendeds = (attended, exchange(attended_sent))
    qgrad, qgrad_sent = query_back_phase(qk_t, scales, dens, up_t, second, norm, heads)
    qgrads = (qgrad, exchange(qgrad_sent))

    kgrad, kgrad_sent, sgrad, sent = key_phase(qk_t, value, third, (qgrad, qgrad_sent), tok, core_at, moments, outs, heads)
    fourth = lax.all_to_all(sent.reshape(n, -1, sent.shape[1]), AXES, 0, 0, tiled=True).reshape(sent.shape)
    kgrads, sgrads = (kgrad, exchange(kgrad_sent)), (sgrad, exchange(sgrad))
    mixed, grad_tokens = outputs_phase(
        core_at, attendeds, qgrads, kgrads, key_feats, sgrads, (weights, other_weights), w_out_whole, heads
    )
    grad_query, grad_key, grad_value, grad_out = finish_phase(
        core_at, fourth, sgrads, (grad_tokens, mixed), heads, scale_factor
    )
    return (mixed, grad_tokens, grad_query, grad_key, grad_value, grad_out)


def solution(mesh):
    chips = mesh.size // 2
    placed = P(AXES, None)
    return jax.shard_map(
        lambda *args: per_device(chips, *args),
        mesh=mesh,
        in_specs=(placed,) * 6,
        out_specs=(placed,) * 6,
        check_vma=False,
    )
```

```python
import jax
import jax.numpy as jnp
from jax import lax
from jax.experimental import pallas as pl
from jax.experimental.pallas import tpu as pltpu
from jax.sharding import PartitionSpec as P

H = 8
DK = 16
DV = 128
BANDS = DK // 2 + 1
FPAD = (BANDS + 2) * DK
SPAD = 256
AXES = ("ctx", "seq")
BLOCK = 512
VMEM = 60 * 2**20
BF = jnp.bfloat16
F32 = jnp.float32
SQUARE = (2.0 * DK) ** (-0.5)
LINEAR = DK ** (-0.25)


def dot(a, b, contract):
    return lax.dot_general(a, b, ((contract[:1], contract[1:]), ((), ())), preferred_element_type=F32)


def band_weight(shape, dim):
    row = lax.broadcasted_iota(jnp.int32, shape, dim)
    twice = (row >= DK) & (row < (BANDS - 1) * DK)
    return jnp.where(twice, 2.0, 1.0).astype(F32)


def shifted(u, d):
    return pltpu.roll(u, DK - d, 0) if d else u


def features(u):
    bands = [u * shifted(u, d) * SQUARE for d in range(BANDS)]
    first = lax.broadcasted_iota(jnp.int32, u.shape, 0) == 0
    return jnp.concatenate(bands + [u * LINEAR, jnp.where(first, 1.0, 0.0)], axis=0).astype(BF)


def features_back(u, fgrad):
    def band(d):
        return fgrad[d * DK : (d + 1) * DK]

    total = band(0) * u + band(BANDS - 1) * shifted(u, BANDS - 1)
    for d in range(1, BANDS - 1):
        total = total + band(d) * shifted(u, d) + shifted(band(d) * u, DK - d)
    return total * (2.0 * SQUARE) + band(BANDS) * LINEAR


def in_parts(row):
    high = row.astype(BF).astype(F32)
    rest = row - high
    mid = rest.astype(BF).astype(F32)
    at = lax.broadcasted_iota(jnp.int32, (16, row.shape[1]), 0)
    low = jnp.where(at == 2, rest - mid, 0.0)
    return jnp.where(at == 0, high, jnp.where(at == 1, mid, low)).astype(BF)


def rows_of(array, head, size):
    return array[head * size : (head + 1) * size]


def head_row(rows, head):
    first, second = rows[4 * head : 4 * head + 2, :], rows[4 * head + 2 : 4 * head + 4, :]
    both = first + second
    return jnp.concatenate([both[:1], both[1:]], axis=1)


def split_rows(per_head):
    found = []
    for row in per_head:
        high = row.astype(BF).astype(F32)
        for part in (high, row - high):
            found += [part[:, :128], part[:, 128:]]
    found += [jnp.zeros((1, 128), F32)] * (16 - len(found))
    return jnp.concatenate(found, axis=0).astype(BF)


def column(row):
    return jnp.broadcast_to(row, (8, row.shape[1])).T[:FPAD, :1]


def add_chips(ref, rows):
    total = ref[:rows, :].astype(F32)
    for at in range(rows, ref.shape[0], rows):
        total = total + ref[at : at + rows, :].astype(F32)
    return total


def lane_sums(x):
    return sum(x[:, i : i + 128] for i in range(0, x.shape[1], 128))


def weighted_turned(state_ref, head):
    whole = state_ref[head * SPAD : (head + 1) * SPAD, :].astype(F32)
    return (whole * band_weight((SPAD, DV), 0)).T.astype(BF)


def call(body, count, ins, kinds, outs, out_kinds, scratch, flops, size=BLOCK):
    block = min(size, count // 2 if "pair" in kinds or "pair1" in out_kinds else count)
    steps = count // block

    def pieces(x, kind):
        if kind in ("pair", "pair1"):
            half = steps // 2
            return pieces_of(0, half, x[0].shape, kind) + pieces_of(1, half, x[1].shape, kind)
        if kind in (0, 1):
            return pieces_of(0, steps, x.shape, kind)
        if kind == "late":
            return [(0, pl.ds(0, x.shape[0]), pl.ds(0, x.shape[1]))]
        if kind is not None and kind[0] == "from":
            return [(0, pl.ds(0, x.shape[0]), pl.ds(kind[1], x.shape[1] - kind[1]))]
        if kind is not None:
            return [(0, pl.ds(0, x.shape[0]), pl.ds(kind[0] * kind[1], kind[0]))]
        return [(0, pl.ds(0, x.shape[0]), pl.ds(0, x.shape[1]))]

    def pieces_of(which, number, dims, kind):
        if kind in (0, "pair"):
            return [(which, pl.ds(i * block, block), pl.ds(0, dims[1])) for i in range(number)]
        return [(which, pl.ds(0, dims[0]), pl.ds(i * block, block)) for i in range(number)]

    def members(x, kind):
        return list(x) if kind in ("pair", "pair1") else [x]

    plans = [[] if kind in ("scalar", "any") else pieces(x, kind) for x, kind in zip(ins, kinds)]
    out_plans = [pieces(x, kind) for x, kind in zip(outs, out_kinds)]
    buffers = [
        pltpu.VMEM((rows.size, cols.size), members(x, kind)[0].dtype)
        for x, kind, plan in zip(tuple(ins) + tuple(outs), tuple(kinds) + tuple(out_kinds), plans + out_plans)
        for _, rows, cols in plan
    ]

    def kernel(*refs):
        refs = list(refs)

        def take(number):
            found = refs[:number]
            del refs[:number]
            return found

        given = [take(len(members(x, kind))) for x, kind in zip(ins, kinds)]
        made = [take(len(members(x, kind))) for x, kind in zip(outs, out_kinds)]
        held, sent = [take(len(plan)) for plan in plans], [take(len(plan)) for plan in out_plans]
        arrived, left = take(2)
        own = refs

        reads, at = [[] for _ in range(steps)], 0
        for source, buffer, plan, kind in zip(given, held, plans, kinds):
            for i, (which, rows, cols) in enumerate(plan):
                reads[steps - 1 if kind == "late" else i].append(pltpu.make_async_copy(source[which].at[rows, cols], buffer[i], arrived.at[at]))
                at += 1
        writes, at = [], 0
        for target, buffer, plan in zip(made, sent, out_plans):
            writes.append([])
            for i, (which, rows, cols) in enumerate(plan):
                writes[-1].append(pltpu.make_async_copy(buffer[i], target[which].at[rows, cols], left.at[at]))
                at += 1
        for step in reads:
            for copy in step:
                copy.start()
        for i in range(steps):
            for copy in reads[i]:
                copy.wait()
            at_first = lambda fn, i=i: fn() if i == 0 else None
            at_first.block = i
            body(
                at_first,
                lambda fn, i=i: fn() if i == steps - 1 else None,
                *[buffer[min(i, len(buffer) - 1)] if buffer else source[0] for buffer, source in zip(held, given)],
                *[buffer[min(i, len(buffer) - 1)] for buffer in sent],
                *own,
            )
            for copies in writes:
                if len(copies) == steps:
                    copies[i].start()
                elif i == steps - 1:
                    copies[0].start()
        for copies in writes:
            for copy in copies:
                copy.wait()

    args = [y for x, kind in zip(ins, kinds) for y in members(x, kind)]
    results = [y for x, kind in zip(outs, out_kinds) for y in members(x, kind)]
    spaces = [pltpu.SMEM if kind == "scalar" else pl.ANY for x, kind in zip(ins, kinds) for _ in members(x, kind)]
    nbytes = sum(x.size * x.dtype.itemsize for x in args + results)
    return pl.pallas_call(
        kernel,
        in_specs=[pl.BlockSpec(memory_space=space) for space in spaces],
        out_specs=[pl.BlockSpec(memory_space=pl.ANY)] * len(results),
        out_shape=results,
        scratch_shapes=buffers
        + [
            pltpu.SemaphoreType.DMA((sum(len(plan) for plan in plans),)),
            pltpu.SemaphoreType.DMA((sum(len(plan) for plan in out_plans),)),
        ]
        + list(scratch),
        compiler_params=pltpu.CompilerParams(vmem_limit_bytes=VMEM),
        cost_estimate=pl.CostEstimate(flops=flops, bytes_accessed=nbytes, transcendentals=0),
    )(*args)


def shape(dims, dtype):
    return jax.ShapeDtypeStruct(dims, dtype)


def clear(*refs):
    for ref in refs:
        ref[...] = jnp.zeros(ref.shape, ref.dtype)


def weights_phase(w_query, w_key, w_value, w_out, chips, heads):
    qk, cols, half = heads * DK, heads * DV, w_out.shape[1] // 2

    def body(q_ref, k_ref, v_ref, o_ref, out_ref, pair_ref, sems):
        query, key, value, rest = (ref[...].astype(F32) for ref in (q_ref, k_ref, v_ref, o_ref))
        halves = [
            jnp.concatenate(
                [
                    query[:, c * qk : (c + 1) * qk],
                    key[:, c * qk : (c + 1) * qk],
                    value[:, c * cols : (c + 1) * cols],
                    rest[:, c * half : (c + 1) * half],
                ],
                axis=1,
            )
            for c in range(2)
        ]
        pair = jnp.concatenate(halves, axis=0).astype(BF)
        for p in range(chips // 8):
            pair_ref[2 * rows * p : 2 * rows * (p + 1), :] = pair
        part = pair_ref.shape[0]
        copies = [pltpu.make_async_copy(pair_ref, out_ref.at[pl.ds(part * k, part), :], sems.at[k]) for k in range(8)]
        for copy in copies:
            copy.start()
        for copy in copies:
            copy.wait()

    rows = w_query.shape[0]
    return pl.pallas_call(
        body,
        out_specs=pl.BlockSpec(memory_space=pl.ANY),
        out_shape=shape((2 * chips * rows, 2 * qk + cols + half), BF),
        scratch_shapes=[pltpu.VMEM((2 * rows * (chips // 8), 2 * qk + cols + half), BF), pltpu.SemaphoreType.DMA((8,))],
        compiler_params=pltpu.CompilerParams(vmem_limit_bytes=VMEM),
        cost_estimate=pl.CostEstimate(flops=0, bytes_accessed=2 * 2 * chips * rows * (2 * qk + cols + half), transcendentals=0),
    )(w_query, w_key, w_value, w_out)


def keys_phase(tokens, w_qkv, chips, heads):
    qk = heads * DK

    def body(at_first, at_last, slab_ref, w_ref, qk_ref, value_ref, feat_ref, sent_ref, state_acc, norm_acc):
        at_first(lambda: clear(state_acc, norm_acc))
        joined = dot(slab_ref[...], w_ref[...], (1, 0))
        qk_t = joined[:, : 2 * qk].T.astype(BF)
        value = joined[:, 2 * qk :].astype(BF)
        qk_ref[...] = qk_t
        value_ref[...] = value
        keys = qk_t.astype(F32)[qk:]
        found = []
        for head in range(heads):
            feat = features(rows_of(keys, head, DK))
            found.append(feat)
            state_acc[head, :FPAD, :] += dot(feat, value[:, head * DV : (head + 1) * DV], (1, 0))
            norm_acc[head, :FPAD, :] += lane_sums(feat.astype(F32))
        feat_ref[...] = jnp.concatenate(found, axis=0)

        @at_last
        def _():
            norm = split_rows([jnp.sum(norm_acc[head], axis=1)[None] for head in range(heads)])
            state = state_acc[...].reshape(heads * SPAD, DV).astype(BF)
            part = heads * SPAD // chips
            for p in range(chips):
                sent_ref[2 * part * p : 2 * part * p + part, :] = state[part * p : part * (p + 1)]
                sent_ref[2 * part * p + part : 2 * part * (p + 1), :] = norm

    count = 2 * tokens[0].shape[0]
    return call(
        body,
        count,
        (tokens, w_qkv),
        ("pair", (2 * qk + heads * DV, 0)),
        (
            shape((2 * qk, count), BF),
            shape((count, heads * DV), BF),
            (shape((heads * FPAD, count // 2), BF),) * 2,
            shape((2 * heads * SPAD, DV), BF),
        ),
        (1, 0, "pair1", None),
        [pltpu.VMEM((heads, SPAD, DV), F32), pltpu.VMEM((heads, SPAD, 128), F32)],
        2 * count * heads * (w_qkv.shape[0] * (2 * DK + DV) + FPAD * DV * 2),
    )


def upstream_phase(core, qk_t, cot, weights, other_weights, heads):
    count, width = qk_t.shape[1], cot[0].shape[1]
    rows, half = heads * DV, width // 2
    joined = 2 * heads * DK + heads * DV

    def body(at_first, at_last, core_ref, qk_ref, slab_ref, mine_ref, theirs_ref, up_ref, feat_ref, w_ref):
        at = core_ref[0, 0]

        @at_first
        def _():
            mine, theirs = mine_ref[...], theirs_ref[...]
            w_ref[:, :half] = jnp.where(at == 0, mine, theirs)
            w_ref[:, half:] = jnp.where(at == 0, theirs, mine)

        here = w_ref[pl.ds(pl.multiple_of(at * rows, rows), rows), :]
        up_ref[...] = dot(here, slab_ref[...], (1, 1)).astype(BF)
        query = qk_ref[...].astype(F32)
        for head in range(heads):
            feat_ref[head * FPAD : (head + 1) * FPAD, :] = features(rows_of(query, head, DK))

    return call(
        body,
        count,
        (core, qk_t, cot, weights, other_weights),
        ("scalar", 1, "pair", ("from", joined), ("from", joined)),
        (shape((rows, count), BF), shape((heads * FPAD, count), BF), shape((2 * rows, width), BF)),
        (1, 1, None),
        [],
        2 * count * rows * width,
    )


def product_phase(turn, rows_t, slabs, after, parts):
    rows, count = rows_t[0].shape[0], 2 * rows_t[0].shape[1]
    size = rows // parts
    width = slabs[0].shape[1]

    def body(at_first, at_last, turn_ref, rows_ref, slab_ref, after_ref, *refs):
        out_refs, acc = refs[:parts], refs[parts]
        at_first(lambda: clear(acc))
        acc[...] += dot(rows_ref[...], slab_ref[...], (1, 0))

        @at_last
        def _():
            for k in range(parts):
                part = turn_ref[0, 0] ^ k
                out_refs[k][...] = acc[pl.ds(pl.multiple_of(part * size, 16), size), :].astype(BF)

    return call(
        body,
        count,
        (turn, rows_t, slabs, after),
        ("scalar", "pair1", "pair", "any"),
        (shape((size, width), BF),) * parts,
        (None,) * parts,
        [pltpu.VMEM((rows, width), F32)],
        2 * count * rows * width,
    )


def query_phase(feats, up_t, first, chips, heads):
    count = up_t.shape[1]
    part = heads * SPAD // chips

    def body(at_first, at_last, feat_ref, up_ref, first_ref, scale_ref, norm_ref, sent_ref, acc, state_own):
        at_first(lambda: clear(acc))

        @at_first
        def _():
            total = add_chips(first_ref, 2 * part)
            state_own[...] = total[:part].astype(BF)
            norm_ref[...] = total[part:]

        at = lax.broadcasted_iota(jnp.int32, scale_ref.shape, 0)
        scales = jnp.zeros(scale_ref.shape, F32)
        for head in range(heads):
            feat = feat_ref[head * FPAD : (head + 1) * FPAD, :]
            parts = in_parts(head_row(norm_ref[...], head) * band_weight((1, SPAD), 1))[:, :FPAD]
            scale = 1.0 / jnp.sum(dot(parts, feat, (1, 0)), axis=0, keepdims=True)
            grad_num = (up_ref[head * DV : (head + 1) * DV, :].astype(F32) * scale).astype(BF)
            acc[head, :FPAD, :] += dot(feat, grad_num, (1, 1))
            scales = jnp.where(at == head, scale, scales)
        scale_ref[...] = scales

        @at_last
        def _():
            sent_ref[:, :DV] = acc[...].reshape(heads * SPAD, DV).astype(BF)
            for p in range(chips):
                sent_ref[p * part : (p + 1) * part, DV:] = state_own[...]

    return call(
        body,
        count,
        (feats, up_t, first),
        (1, 1, None),
        (shape((8, count), F32), shape((16, 128), F32), shape((heads * SPAD, 2 * DV), BF)),
        (1, None, None),
        [pltpu.VMEM((heads, SPAD, DV), F32), pltpu.VMEM((part, DV), BF)],
        2 * count * heads * FPAD * DV * 2,
    )


def attend_phase(turn, feats, scales, up_t, second, cot, chips, heads):
    count = up_t.shape[1]
    width = cot[0].shape[1]
    quarter = width // 4

    def body(
        at_first, at_last, turn_ref, feat_ref, scale_ref, up_ref, state_ref, sgrad_ref, slab_ref,
        att_ref, den_ref, sent_ref, out0, out1, out2, out3, turned, acc, out_acc,
    ):
        at_first(lambda: clear(acc, out_acc))

        @at_first
        def _():
            for head in range(heads):
                turned[head] = weighted_turned(state_ref, head)

        at = lax.broadcasted_iota(jnp.int32, den_ref.shape, 0)
        dens = jnp.zeros(den_ref.shape, F32)
        found = []
        for head in range(heads):
            feat = feat_ref[head * FPAD : (head + 1) * FPAD, :]
            scale = scale_ref[head : head + 1, :]
            att = dot(turned[head, :, :FPAD], feat, (1, 0)) * scale
            grad_num = up_ref[head * DV : (head + 1) * DV, :].astype(F32) * scale
            grad_den = -jnp.sum(grad_num * att, axis=0, keepdims=True)
            acc[head, :FPAD, :] += lane_sums(feat.astype(F32) * grad_den)
            found.append(att.astype(BF))
            dens = jnp.where(at == head, grad_den, dens)
        den_ref[...] = dens
        attended = jnp.concatenate(found, axis=0)
        att_ref[...] = attended
        out_acc[...] += dot(attended, slab_ref[...], (1, 0))

        @at_last
        def _():
            ngrad = split_rows([jnp.sum(acc[head], axis=1)[None] for head in range(heads)])
            sgrad_own = add_chips(sgrad_ref, ngrad.shape[0]).astype(BF)
            both = jnp.concatenate([sgrad_own, ngrad], axis=1)
            for p in range(chips):
                sent_ref[p * both.shape[0] : (p + 1) * both.shape[0], :] = both
            for k, out_ref in enumerate((out0, out1, out2, out3)):
                part = turn_ref[0, 0] ^ k
                out_ref[...] = out_acc[:, pl.ds(pl.multiple_of(part * quarter, 128), quarter)].astype(BF)

    return call(
        body,
        count,
        (turn, feats, scales, up_t, second, second, cot),
        ("scalar", 1, 1, 1, (DV, 1), (DV, 0), "pair"),
        (
            (shape((heads * DV, count // 2), BF),) * 2,
            shape((8, count), F32),
            shape(second.shape, BF),
        )
        + (shape((heads * DV, quarter), BF),) * 4,
        ("pair1", 1) + (None,) * 5,
        [
            pltpu.VMEM((heads, DV, SPAD), BF),
            pltpu.VMEM((heads, SPAD, 128), F32),
            pltpu.VMEM((heads * DV, width), F32),
        ],
        2 * count * (heads * FPAD * DV * 2 + heads * DV * width),
    )


def query_back_phase(qk_t, scales, dens, up_t, second, norm, heads):
    count = up_t.shape[1]

    def body(at_first, at_last, qk_ref, scale_ref, den_ref, up_ref, state_ref, norm_ref, qgrad_ref):
        query = qk_ref[...].astype(F32)
        found = []
        for head in range(heads):
            grad_num = (up_ref[head * DV : (head + 1) * DV, :].astype(F32) * scale_ref[head : head + 1, :]).astype(BF)
            fgrad = dot(state_ref[head * SPAD : head * SPAD + FPAD, :], grad_num, (1, 0))
            fgrad = fgrad + column(head_row(norm_ref[...], head)) * den_ref[head : head + 1, :]
            found.append(features_back(rows_of(query, head, DK), fgrad).astype(BF))
        qgrad_ref[...] = jnp.concatenate(found, axis=0)

    return call(
        body,
        count,
        (qk_t, scales, dens, up_t, second, norm),
        (1, 1, 1, 1, (DV, 1), None),
        ((shape((heads * DK, count // 2), BF),) * 2,),
        ("pair1",),
        [],
        2 * count * heads * FPAD * DV,
    )


def key_phase(qk_t, value, third, qgrads, tokens, core, moments, outs, heads):
    count, qk = value.shape[0], heads * DK
    width = tokens[0].shape[1]

    def body(
        at_first, at_last, qk_ref, value_ref, sgrad_ref, rows_ref, qgrad_ref, slab_ref, core_ref, m0, m1, m2, m3, o0, o1, o2, o3,
        kgrad_ref, copy_ref, sent_ref, acc, ngrad_ref,
    ):
        at_first(lambda: clear(acc))

        @at_first
        def _():
            ngrad_ref[...] = add_chips(rows_ref, 16)
            copy_ref[...] = sgrad_ref[...]

        keys = qk_ref[...].astype(F32)[qk:]
        found = []
        for head in range(heads):
            fgrad = dot(
                sgrad_ref[head * SPAD : head * SPAD + FPAD, :],
                value_ref[:, head * DV : (head + 1) * DV],
                (1, 1),
            )
            fgrad = fgrad + column(head_row(ngrad_ref[...], head))
            found.append(features_back(rows_of(keys, head, DK), fgrad))
        kgrad = jnp.concatenate(found, axis=0).astype(BF)
        kgrad_ref[...] = kgrad
        both = jnp.concatenate([qgrad_ref[...], kgrad], axis=0)
        acc[...] += dot(both, slab_ref[...], (1, 0))

        @at_last
        def _():
            sent_ref[:, : 2 * qk] = acc[...].T.astype(BF)
            sent_ref[:, 2 * qk : 2 * qk + FPAD] = sum(ref[...].astype(F32) for ref in (m0, m1, m2, m3)).T.astype(BF)
            first = core_ref[0, 0] == 0
            out = sum(ref[...].astype(F32) for ref in (o0, o1, o2, o3))
            half = out.shape[0]
            for j in range(2):
                sent_ref[j * half : (j + 1) * half, 2 * qk + FPAD :] = jnp.where(first == (j == 0), out, 0.0).astype(BF)

    return call(
        body,
        count,
        (qk_t, value, third, third, qgrads, tokens, core, *moments, *outs),
        (1, 0, (DV, 0), (DV, 1), "pair1", "pair", "scalar") + ("late",) * 8,
        (
            (shape((qk, count // 2), BF),) * 2,
            shape((third.shape[0], DV), BF),
            shape((width, 2 * qk + FPAD + outs[0].shape[1]), BF),
        ),
        ("pair1", None, None),
        [pltpu.VMEM((2 * qk, width), F32), pltpu.VMEM((16, DV), F32)],
        2 * count * (heads * FPAD * DV + 2 * qk * width),
    )


def outputs_phase(core, attended, qgrads, kgrads, feats, sgrads, weights, w_out, heads):
    count, width = attended[0].shape[1], w_out.shape[1]
    rows, joined = heads * DV, 2 * heads * DK + heads * DV

    def body(at_first, at_last, core_ref, *refs):
        atts, qs, ks, fs, ss, ws = (refs[2 * i : 2 * i + 2] for i in range(6))
        out_ref, mixed_ref, gtok_ref, turned = refs[12:]
        at = core_ref[0, 0]

        @at_first
        def _():
            for c in range(2):
                for head in range(heads):
                    turned[c, head] = weighted_turned(ss[c], head)

        mixed, gtok = 0.0, 0.0
        for c in range(2):
            first = pl.multiple_of((at if c == 0 else 1 - at) * rows, rows)
            mixed = mixed + dot(atts[c][...], out_ref[pl.ds(first, rows), :], (0, 0))
            parts = [qs[c][...], ks[c][...]]
            for head in range(heads):
                feat = fs[c][head * FPAD : (head + 1) * FPAD, :]
                parts.append(dot(turned[c, head, :, :FPAD], feat, (1, 0)).astype(BF))
            gtok = gtok + dot(jnp.concatenate(parts, axis=0), ws[c][...], (0, 1))
        mixed_ref[...] = mixed.astype(BF)
        gtok_ref[...] = gtok.astype(BF)

    return call(
        body,
        count,
        (core, *attended, *qgrads, *kgrads, *feats, *sgrads, *weights, w_out),
        ("scalar",) + (1,) * 8 + (None,) * 2 + ((joined, 0),) * 2 + (None,),
        (shape((count, width), BF), shape((count, width), BF)),
        (0, 0),
        [pltpu.VMEM((2, heads, DV, SPAD), BF)],
        2 * count * 2 * (joined * width + rows * width + heads * FPAD * DV),
    )


def finish_phase(core, fourth, sgrads, after, heads, scale_factor):
    rows, qk = 8, heads * DK
    quarter = fourth.shape[1] - 2 * qk - FPAD

    def body(at_first, at_last, core_ref, recv_ref, mine_ref, other_ref, *refs):
        query_ref, key_ref, value_ref, out_ref, wgrad, moment, out = refs[-7:]

        at_first(lambda: clear(wgrad, moment, out))
        odd = at_first.block % 2
        wgrad[...] += add_chips(recv_ref.at[:, pl.ds(0, 2 * qk)], 2 * rows)
        parts = recv_ref.shape[0] // (2 * rows)
        for which in range(2):
            some = [p for p in range(parts) if p // 2 % 2 == which]
            moment[2 * odd + which] += sum(
                recv_ref[2 * rows * p : 2 * rows * (p + 1), 2 * qk : 2 * qk + FPAD].astype(F32) for p in some
            )
            some = [p for p in range(parts) if p % 2 == which]
            out[2 * which + 1 - odd] += sum(
                recv_ref[2 * rows * p : 2 * rows * (p + 1), 2 * qk + FPAD :].astype(F32) for p in some
            )
        @at_last
        def _():
            for x in range(4):
                out_ref[:, x * quarter : (x + 1) * quarter] = (out[x, :rows] + out[x, rows:]) * scale_factor
            first = core_ref[0, 0] == 0
            both = wgrad[...] * scale_factor
            query_ref[...] = jnp.concatenate([both[:rows, :qk], both[rows:, :qk]], axis=1)
            key_ref[...] = jnp.concatenate([both[:rows, qk:], both[rows:, qk:]], axis=1)
            weight = band_weight((1, FPAD), 1) * scale_factor
            found = [[], []]
            for head in range(heads):
                whole = moment[head] * weight
                high = whole.astype(BF)
                split = jnp.concatenate([high, (whole - high.astype(F32)).astype(BF)], axis=0)
                for which, ref in enumerate((mine_ref, other_ref)):
                    both = dot(split, ref[head * SPAD : head * SPAD + FPAD, :], (1, 0))
                    both = both[: 2 * rows] + both[2 * rows :]
                    low, up = both[:rows], both[rows:]
                    found[which].append(jnp.where(first, low, up) if which == 0 else jnp.where(first, up, low))
            mine, other = (jnp.concatenate(part, axis=1) for part in found)
            value_ref[:, : heads * DV] = jnp.where(first, mine, other)
            value_ref[:, heads * DV :] = jnp.where(first, other, mine)

    return call(
        body,
        fourth.shape[0],
        (core, fourth, *sgrads, *after),
        ("scalar", 0, "late", "late") + ("any",) * len(after),
        (
            shape((rows, 2 * qk), F32),
            shape((rows, 2 * qk), F32),
            shape((rows, 2 * heads * DV), F32),
            shape((rows, 4 * quarter), F32),
        ),
        (None,) * 4,
        [
            pltpu.VMEM((2 * rows, 2 * qk), F32),
            pltpu.VMEM((heads, 2 * rows, FPAD), F32),
            pltpu.VMEM((4, 2 * rows, quarter), F32),
        ],
        0,
        fourth.shape[0] // 4,
    )


def per_device(chips, tokens, w_query, w_key, w_value, w_out, cotangent):
    n = 2 * chips
    heads = H // 2
    own, width = tokens.shape
    qk = heads * DK
    core = lax.axis_index("seq") % 2
    core_at = core.astype(jnp.int32).reshape(1, 1)
    same_core = [[2 * p + c for p in range(chips)] for c in range(2)]
    swap = [(i, i ^ 1) for i in range(n)]
    scale_factor = (own * n) ** (-0.5)

    def exchange(x):
        return lax.ppermute(x, AXES, swap)

    def spread(x):
        return lax.all_to_all(x, AXES, 0, 0, axis_index_groups=same_core, tiled=True)

    def among_four(flips, parts):
        found = [parts[0]]
        for step in (1, 2, 3):
            moves = []
            for i in range(n):
                at = place(i)
                for bit in (0, 1):
                    at = flips[bit](*at) if step >> bit & 1 else at
                moves.append((i, device(*at)))
            found.append(lax.ppermute(parts[step], AXES, moves))
        return found

    yz = (lambda y, x, z, c: (y, x, z ^ 1, c), lambda y, x, z, c: (y ^ 1, x, z, c))
    xy = (lambda y, x, z, c: ((y + 2 * (y % 2) - 1) % 4, x, z, c), lambda y, x, z, c: (y, x ^ 1, z, c))

    def place(i):
        return (i // 32, 2 * (i // 16 % 2) + i // 2 % 2, i // 4 % 4, i % 2)

    def device(y, x, z, c):
        return (((y * 2 + x // 2) * 4 + z) * 2 + x % 2) * 2 + c

    def to_each(x):
        return x.reshape(chips, -1, x.shape[1])

    ctx, seq = lax.axis_index("ctx"), lax.axis_index("seq")
    in_yz, in_xy = (
        v.astype(jnp.int32).reshape(1, 1)
        for v in (2 * (ctx // 8 % 2) + ctx % 2, 2 * (seq // 2) + 1 - ctx // 8 % 2)
    )

    to_send = weights_phase(w_query, w_key, w_value, w_out, chips, heads)
    weights = lax.all_to_all(to_send.reshape(n, -1, to_send.shape[1]), AXES, 0, 0, tiled=True)
    weights = weights.reshape(-1, to_send.shape[1])
    tok = (tokens, exchange(tokens))
    cot = (cotangent, exchange(cotangent))
    other_weights = exchange(weights)

    qk_t, value, key_feat, key_feat_sent, sent = keys_phase(tok, weights, chips, heads)
    first = spread(to_each(sent)).reshape(sent.shape)
    key_feats = (key_feat, exchange(key_feat_sent))

    up_t, query_feat, w_out_whole = upstream_phase(core_at, qk_t, cot, weights, other_weights, heads)
    moments = among_four(yz, product_phase(in_yz, (key_feat, key_feat_sent), tok, up_t, heads))
    scales, norm, sent = query_phase(query_feat, up_t, first, chips, heads)
    second = spread(to_each(sent)).reshape(sent.shape)

    attended, attended_sent, dens, sent, *outs = attend_phase(
        in_xy, query_feat, scales, up_t, second, cot, chips, heads
    )
    third = spread(to_each(sent)).reshape(sent.shape)
    outs = among_four(xy, outs)
    attendeds = (attended, exchange(attended_sent))
    qgrad, qgrad_sent = query_back_phase(qk_t, scales, dens, up_t, second, norm, heads)
    qgrads = (qgrad, exchange(qgrad_sent))

    kgrad, kgrad_sent, sgrad, sent = key_phase(qk_t, value, third, (qgrad, qgrad_sent), tok, core_at, moments, outs, heads)
    fourth = lax.all_to_all(sent.reshape(n, -1, sent.shape[1]), AXES, 0, 0, tiled=True).reshape(sent.shape)
    kgrads, sgrads = (kgrad, exchange(kgrad_sent)), (sgrad, exchange(sgrad))
    mixed, grad_tokens = outputs_phase(
        core_at, attendeds, qgrads, kgrads, key_feats, sgrads, (weights, other_weights), w_out_whole, heads
    )
    grad_query, grad_key, grad_value, grad_out = finish_phase(
        core_at, fourth, sgrads, (grad_tokens, mixed), heads, scale_factor
    )
    return (mixed, grad_tokens, grad_query, grad_key, grad_value, grad_out)


def solution(mesh):
    chips = mesh.size // 2
    placed = P(AXES, None)
    return jax.shard_map(
        lambda *args: per_device(chips, *args),
        mesh=mesh,
        in_specs=(placed,) * 6,
        out_specs=(placed,) * 6,
        check_vma=False,
    )
```

```python
import jax
import jax.numpy as jnp
from jax import lax
from jax.experimental import pallas as pl
from jax.experimental.pallas import tpu as pltpu
from jax.sharding import PartitionSpec as P

H = 8
DK = 16
DV = 128
BANDS = DK // 2 + 1
FPAD = (BANDS + 2) * DK
SPAD = 256
AXES = ("ctx", "seq")
BLOCK = 512
VMEM = 60 * 2**20
BF = jnp.bfloat16
F32 = jnp.float32
SQUARE = (2.0 * DK) ** (-0.5)
LINEAR = DK ** (-0.25)


def dot(a, b, contract):
    return lax.dot_general(a, b, ((contract[:1], contract[1:]), ((), ())), preferred_element_type=F32)


def band_weight(shape, dim):
    row = lax.broadcasted_iota(jnp.int32, shape, dim)
    twice = (row >= DK) & (row < (BANDS - 1) * DK)
    return jnp.where(twice, 2.0, 1.0).astype(F32)


def shifted(u, d):
    return pltpu.roll(u, DK - d, 0) if d else u


def features(u):
    bands = [u * shifted(u, d) * SQUARE for d in range(BANDS)]
    first = lax.broadcasted_iota(jnp.int32, u.shape, 0) == 0
    return jnp.concatenate(bands + [u * LINEAR, jnp.where(first, 1.0, 0.0)], axis=0).astype(BF)


def features_back(u, fgrad):
    def band(d):
        return fgrad[d * DK : (d + 1) * DK]

    total = band(0) * u + band(BANDS - 1) * shifted(u, BANDS - 1)
    for d in range(1, BANDS - 1):
        total = total + band(d) * shifted(u, d) + shifted(band(d) * u, DK - d)
    return total * (2.0 * SQUARE) + band(BANDS) * LINEAR


def in_parts(row):
    high = row.astype(BF).astype(F32)
    rest = row - high
    mid = rest.astype(BF).astype(F32)
    at = lax.broadcasted_iota(jnp.int32, (16, row.shape[1]), 0)
    low = jnp.where(at == 2, rest - mid, 0.0)
    return jnp.where(at == 0, high, jnp.where(at == 1, mid, low)).astype(BF)


def rows_of(array, head, size):
    return array[head * size : (head + 1) * size]


def head_row(rows, head):
    first, second = rows[4 * head : 4 * head + 2, :], rows[4 * head + 2 : 4 * head + 4, :]
    both = first + second
    return jnp.concatenate([both[:1], both[1:]], axis=1)


def split_rows(per_head):
    found = []
    for row in per_head:
        high = row.astype(BF).astype(F32)
        for part in (high, row - high):
            found += [part[:, :128], part[:, 128:]]
    found += [jnp.zeros((1, 128), F32)] * (16 - len(found))
    return jnp.concatenate(found, axis=0).astype(BF)


def column(row):
    return jnp.broadcast_to(row, (8, row.shape[1])).T[:FPAD, :1]


def add_chips(ref, rows):
    total = ref[:rows, :].astype(F32)
    for at in range(rows, ref.shape[0], rows):
        total = total + ref[at : at + rows, :].astype(F32)
    return total


def lane_sums(x):
    return sum(x[:, i : i + 128] for i in range(0, x.shape[1], 128))


def weighted_turned(state_ref, head):
    whole = state_ref[head * SPAD : (head + 1) * SPAD, :].astype(F32)
    return (whole * band_weight((SPAD, DV), 0)).T.astype(BF)


def call(body, count, ins, kinds, outs, out_kinds, scratch, flops, size=BLOCK):
    block = min(size, count // 2 if "pair" in kinds or "pair1" in out_kinds else count)
    steps = count // block

    def pieces(x, kind):
        if kind in ("pair", "pair1"):
            half = steps // 2
            return pieces_of(0, half, x[0].shape, kind) + pieces_of(1, half, x[1].shape, kind)
        if kind in (0, 1):
            return pieces_of(0, steps, x.shape, kind)
        if kind == "late":
            return [(0, pl.ds(0, x.shape[0]), pl.ds(0, x.shape[1]))]
        if kind is not None and kind[0] == "from":
            return [(0, pl.ds(0, x.shape[0]), pl.ds(kind[1], x.shape[1] - kind[1]))]
        if kind is not None:
            return [(0, pl.ds(0, x.shape[0]), pl.ds(kind[0] * kind[1], kind[0]))]
        return [(0, pl.ds(0, x.shape[0]), pl.ds(0, x.shape[1]))]

    def pieces_of(which, number, dims, kind):
        if kind in (0, "pair"):
            return [(which, pl.ds(i * block, block), pl.ds(0, dims[1])) for i in range(number)]
        return [(which, pl.ds(0, dims[0]), pl.ds(i * block, block)) for i in range(number)]

    def members(x, kind):
        return list(x) if kind in ("pair", "pair1") else [x]

    plans = [[] if kind in ("scalar", "any") else pieces(x, kind) for x, kind in zip(ins, kinds)]
    out_plans = [pieces(x, kind) for x, kind in zip(outs, out_kinds)]
    buffers = [
        pltpu.VMEM((rows.size, cols.size), members(x, kind)[0].dtype)
        for x, kind, plan in zip(tuple(ins) + tuple(outs), tuple(kinds) + tuple(out_kinds), plans + out_plans)
        for _, rows, cols in plan
    ]

    def kernel(*refs):
        refs = list(refs)

        def take(number):
            found = refs[:number]
            del refs[:number]
            return found

        given = [take(len(members(x, kind))) for x, kind in zip(ins, kinds)]
        made = [take(len(members(x, kind))) for x, kind in zip(outs, out_kinds)]
        held, sent = [take(len(plan)) for plan in plans], [take(len(plan)) for plan in out_plans]
        arrived, left = take(2)
        own = refs

        reads, at = [[] for _ in range(steps)], 0
        for source, buffer, plan, kind in zip(given, held, plans, kinds):
            for i, (which, rows, cols) in enumerate(plan):
                reads[steps - 1 if kind == "late" else i].append(pltpu.make_async_copy(source[which].at[rows, cols], buffer[i], arrived.at[at]))
                at += 1
        writes, at = [], 0
        for target, buffer, plan in zip(made, sent, out_plans):
            writes.append([])
            for i, (which, rows, cols) in enumerate(plan):
                writes[-1].append(pltpu.make_async_copy(buffer[i], target[which].at[rows, cols], left.at[at]))
                at += 1
        for step in reads[:2]:
            for copy in step:
                copy.start()
        for i in range(steps):
            for copy in reads[i]:
                copy.wait()
            for copy in reads[i + 2] if i + 2 < steps else []:
                copy.start()
            at_first = lambda fn, i=i: fn() if i == 0 else None
            at_first.block = i
            body(
                at_first,
                lambda fn, i=i: fn() if i == steps - 1 else None,
                *[buffer[min(i, len(buffer) - 1)] if buffer else source[0] for buffer, source in zip(held, given)],
                *[buffer[min(i, len(buffer) - 1)] for buffer in sent],
                *own,
            )
            for copies in writes:
                if len(copies) == steps:
                    copies[i].start()
                elif i == steps - 1:
                    copies[0].start()
        for copies in writes:
            for copy in copies:
                copy.wait()

    args = [y for x, kind in zip(ins, kinds) for y in members(x, kind)]
    results = [y for x, kind in zip(outs, out_kinds) for y in members(x, kind)]
    spaces = [pltpu.SMEM if kind == "scalar" else pl.ANY for x, kind in zip(ins, kinds) for _ in members(x, kind)]
    nbytes = sum(x.size * x.dtype.itemsize for x in args + results)
    return pl.pallas_call(
        kernel,
        in_specs=[pl.BlockSpec(memory_space=space) for space in spaces],
        out_specs=[pl.BlockSpec(memory_space=pl.ANY)] * len(results),
        out_shape=results,
        scratch_shapes=buffers
        + [
            pltpu.SemaphoreType.DMA((sum(len(plan) for plan in plans),)),
            pltpu.SemaphoreType.DMA((sum(len(plan) for plan in out_plans),)),
        ]
        + list(scratch),
        compiler_params=pltpu.CompilerParams(vmem_limit_bytes=VMEM),
        cost_estimate=pl.CostEstimate(flops=flops, bytes_accessed=nbytes, transcendentals=0),
    )(*args)


def shape(dims, dtype):
    return jax.ShapeDtypeStruct(dims, dtype)


def clear(*refs):
    for ref in refs:
        ref[...] = jnp.zeros(ref.shape, ref.dtype)


def weights_phase(w_query, w_key, w_value, w_out, chips, heads):
    qk, cols, half = heads * DK, heads * DV, w_out.shape[1] // 2

    def body(q_ref, k_ref, v_ref, o_ref, out_ref, pair_ref, sems):
        query, key, value, rest = (ref[...].astype(F32) for ref in (q_ref, k_ref, v_ref, o_ref))
        halves = [
            jnp.concatenate(
                [
                    query[:, c * qk : (c + 1) * qk],
                    key[:, c * qk : (c + 1) * qk],
                    value[:, c * cols : (c + 1) * cols],
                    rest[:, c * half : (c + 1) * half],
                ],
                axis=1,
            )
            for c in range(2)
        ]
        pair = jnp.concatenate(halves, axis=0).astype(BF)
        for p in range(chips // 8):
            pair_ref[2 * rows * p : 2 * rows * (p + 1), :] = pair
        part = pair_ref.shape[0]
        copies = [pltpu.make_async_copy(pair_ref, out_ref.at[pl.ds(part * k, part), :], sems.at[k]) for k in range(8)]
        for copy in copies:
            copy.start()
        for copy in copies:
            copy.wait()

    rows = w_query.shape[0]
    return pl.pallas_call(
        body,
        out_specs=pl.BlockSpec(memory_space=pl.ANY),
        out_shape=shape((2 * chips * rows, 2 * qk + cols + half), BF),
        scratch_shapes=[pltpu.VMEM((2 * rows * (chips // 8), 2 * qk + cols + half), BF), pltpu.SemaphoreType.DMA((8,))],
        compiler_params=pltpu.CompilerParams(vmem_limit_bytes=VMEM),
        cost_estimate=pl.CostEstimate(flops=0, bytes_accessed=2 * 2 * chips * rows * (2 * qk + cols + half), transcendentals=0),
    )(w_query, w_key, w_value, w_out)


def keys_phase(tokens, w_qkv, chips, heads):
    qk = heads * DK

    def body(at_first, at_last, slab_ref, w_ref, qk_ref, value_ref, feat_ref, sent_ref, state_acc, norm_acc):
        at_first(lambda: clear(state_acc, norm_acc))
        joined = dot(slab_ref[...], w_ref[...], (1, 0))
        qk_t = joined[:, : 2 * qk].T.astype(BF)
        value = joined[:, 2 * qk :].astype(BF)
        qk_ref[...] = qk_t
        value_ref[...] = value
        keys = qk_t.astype(F32)[qk:]
        found = []
        for head in range(heads):
            feat = features(rows_of(keys, head, DK))
            found.append(feat)
            state_acc[head, :FPAD, :] += dot(feat, value[:, head * DV : (head + 1) * DV], (1, 0))
            norm_acc[head, :FPAD, :] += lane_sums(feat.astype(F32))
        feat_ref[...] = jnp.concatenate(found, axis=0)

        @at_last
        def _():
            norm = split_rows([jnp.sum(norm_acc[head], axis=1)[None] for head in range(heads)])
            state = state_acc[...].reshape(heads * SPAD, DV).astype(BF)
            part = heads * SPAD // chips
            for p in range(chips):
                sent_ref[2 * part * p : 2 * part * p + part, :] = state[part * p : part * (p + 1)]
                sent_ref[2 * part * p + part : 2 * part * (p + 1), :] = norm

    count = 2 * tokens[0].shape[0]
    return call(
        body,
        count,
        (tokens, w_qkv),
        ("pair", (2 * qk + heads * DV, 0)),
        (
            shape((2 * qk, count), BF),
            shape((count, heads * DV), BF),
            (shape((heads * FPAD, count // 2), BF),) * 2,
            shape((2 * heads * SPAD, DV), BF),
        ),
        (1, 0, "pair1", None),
        [pltpu.VMEM((heads, SPAD, DV), F32), pltpu.VMEM((heads, SPAD, 128), F32)],
        2 * count * heads * (w_qkv.shape[0] * (2 * DK + DV) + FPAD * DV * 2),
    )


def upstream_phase(core, qk_t, cot, weights, other_weights, heads):
    count, width = qk_t.shape[1], cot[0].shape[1]
    rows, half = heads * DV, width // 2
    joined = 2 * heads * DK + heads * DV

    def body(at_first, at_last, core_ref, qk_ref, slab_ref, mine_ref, theirs_ref, up_ref, feat_ref, w_ref):
        at = core_ref[0, 0]

        @at_first
        def _():
            mine, theirs = mine_ref[...], theirs_ref[...]
            w_ref[:, :half] = jnp.where(at == 0, mine, theirs)
            w_ref[:, half:] = jnp.where(at == 0, theirs, mine)

        here = w_ref[pl.ds(pl.multiple_of(at * rows, rows), rows), :]
        up_ref[...] = dot(here, slab_ref[...], (1, 1)).astype(BF)
        query = qk_ref[...].astype(F32)
        for head in range(heads):
            feat_ref[head * FPAD : (head + 1) * FPAD, :] = features(rows_of(query, head, DK))

    return call(
        body,
        count,
        (core, qk_t, cot, weights, other_weights),
        ("scalar", 1, "pair", ("from", joined), ("from", joined)),
        (shape((rows, count), BF), shape((heads * FPAD, count), BF), shape((2 * rows, width), BF)),
        (1, 1, None),
        [],
        2 * count * rows * width,
    )


def product_phase(turn, rows_t, slabs, after, parts):
    rows, count = rows_t[0].shape[0], 2 * rows_t[0].shape[1]
    size = rows // parts
    width = slabs[0].shape[1]

    def body(at_first, at_last, turn_ref, rows_ref, slab_ref, after_ref, *refs):
        out_refs, acc = refs[:parts], refs[parts]
        at_first(lambda: clear(acc))
        acc[...] += dot(rows_ref[...], slab_ref[...], (1, 0))

        @at_last
        def _():
            for k in range(parts):
                part = turn_ref[0, 0] ^ k
                out_refs[k][...] = acc[pl.ds(pl.multiple_of(part * size, 16), size), :].astype(BF)

    return call(
        body,
        count,
        (turn, rows_t, slabs, after),
        ("scalar", "pair1", "pair", "any"),
        (shape((size, width), BF),) * parts,
        (None,) * parts,
        [pltpu.VMEM((rows, width), F32)],
        2 * count * rows * width,
    )


def query_phase(feats, up_t, first, chips, heads):
    count = up_t.shape[1]
    part = heads * SPAD // chips

    def body(at_first, at_last, feat_ref, up_ref, first_ref, scale_ref, norm_ref, sent_ref, acc, state_own):
        at_first(lambda: clear(acc))

        @at_first
        def _():
            total = add_chips(first_ref, 2 * part)
            state_own[...] = total[:part].astype(BF)
            norm_ref[...] = total[part:]

        at = lax.broadcasted_iota(jnp.int32, scale_ref.shape, 0)
        scales = jnp.zeros(scale_ref.shape, F32)
        for head in range(heads):
            feat = feat_ref[head * FPAD : (head + 1) * FPAD, :]
            parts = in_parts(head_row(norm_ref[...], head) * band_weight((1, SPAD), 1))[:, :FPAD]
            scale = 1.0 / jnp.sum(dot(parts, feat, (1, 0)), axis=0, keepdims=True)
            grad_num = (up_ref[head * DV : (head + 1) * DV, :].astype(F32) * scale).astype(BF)
            acc[head, :FPAD, :] += dot(feat, grad_num, (1, 1))
            scales = jnp.where(at == head, scale, scales)
        scale_ref[...] = scales

        @at_last
        def _():
            sent_ref[:, :DV] = acc[...].reshape(heads * SPAD, DV).astype(BF)
            for p in range(chips):
                sent_ref[p * part : (p + 1) * part, DV:] = state_own[...]

    return call(
        body,
        count,
        (feats, up_t, first),
        (1, 1, None),
        (shape((8, count), F32), shape((16, 128), F32), shape((heads * SPAD, 2 * DV), BF)),
        (1, None, None),
        [pltpu.VMEM((heads, SPAD, DV), F32), pltpu.VMEM((part, DV), BF)],
        2 * count * heads * FPAD * DV * 2,
    )


def attend_phase(turn, feats, scales, up_t, second, cot, chips, heads):
    count = up_t.shape[1]
    width = cot[0].shape[1]
    quarter = width // 4

    def body(
        at_first, at_last, turn_ref, feat_ref, scale_ref, up_ref, state_ref, sgrad_ref, slab_ref,
        att_ref, den_ref, sent_ref, out0, out1, out2, out3, turned, acc, out_acc,
    ):
        at_first(lambda: clear(acc, out_acc))

        @at_first
        def _():
            for head in range(heads):
                turned[head] = weighted_turned(state_ref, head)

        at = lax.broadcasted_iota(jnp.int32, den_ref.shape, 0)
        dens = jnp.zeros(den_ref.shape, F32)
        found = []
        for head in range(heads):
            feat = feat_ref[head * FPAD : (head + 1) * FPAD, :]
            scale = scale_ref[head : head + 1, :]
            att = dot(turned[head, :, :FPAD], feat, (1, 0)) * scale
            grad_num = up_ref[head * DV : (head + 1) * DV, :].astype(F32) * scale
            grad_den = -jnp.sum(grad_num * att, axis=0, keepdims=True)
            acc[head, :FPAD, :] += lane_sums(feat.astype(F32) * grad_den)
            found.append(att.astype(BF))
            dens = jnp.where(at == head, grad_den, dens)
        den_ref[...] = dens
        attended = jnp.concatenate(found, axis=0)
        att_ref[...] = attended
        out_acc[...] += dot(attended, slab_ref[...], (1, 0))

        @at_last
        def _():
            ngrad = split_rows([jnp.sum(acc[head], axis=1)[None] for head in range(heads)])
            sgrad_own = add_chips(sgrad_ref, ngrad.shape[0]).astype(BF)
            both = jnp.concatenate([sgrad_own, ngrad], axis=1)
            for p in range(chips):
                sent_ref[p * both.shape[0] : (p + 1) * both.shape[0], :] = both
            for k, out_ref in enumerate((out0, out1, out2, out3)):
                part = turn_ref[0, 0] ^ k
                out_ref[...] = out_acc[:, pl.ds(pl.multiple_of(part * quarter, 128), quarter)].astype(BF)

    return call(
        body,
        count,
        (turn, feats, scales, up_t, second, second, cot),
        ("scalar", 1, 1, 1, (DV, 1), (DV, 0), "pair"),
        (
            (shape((heads * DV, count // 2), BF),) * 2,
            shape((8, count), F32),
            shape(second.shape, BF),
        )
        + (shape((heads * DV, quarter), BF),) * 4,
        ("pair1", 1) + (None,) * 5,
        [
            pltpu.VMEM((heads, DV, SPAD), BF),
            pltpu.VMEM((heads, SPAD, 128), F32),
            pltpu.VMEM((heads * DV, width), F32),
        ],
        2 * count * (heads * FPAD * DV * 2 + heads * DV * width),
    )


def query_back_phase(qk_t, scales, dens, up_t, second, norm, heads):
    count = up_t.shape[1]

    def body(at_first, at_last, qk_ref, scale_ref, den_ref, up_ref, state_ref, norm_ref, qgrad_ref):
        query = qk_ref[...].astype(F32)
        found = []
        for head in range(heads):
            grad_num = (up_ref[head * DV : (head + 1) * DV, :].astype(F32) * scale_ref[head : head + 1, :]).astype(BF)
            fgrad = dot(state_ref[head * SPAD : head * SPAD + FPAD, :], grad_num, (1, 0))
            fgrad = fgrad + column(head_row(norm_ref[...], head)) * den_ref[head : head + 1, :]
            found.append(features_back(rows_of(query, head, DK), fgrad).astype(BF))
        qgrad_ref[...] = jnp.concatenate(found, axis=0)

    return call(
        body,
        count,
        (qk_t, scales, dens, up_t, second, norm),
        (1, 1, 1, 1, (DV, 1), None),
        ((shape((heads * DK, count // 2), BF),) * 2,),
        ("pair1",),
        [],
        2 * count * heads * FPAD * DV,
    )


def key_phase(qk_t, value, third, qgrads, tokens, core, moments, outs, heads):
    count, qk = value.shape[0], heads * DK
    width = tokens[0].shape[1]

    def body(
        at_first, at_last, qk_ref, value_ref, sgrad_ref, rows_ref, qgrad_ref, slab_ref, core_ref, m0, m1, m2, m3, o0, o1, o2, o3,
        kgrad_ref, copy_ref, sent_ref, acc, ngrad_ref,
    ):
        at_first(lambda: clear(acc))

        @at_first
        def _():
            ngrad_ref[...] = add_chips(rows_ref, 16)
            copy_ref[...] = sgrad_ref[...]

        keys = qk_ref[...].astype(F32)[qk:]
        found = []
        for head in range(heads):
            fgrad = dot(
                sgrad_ref[head * SPAD : head * SPAD + FPAD, :],
                value_ref[:, head * DV : (head + 1) * DV],
                (1, 1),
            )
            fgrad = fgrad + column(head_row(ngrad_ref[...], head))
            found.append(features_back(rows_of(keys, head, DK), fgrad))
        kgrad = jnp.concatenate(found, axis=0).astype(BF)
        kgrad_ref[...] = kgrad
        both = jnp.concatenate([qgrad_ref[...], kgrad], axis=0)
        acc[...] += dot(both, slab_ref[...], (1, 0))

        @at_last
        def _():
            sent_ref[:, : 2 * qk] = acc[...].T.astype(BF)
            sent_ref[:, 2 * qk : 2 * qk + FPAD] = sum(ref[...].astype(F32) for ref in (m0, m1, m2, m3)).T.astype(BF)
            first = core_ref[0, 0] == 0
            out = sum(ref[...].astype(F32) for ref in (o0, o1, o2, o3))
            half = out.shape[0]
            for j in range(2):
                sent_ref[j * half : (j + 1) * half, 2 * qk + FPAD :] = jnp.where(first == (j == 0), out, 0.0).astype(BF)

    return call(
        body,
        count,
        (qk_t, value, third, third, qgrads, tokens, core, *moments, *outs),
        (1, 0, (DV, 0), (DV, 1), "pair1", "pair", "scalar") + ("late",) * 8,
        (
            (shape((qk, count // 2), BF),) * 2,
            shape((third.shape[0], DV), BF),
            shape((width, 2 * qk + FPAD + outs[0].shape[1]), BF),
        ),
        ("pair1", None, None),
        [pltpu.VMEM((2 * qk, width), F32), pltpu.VMEM((16, DV), F32)],
        2 * count * (heads * FPAD * DV + 2 * qk * width),
    )


def outputs_phase(core, attended, qgrads, kgrads, feats, sgrads, weights, w_out, heads):
    count, width = attended[0].shape[1], w_out.shape[1]
    rows, joined = heads * DV, 2 * heads * DK + heads * DV

    def body(at_first, at_last, core_ref, *refs):
        atts, qs, ks, fs, ss, ws = (refs[2 * i : 2 * i + 2] for i in range(6))
        out_ref, mixed_ref, gtok_ref, turned = refs[12:]
        at = core_ref[0, 0]

        @at_first
        def _():
            for c in range(2):
                for head in range(heads):
                    turned[c, head] = weighted_turned(ss[c], head)

        mixed, gtok = 0.0, 0.0
        for c in range(2):
            first = pl.multiple_of((at if c == 0 else 1 - at) * rows, rows)
            mixed = mixed + dot(atts[c][...], out_ref[pl.ds(first, rows), :], (0, 0))
            parts = [qs[c][...], ks[c][...]]
            for head in range(heads):
                feat = fs[c][head * FPAD : (head + 1) * FPAD, :]
                parts.append(dot(turned[c, head, :, :FPAD], feat, (1, 0)).astype(BF))
            gtok = gtok + dot(jnp.concatenate(parts, axis=0), ws[c][...], (0, 1))
        mixed_ref[...] = mixed.astype(BF)
        gtok_ref[...] = gtok.astype(BF)

    return call(
        body,
        count,
        (core, *attended, *qgrads, *kgrads, *feats, *sgrads, *weights, w_out),
        ("scalar",) + (1,) * 8 + (None,) * 2 + ((joined, 0),) * 2 + (None,),
        (shape((count, width), BF), shape((count, width), BF)),
        (0, 0),
        [pltpu.VMEM((2, heads, DV, SPAD), BF)],
        2 * count * 2 * (joined * width + rows * width + heads * FPAD * DV),
    )


def finish_phase(core, fourth, sgrads, after, heads, scale_factor):
    rows, qk = 8, heads * DK
    quarter = fourth.shape[1] - 2 * qk - FPAD

    def body(at_first, at_last, core_ref, recv_ref, mine_ref, other_ref, *refs):
        query_ref, key_ref, value_ref, out_ref, wgrad, moment, out = refs[-7:]

        at_first(lambda: clear(wgrad, moment, out))
        odd = at_first.block % 2
        wgrad[...] += add_chips(recv_ref.at[:, pl.ds(0, 2 * qk)], 2 * rows)
        parts = recv_ref.shape[0] // (2 * rows)
        for which in range(2):
            some = [p for p in range(parts) if p // 2 % 2 == which]
            moment[2 * odd + which] += sum(
                recv_ref[2 * rows * p : 2 * rows * (p + 1), 2 * qk : 2 * qk + FPAD].astype(F32) for p in some
            )
            some = [p for p in range(parts) if p % 2 == which]
            out[2 * which + 1 - odd] += sum(
                recv_ref[2 * rows * p : 2 * rows * (p + 1), 2 * qk + FPAD :].astype(F32) for p in some
            )
        @at_last
        def _():
            for x in range(4):
                out_ref[:, x * quarter : (x + 1) * quarter] = (out[x, :rows] + out[x, rows:]) * scale_factor
            first = core_ref[0, 0] == 0
            both = wgrad[...] * scale_factor
            query_ref[...] = jnp.concatenate([both[:rows, :qk], both[rows:, :qk]], axis=1)
            key_ref[...] = jnp.concatenate([both[:rows, qk:], both[rows:, qk:]], axis=1)
            weight = band_weight((1, FPAD), 1) * scale_factor
            found = [[], []]
            for head in range(heads):
                whole = moment[head] * weight
                high = whole.astype(BF)
                split = jnp.concatenate([high, (whole - high.astype(F32)).astype(BF)], axis=0)
                for which, ref in enumerate((mine_ref, other_ref)):
                    both = dot(split, ref[head * SPAD : head * SPAD + FPAD, :], (1, 0))
                    both = both[: 2 * rows] + both[2 * rows :]
                    low, up = both[:rows], both[rows:]
                    found[which].append(jnp.where(first, low, up) if which == 0 else jnp.where(first, up, low))
            mine, other = (jnp.concatenate(part, axis=1) for part in found)
            value_ref[:, : heads * DV] = jnp.where(first, mine, other)
            value_ref[:, heads * DV :] = jnp.where(first, other, mine)

    return call(
        body,
        fourth.shape[0],
        (core, fourth, *sgrads, *after),
        ("scalar", 0, "late", "late") + ("any",) * len(after),
        (
            shape((rows, 2 * qk), F32),
            shape((rows, 2 * qk), F32),
            shape((rows, 2 * heads * DV), F32),
            shape((rows, 4 * quarter), F32),
        ),
        (None,) * 4,
        [
            pltpu.VMEM((2 * rows, 2 * qk), F32),
            pltpu.VMEM((heads, 2 * rows, FPAD), F32),
            pltpu.VMEM((4, 2 * rows, quarter), F32),
        ],
        0,
        fourth.shape[0] // 4,
    )


def per_device(chips, tokens, w_query, w_key, w_value, w_out, cotangent):
    n = 2 * chips
    heads = H // 2
    own, width = tokens.shape
    qk = heads * DK
    core = lax.axis_index("seq") % 2
    core_at = core.astype(jnp.int32).reshape(1, 1)
    same_core = [[2 * p + c for p in range(chips)] for c in range(2)]
    swap = [(i, i ^ 1) for i in range(n)]
    scale_factor = (own * n) ** (-0.5)

    def exchange(x):
        return lax.ppermute(x, AXES, swap)

    def spread(x):
        return lax.all_to_all(x, AXES, 0, 0, axis_index_groups=same_core, tiled=True)

    def among_four(flips, parts):
        found = [parts[0]]
        for step in (1, 2, 3):
            moves = []
            for i in range(n):
                at = place(i)
                for bit in (0, 1):
                    at = flips[bit](*at) if step >> bit & 1 else at
                moves.append((i, device(*at)))
            found.append(lax.ppermute(parts[step], AXES, moves))
        return found

    yz = (lambda y, x, z, c: (y, x, z ^ 1, c), lambda y, x, z, c: (y ^ 1, x, z, c))
    xy = (lambda y, x, z, c: ((y + 2 * (y % 2) - 1) % 4, x, z, c), lambda y, x, z, c: (y, x ^ 1, z, c))

    def place(i):
        return (i // 32, 2 * (i // 16 % 2) + i // 2 % 2, i // 4 % 4, i % 2)

    def device(y, x, z, c):
        return (((y * 2 + x // 2) * 4 + z) * 2 + x % 2) * 2 + c

    def to_each(x):
        return x.reshape(chips, -1, x.shape[1])

    ctx, seq = lax.axis_index("ctx"), lax.axis_index("seq")
    in_yz, in_xy = (
        v.astype(jnp.int32).reshape(1, 1)
        for v in (2 * (ctx // 8 % 2) + ctx % 2, 2 * (seq // 2) + 1 - ctx // 8 % 2)
    )

    to_send = weights_phase(w_query, w_key, w_value, w_out, chips, heads)
    weights = lax.all_to_all(to_send.reshape(n, -1, to_send.shape[1]), AXES, 0, 0, tiled=True)
    weights = weights.reshape(-1, to_send.shape[1])
    tok = (tokens, exchange(tokens))
    cot = (cotangent, exchange(cotangent))
    other_weights = exchange(weights)

    qk_t, value, key_feat, key_feat_sent, sent = keys_phase(tok, weights, chips, heads)
    first = spread(to_each(sent)).reshape(sent.shape)
    key_feats = (key_feat, exchange(key_feat_sent))

    up_t, query_feat, w_out_whole = upstream_phase(core_at, qk_t, cot, weights, other_weights, heads)
    moments = among_four(yz, product_phase(in_yz, (key_feat, key_feat_sent), tok, up_t, heads))
    scales, norm, sent = query_phase(query_feat, up_t, first, chips, heads)
    second = spread(to_each(sent)).reshape(sent.shape)

    attended, attended_sent, dens, sent, *outs = attend_phase(
        in_xy, query_feat, scales, up_t, second, cot, chips, heads
    )
    third = spread(to_each(sent)).reshape(sent.shape)
    outs = among_four(xy, outs)
    attendeds = (attended, exchange(attended_sent))
    qgrad, qgrad_sent = query_back_phase(qk_t, scales, dens, up_t, second, norm, heads)
    qgrads = (qgrad, exchange(qgrad_sent))

    kgrad, kgrad_sent, sgrad, sent = key_phase(qk_t, value, third, (qgrad, qgrad_sent), tok, core_at, moments, outs, heads)
    fourth = lax.all_to_all(sent.reshape(n, -1, sent.shape[1]), AXES, 0, 0, tiled=True).reshape(sent.shape)
    kgrads, sgrads = (kgrad, exchange(kgrad_sent)), (sgrad, exchange(sgrad))
    mixed, grad_tokens = outputs_phase(
        core_at, attendeds, qgrads, kgrads, key_feats, sgrads, (weights, other_weights), w_out_whole, heads
    )
    grad_query, grad_key, grad_value, grad_out = finish_phase(
        core_at, fourth, sgrads, (grad_tokens, mixed), heads, scale_factor
    )
    return (mixed, grad_tokens, grad_query, grad_key, grad_value, grad_out)


def solution(mesh):
    chips = mesh.size // 2
    placed = P(AXES, None)
    return jax.shard_map(
        lambda *args: per_device(chips, *args),
        mesh=mesh,
        in_specs=(placed,) * 6,
        out_specs=(placed,) * 6,
        check_vma=False,
    )
```
